32 devices in a mesh: clip: 4 (over y, x), frame: 4 (over z), tile: 2 (over core).
Axes of the slice: x: 2, y: 2, z: 4, core: 2. Of those that a mesh axis runs over, the one named last changes fastest.
Arguments:
- clip_feats: bfloat16 [128, 8, 16, 256], P(('clip', 'frame'), 'tile'), parts along dimension 0, may hold values from -6 to 6
- out_grad: bfloat16 [128, 8, 16, 256], P(('clip', 'frame'), 'tile'), parts along dimension 0, may hold values from -6 to 6
- spatial_weight: bfloat16 [2304, 256], replicated, may hold values from -0.125 to 0.125
- temporal_weight: bfloat16 [2304, 256], replicated, may hold values from -0.125 to 0.125
Outputs:
- block_out: bfloat16 [128, 8, 16, 256], P(('clip', 'frame'), 'tile'), parts along dimension 0
- input_grad: bfloat16 [128, 8, 16, 256], P(('clip', 'frame'), 'tile'), parts along dimension 0
- weight_grad: float32 [9216, 256], P(('clip', 'frame', 'tile')), parts along dimension 0
The draws below stay inside these ranges and needn't reach their ends.
There are 4 independent parts, one for each index of `clip`. The reference program is written for one: setup_inputs(seed, part) draws one part's arguments, and reference() takes and returns one part's arrays. A program takes and returns all parts, laid end to end along the dimension named above; an argument that names none is the same for every part. Nothing has to cross between parts.
All inputs are finite; a program needn't handle non-finite values.
Results may differ from the reference program's by a relative error of at most 0.009.
Values may be sent and summed in bfloat16 or wider, within the bound.
No kernel may reach another device: no remote copies, remote signals or barrier semaphores. Data moves between devices by JAX's collectives and lax.ppermute only.
A program may use at most 64 MiB of HBM per device.

```python
import math
import jax
import jax.numpy as jnp
from jax import lax

C = 256
TAP_DILATION = 2
W = 16
FRAMES = 32
HEIGHT = 8


def raised(values, stream_key, source, target, parts, factor):
    def block_of(dim):
        return (jnp.arange(values.shape[dim]) // (values.shape[dim] // parts)).reshape((-1,) + (1,) * (values.ndim - 1 - dim))

    near = jax.random.permutation(stream_key, parts)[block_of(target)]
    far = (block_of(target) + parts // 2) % parts
    return jnp.where((block_of(source) == near) | (block_of(source) == far), factor * values, values)


def shard_levels(stream_key, extent, cuts, least, top_value):
    gain = 1.0
    for axis_at, blocks in cuts:
        heights = jax.random.uniform(jax.random.fold_in(jax.random.fold_in(stream_key, 6), axis_at), (blocks,), jnp.float32, least / len(cuts), top_value / len(cuts))
        gain = gain * jnp.repeat(jnp.exp(heights), extent[axis_at] // blocks).reshape((-1,) + (1,) * (len(extent) - 1 - axis_at))
    return gain


def centred(key, shape, scale, bound, cuts=(), kind=jnp.bfloat16):
    gain = shard_levels(key, shape, cuts, -0.22, 0.18) if cuts else 1.0
    drawn = jax.random.normal(key, shape, jnp.float32) * scale * gain
    return jnp.minimum(jnp.maximum(drawn, -bound), bound).astype(kind)


def noise_with(stream_key, shape, width, limit, shards, heavy, held_as=jnp.bfloat16):
    result = width * jax.random.normal(stream_key, shape, jnp.float32)
    if shards:
        result = result * shard_levels(stream_key, shape, shards, -0.22, 0.18)
    return jnp.clip(raised(result, jax.random.fold_in(stream_key, 3), *heavy), -limit, limit).astype(held_as)


def setup_inputs(seed: int = 0, part: int = 0) -> dict:
    key_of = jax.random.split(jax.random.key(seed), 5)
    part_splits = jax.random.split(jax.random.fold_in(key_of[4], part), 5)
    return {
        "clip_feats": noise_with(part_splits[0], (FRAMES, HEIGHT, W, C), 1.0, 6.0, ((0, 4), (1, 2)), (1, 3, 2, 2.0)),
        "out_grad": centred(part_splits[1], (FRAMES, HEIGHT, W, C), 1.0, 6.0, ((0, 4), (1, 2))),
        "spatial_weight": centred(key_of[2], (9 * C, C), (9 * C) ** -0.5, 0.125),
        "temporal_weight": centred(key_of[3], (9 * C, C), (9 * C) ** -0.5, 0.125),
    }


def frame_columns(frame_feats, backward_pass):
    padded = jnp.pad(frame_feats, ((1, 1), (1, 1), (0, 0)))
    pieces = []
    for row_shift in range(3):
        for col_shift in range(3):
            row_start = 2 - row_shift if backward_pass else row_shift
            col_start = 2 - col_shift if backward_pass else col_shift
            pieces.append(padded[row_start:row_start + HEIGHT, col_start:col_start + W, :])
    return jnp.concatenate(pieces, axis=-1).reshape(HEIGHT * W, 9 * C)

def reference(clip_feats, out_grad, spatial_weight, temporal_weight):
    positions = HEIGHT * W
    spatial_back = spatial_weight.reshape(9, C, C).transpose(0, 2, 1).reshape(9 * C, C)

    def forward_frame(frame_feats):
        return jnp.dot(frame_columns(frame_feats, False), spatial_weight, preferred_element_type=jnp.float32)
    pre = lax.map(forward_frame, clip_feats)
    act = jax.nn.silu(pre).astype(jnp.bfloat16)
    temporal_reach = 4 * TAP_DILATION
    act_pad = jnp.pad(act, ((temporal_reach, temporal_reach), (0, 0), (0, 0)))
    grad_pad = jnp.pad(out_grad.reshape(FRAMES, positions, C), ((temporal_reach, temporal_reach), (0, 0), (0, 0)))
    temporal_out = jnp.zeros((FRAMES * positions, C), jnp.float32)
    act_grad = jnp.zeros((FRAMES * positions, C), jnp.float32)
    for temporal_tap_index in range(9):
        block = temporal_weight[temporal_tap_index * C:(temporal_tap_index + 1) * C]
        forward_first_frame = temporal_tap_index * TAP_DILATION
        backward_first_frame = (8 - temporal_tap_index) * TAP_DILATION
        temporal_out = temporal_out + jnp.dot(act_pad[forward_first_frame:forward_first_frame + FRAMES].reshape(-1, C), block, preferred_element_type=jnp.float32)
        act_grad = act_grad + jnp.dot(grad_pad[backward_first_frame:backward_first_frame + FRAMES].reshape(-1, C), block.T, preferred_element_type=jnp.float32)
    block_out = (clip_feats.reshape(-1, C).astype(jnp.float32) + temporal_out).astype(jnp.bfloat16).reshape(FRAMES, HEIGHT, W, C)
    act_grad = act_grad.astype(jnp.bfloat16)
    sig = jax.nn.sigmoid(pre.reshape(-1, C))
    pre_grad = (act_grad.astype(jnp.float32) * (sig * (1.0 + pre.reshape(-1, C) * (1.0 - sig)))).astype(jnp.bfloat16)
    pre_grad = pre_grad.reshape(FRAMES, HEIGHT, W, C)

    def grad_step(total, pair):
        columns = frame_columns(pair[0], False)
        term = lax.dot_general(columns, pair[1].reshape(positions, C), (((0,), (0,)), ((), ())), preferred_element_type=jnp.float32)
        return (total + term, None)
    total, _ = lax.scan(grad_step, jnp.zeros((9 * C, C), jnp.float32), (clip_feats, pre_grad))
    weight_grad = total * jnp.float32(1.0 / math.sqrt(FRAMES * HEIGHT * W))

    def back_frame(pair):
        columns = frame_columns(pair[0], True)
        local = jnp.dot(columns, spatial_back, preferred_element_type=jnp.float32)
        return (pair[1].reshape(positions, C).astype(jnp.float32) + local).astype(jnp.bfloat16).reshape(HEIGHT, W, C)
    input_grad = lax.map(back_frame, (pre_grad, out_grad))
    return (block_out, input_grad, weight_grad)
```

```python
import math

import jax
import jax.numpy as jnp
from jax import lax
from jax.experimental import pallas as pl
from jax.experimental.pallas import tpu as pltpu
from jax.sharding import PartitionSpec as P

TAP_DILATION = 2
VMEM_LIMIT = 32 * 1024 * 1024


def padded_2(block, sides, width):
    for axis, dim in sides:
        count = lax.axis_size(axis)
        forward = [(i, i + 1) for i in range(count - 1)]
        backward = [(target, source) for source, target in forward]
        low = lax.ppermute(
            lax.slice_in_dim(block, block.shape[dim] - width, None, axis=dim), axis, forward
        )
        high = lax.ppermute(lax.slice_in_dim(block, 0, width, axis=dim), axis, backward)
        block = jnp.concatenate([low, block, high], axis=dim)
    return block


def tile_columns(extended, tile_rows, width_cells, backward_pass):
    padded = jnp.pad(extended, ((0, 0), (0, 0), (1, 1), (0, 0)))
    pieces = []
    for row_shift in range(3):
        for col_shift in range(3):
            row_start = 2 - row_shift if backward_pass else row_shift
            col_start = 2 - col_shift if backward_pass else col_shift
            pieces.append(
                padded[:, row_start : row_start + tile_rows, col_start : col_start + width_cells, :]
            )
    channels = extended.shape[3]
    return jnp.concatenate(pieces, axis=-1).reshape(-1, 9 * channels)


def temporal_taps(padded_seq, weight, frame_count, backward_pass):
    pieces = []
    for temporal_tap_index in range(9):
        first_frame_index = (
            (8 - temporal_tap_index) * TAP_DILATION
            if backward_pass
            else temporal_tap_index * TAP_DILATION
        )
        pieces.append(padded_seq[first_frame_index : first_frame_index + frame_count])
    channels = padded_seq.shape[2]
    columns = jnp.concatenate(pieces, axis=-1).reshape(-1, 9 * channels)
    return jnp.dot(columns, weight, preferred_element_type=jnp.float32)


def per_device_any(clip_feats, out_grad, spatial_weight, temporal_weight):
    slab_frames, tile_rows, width_cells, channels = clip_feats.shape
    row_count = slab_frames * tile_rows * width_cells
    frame_devs = lax.axis_size("frame")
    tile_devs = lax.axis_size("tile")
    grad_scale = jnp.float32(
        1.0 / math.sqrt(slab_frames * frame_devs * tile_rows * tile_devs * width_cells)
    )
    spatial_back = (
        spatial_weight.reshape(9, channels, channels)
        .transpose(0, 2, 1)
        .reshape(9 * channels, channels)
    )
    temporal_back = (
        temporal_weight.reshape(9, channels, channels)
        .transpose(0, 2, 1)
        .reshape(9 * channels, channels)
    )
    feat_ext = padded_2(clip_feats, (("tile", 1),), 1)
    feat_columns = tile_columns(feat_ext, tile_rows, width_cells, False)
    pre = jnp.dot(feat_columns, spatial_weight, preferred_element_type=jnp.float32)
    act = jax.nn.silu(pre).astype(jnp.bfloat16)
    temporal_reach = 4 * TAP_DILATION
    per_group = tile_rows * width_cells // frame_devs
    grouped = (slab_frames, frame_devs, per_group, channels)
    act_part = lax.all_to_all(
        act.reshape(grouped), "frame", split_axis=1, concat_axis=0, tiled=True
    )
    grad_part = lax.all_to_all(out_grad, "frame", split_axis=1, concat_axis=0, tiled=True)
    feat_part = lax.all_to_all(clip_feats, "frame", split_axis=1, concat_axis=0, tiled=True)
    frame_count = act_part.shape[0]
    item_count = act_part.shape[2]
    act_pad = jnp.pad(
        act_part.reshape(frame_count, item_count, channels),
        ((temporal_reach, temporal_reach), (0, 0), (0, 0)),
    )
    grad_pad = jnp.pad(
        grad_part.reshape(frame_count, item_count, channels),
        ((temporal_reach, temporal_reach), (0, 0), (0, 0)),
    )
    mixed = temporal_taps(act_pad, temporal_weight, frame_count, False)
    out_part = (feat_part.reshape(-1, channels).astype(jnp.float32) + mixed).astype(jnp.bfloat16)
    back_part = temporal_taps(grad_pad, temporal_back, frame_count, True).astype(jnp.bfloat16)
    out_part = out_part.reshape(frame_count, 1, item_count, channels)
    back_part = back_part.reshape(frame_count, 1, item_count, channels)
    out_slab = lax.all_to_all(out_part, "frame", split_axis=0, concat_axis=1, tiled=True)
    grad_slab = lax.all_to_all(back_part, "frame", split_axis=0, concat_axis=1, tiled=True)
    act_grad = grad_slab.reshape(row_count, channels)
    sig = jax.nn.sigmoid(pre)
    pre_grad = (act_grad.astype(jnp.float32) * (sig * (1.0 + pre * (1.0 - sig)))).astype(
        jnp.bfloat16
    )
    full_term = lax.dot_general(
        feat_columns, pre_grad, (((0,), (0,)), ((), ())), preferred_element_type=jnp.float32
    )
    summed = lax.psum_scatter(full_term, ("frame", "tile"), scatter_dimension=0, tiled=True)
    weight_grad = summed * grad_scale
    grad_ext = padded_2(
        pre_grad.reshape(slab_frames, tile_rows, width_cells, channels), (("tile", 1),), 1
    )
    grad_columns = tile_columns(grad_ext, tile_rows, width_cells, True)
    local_back = jnp.dot(grad_columns, spatial_back, preferred_element_type=jnp.float32)
    input_grad = (out_grad.reshape(row_count, channels).astype(jnp.float32) + local_back).astype(
        jnp.bfloat16
    )
    input_grad = input_grad.reshape(slab_frames, tile_rows, width_cells, channels)
    return (out_slab, input_grad, weight_grad)


def kernel_call(body, outs, scratch, flops, *args):
    moved = sum(a.size * a.dtype.itemsize for a in args)
    moved += sum(math.prod(shape) * jnp.dtype(kind).itemsize for shape, kind in outs)
    return pl.pallas_call(
        body,
        out_shape=tuple(jax.ShapeDtypeStruct(shape, kind) for shape, kind in outs),
        in_specs=[pl.BlockSpec(memory_space=pltpu.VMEM)] * len(args),
        out_specs=tuple(pl.BlockSpec(memory_space=pltpu.VMEM) for _ in outs),
        scratch_shapes=[pltpu.VMEM(shape, kind) for shape, kind in scratch],
        compiler_params=pltpu.CompilerParams(vmem_limit_bytes=VMEM_LIMIT),
        cost_estimate=pl.CostEstimate(flops=flops, bytes_accessed=moved, transcendentals=0),
    )(*args)


def shifted(values, width, step):
    rows = values.shape[0]
    at = lax.broadcasted_iota(jnp.int32, values.shape, 0) % width
    moved = pltpu.roll(values, step % rows, 0)
    inside = at >= step if step > 0 else at < width + step
    return jnp.where(inside, moved, 0.0)


def column_shifts(values, width):
    wide = values.astype(jnp.float32)
    return (
        shifted(wide, width, 1).astype(values.dtype),
        values,
        shifted(wide, width, -1).astype(values.dtype),
    )


def with_edges(own, other, ext):
    rows = own.shape[1]
    tile = lax.axis_index("tile")
    ext[:, 1 : rows + 1] = own[...]
    above, below = other[:, rows - 1], other[:, 0]
    ext[:, 0] = jnp.where(tile == 1, above, jnp.zeros_like(above))
    ext[:, rows + 1] = jnp.where(tile == 0, below, jnp.zeros_like(below))


def spatial_kernel(own, other, weight, pre_ref, act_ref, ext):
    frames, rows, width, channels = own.shape
    with_edges(own, other, ext)
    shifts = column_shifts(ext[...].reshape(-1, channels), width)
    shifts = [piece.reshape(ext.shape) for piece in shifts]
    columns = jnp.concatenate(
        [
            shifts[s][:, r : r + rows].reshape(-1, channels)
            for r in range(3)
            for s in range(3)
        ],
        axis=1,
    )
    pre = jnp.dot(columns, weight[...], preferred_element_type=jnp.float32)
    pre_ref[...] = pre
    act_ref[...] = (pre * jax.nn.sigmoid(pre)).astype(jnp.bfloat16)


def transpose_kernel(own, other, out_ref, image):
    frames, rows, width, channels = own.shape
    tile = lax.axis_index("tile")
    image[:, pl.ds(tile * rows, rows)] = own[...]
    image[:, pl.ds((1 - tile) * rows, rows)] = other[...]
    out_ref[...] = image[...].reshape(-1, channels).T


def act_grad_kernel(own, low, high, weight, pre_ref, out_ref, ext):
    count, channels = own.shape
    ext[0:count] = low[...]
    ext[count : 2 * count] = own[...]
    ext[2 * count : 3 * count] = high[...]
    hop = count // 4
    total = None
    for k in range(9):
        first = (8 - k) * hop
        term = lax.dot_general(
            ext[first : first + count],
            weight[k * channels : (k + 1) * channels],
            (((1,), (1,)), ((), ())),
            preferred_element_type=jnp.float32,
        )
        total = term if total is None else total + term
    act_grad = total.astype(jnp.bfloat16).astype(jnp.float32)
    pre = pre_ref[...]
    sig = jax.nn.sigmoid(pre)
    out_ref[...] = (act_grad * (sig * (1.0 + pre * (1.0 - sig)))).astype(jnp.bfloat16)


def temporal_kernel(feats, own, low, high, weight, out_ref, ext):
    count, channels = own.shape
    ext[0:count] = low[...]
    ext[count : 2 * count] = own[...]
    ext[2 * count : 3 * count] = high[...]
    hop = count // 4
    columns = jnp.concatenate(
        [ext[k * hop : k * hop + count] for k in range(9)], axis=1
    )
    mixed = jnp.dot(columns, weight[...], preferred_element_type=jnp.float32)
    out_ref[...] = (feats[...].astype(jnp.float32) + mixed).astype(jnp.bfloat16)


def kernel_grad_kernel(feats_t, own, other, far_ref, pass_ref, near_ref, keep_ref, image, total):
    frames, rows, width, channels = own.shape
    tile = lax.axis_index("tile")
    chip = lax.axis_index("frame")
    image[:, 0] = jnp.zeros_like(image[:, 0])
    image[:, 2 * rows + 1] = jnp.zeros_like(image[:, 2 * rows + 1])
    image[:, pl.ds(1 + tile * rows, rows)] = own[...]
    image[:, pl.ds(1 + (1 - tile) * rows, rows)] = other[...]
    after, same, before = column_shifts(image[...].reshape(-1, channels), width)
    shifts = [piece.reshape(image.shape) for piece in (before, same, after)]
    left = feats_t[...]
    for r in range(3):
        for s in range(3):
            right = shifts[s][:, 2 - r : 2 - r + 2 * rows].reshape(-1, channels)
            tap = 3 * r + s
            total[tap * channels : (tap + 1) * channels] = jnp.dot(
                left, right, preferred_element_type=jnp.float32
            )
    share = keep_ref.shape[0]
    for distance, ref in ((3, far_ref), (2, pass_ref), (1, near_ref), (0, keep_ref)):
        first = (2 * (chip ^ distance) + tile) * share
        ref[...] = total[pl.ds(pl.multiple_of(first, 32), share)].astype(ref.dtype)


def input_grad_kernel(out_grad, own, other, weight, out_ref, ext):
    frames, rows, width, channels = own.shape
    with_edges(own, other, ext)
    after, same, before = column_shifts(ext[...].reshape(-1, channels), width)
    shifts = [piece.reshape(ext.shape) for piece in (before, same, after)]
    total = out_grad[...].astype(jnp.float32)
    for r in range(3):
        for s in range(3):
            tap = 3 * r + s
            total = total + lax.dot_general(
                shifts[s][:, 2 - r : 2 - r + rows].reshape(-1, channels),
                weight[tap * channels : (tap + 1) * channels],
                (((1,), (1,)), ((), ())),
                preferred_element_type=jnp.float32,
            )
    out_ref[...] = total.astype(jnp.bfloat16)


def per_device_pair(clip_feats, out_grad, spatial_weight, temporal_weight):
    frames, rows, width, channels = clip_feats.shape
    count = frames * rows * width
    chips = lax.axis_size("frame")
    cores = lax.axis_size("tile")
    scale = jnp.float32(1.0 / math.sqrt(frames * chips * rows * cores * width))
    up = [(z, z + 1) for z in range(chips - 1)]
    down = [(z + 1, z) for z in range(chips - 1)]
    swap = [(0, 1), (1, 0)]
    bf16, f32 = jnp.bfloat16, jnp.float32
    product = 2 * count * 9 * channels * channels
    flat = (count, channels)

    grad_flat = out_grad.reshape(flat)
    feat_flat = clip_feats.reshape(flat)
    grad_low = lax.ppermute(grad_flat, "frame", up)
    grad_high = lax.ppermute(grad_flat, "frame", down)
    feat_other = lax.ppermute(clip_feats, "tile", swap)

    ext = ((frames, rows + 2, width, channels), bf16)
    pre, act = kernel_call(
        spatial_kernel,
        [(flat, f32), (flat, bf16)],
        [ext],
        product,
        clip_feats, feat_other, spatial_weight,
    )
    act_low = lax.ppermute(act, "frame", up)
    act_high = lax.ppermute(act, "frame", down)
    (feats_t,) = kernel_call(
        transpose_kernel,
        [((channels, 2 * count), bf16)],
        [((frames, 2 * rows, width, channels), bf16)],
        0,
        clip_feats, feat_other,
    )
    (pre_grad,) = kernel_call(
        act_grad_kernel,
        [(flat, bf16)],
        [((3 * count, channels), bf16)],
        product,
        grad_flat, grad_low, grad_high, temporal_weight, pre,
    )
    pre_grad = pre_grad.reshape(clip_feats.shape)
    pre_other = lax.ppermute(pre_grad, "tile", swap)

    share = (9 * channels // (chips * cores), channels)
    far, onward, near, keep = kernel_call(
        kernel_grad_kernel,
        [(share, bf16), (share, f32), (share, bf16), (share, f32)],
        [
            ((frames, 2 * rows + 2, width, channels), bf16),
            ((9 * channels, channels), f32),
        ],
        2 * product,
        feats_t, pre_grad, pre_other,
    )
    beside = [(z, z ^ 1) for z in range(chips)]
    across = [(z, z ^ 2) for z in range(chips)]
    far_in = lax.ppermute(far, "frame", beside)
    near_in = lax.ppermute(near, "frame", beside)
    onward = (onward + far_in.astype(f32)).astype(bf16)
    last_in = lax.ppermute(onward, "frame", across)

    (input_grad,) = kernel_call(
        input_grad_kernel,
        [(flat, bf16)],
        [ext],
        product,
        grad_flat, pre_grad, pre_other, spatial_weight,
    )
    (block_out,) = kernel_call(
        temporal_kernel,
        [(flat, bf16)],
        [((3 * count, channels), bf16)],
        product,
        feat_flat, act, act_low, act_high, temporal_weight,
    )
    weight_grad = (keep + near_in.astype(f32) + last_in.astype(f32)) * scale
    return (
        block_out.reshape(clip_feats.shape),
        input_grad.reshape(clip_feats.shape),
        weight_grad,
    )


def per_device(clip_feats, *rest):
    pairs = lax.axis_size("tile") == 2 and lax.axis_size("frame") == 4
    if pairs and clip_feats.shape[0] == 4 * TAP_DILATION:
        return per_device_pair(clip_feats, *rest)
    return per_device_any(clip_feats, *rest)


def solution(mesh):
    return jax.shard_map(
        per_device,
        mesh=mesh,
        in_specs=(
            P(("clip", "frame"), "tile", None, None),
            P(("clip", "frame"), "tile", None, None),
            P(),
            P(),
        ),
        out_specs=(
            P(("clip", "frame"), "tile", None, None),
            P(("clip", "frame"), "tile", None, None),
            P(("clip", "frame", "tile"), None),
        ),
        check_vma=False,
    )
```

```python
import math

import jax
import jax.numpy as jnp
from jax import lax
from jax.experimental import pallas as pl
from jax.experimental.pallas import tpu as pltpu
from jax.sharding import PartitionSpec as P

TAP_DILATION = 2
VMEM_LIMIT = 32 * 1024 * 1024


def padded_2(block, sides, width):
    for axis, dim in sides:
        count = lax.axis_size(axis)
        forward = [(i, i + 1) for i in range(count - 1)]
        backward = [(target, source) for source, target in forward]
        low = lax.ppermute(
            lax.slice_in_dim(block, block.shape[dim] - width, None, axis=dim), axis, forward
        )
        high = lax.ppermute(lax.slice_in_dim(block, 0, width, axis=dim), axis, backward)
        block = jnp.concatenate([low, block, high], axis=dim)
    return block


def tile_columns(extended, tile_rows, width_cells, backward_pass):
    padded = jnp.pad(extended, ((0, 0), (0, 0), (1, 1), (0, 0)))
    pieces = []
    for row_shift in range(3):
        for col_shift in range(3):
            row_start = 2 - row_shift if backward_pass else row_shift
            col_start = 2 - col_shift if backward_pass else col_shift
            pieces.append(
                padded[:, row_start : row_start + tile_rows, col_start : col_start + width_cells, :]
            )
    channels = extended.shape[3]
    return jnp.concatenate(pieces, axis=-1).reshape(-1, 9 * channels)


def temporal_taps(padded_seq, weight, frame_count, backward_pass):
    pieces = []
    for temporal_tap_index in range(9):
        first_frame_index = (
            (8 - temporal_tap_index) * TAP_DILATION
            if backward_pass
            else temporal_tap_index * TAP_DILATION
        )
        pieces.append(padded_seq[first_frame_index : first_frame_index + frame_count])
    channels = padded_seq.shape[2]
    columns = jnp.concatenate(pieces, axis=-1).reshape(-1, 9 * channels)
    return jnp.dot(columns, weight, preferred_element_type=jnp.float32)


def per_device_any(clip_feats, out_grad, spatial_weight, temporal_weight):
    slab_frames, tile_rows, width_cells, channels = clip_feats.shape
    row_count = slab_frames * tile_rows * width_cells
    frame_devs = lax.axis_size("frame")
    tile_devs = lax.axis_size("tile")
    grad_scale = jnp.float32(
        1.0 / math.sqrt(slab_frames * frame_devs * tile_rows * tile_devs * width_cells)
    )
    spatial_back = (
        spatial_weight.reshape(9, channels, channels)
        .transpose(0, 2, 1)
        .reshape(9 * channels, channels)
    )
    temporal_back = (
        temporal_weight.reshape(9, channels, channels)
        .transpose(0, 2, 1)
        .reshape(9 * channels, channels)
    )
    feat_ext = padded_2(clip_feats, (("tile", 1),), 1)
    feat_columns = tile_columns(feat_ext, tile_rows, width_cells, False)
    pre = jnp.dot(feat_columns, spatial_weight, preferred_element_type=jnp.float32)
    act = jax.nn.silu(pre).astype(jnp.bfloat16)
    temporal_reach = 4 * TAP_DILATION
    per_group = tile_rows * width_cells // frame_devs
    grouped = (slab_frames, frame_devs, per_group, channels)
    act_part = lax.all_to_all(
        act.reshape(grouped), "frame", split_axis=1, concat_axis=0, tiled=True
    )
    grad_part = lax.all_to_all(out_grad, "frame", split_axis=1, concat_axis=0, tiled=True)
    feat_part = lax.all_to_all(clip_feats, "frame", split_axis=1, concat_axis=0, tiled=True)
    frame_count = act_part.shape[0]
    item_count = act_part.shape[2]
    act_pad = jnp.pad(
        act_part.reshape(frame_count, item_count, channels),
        ((temporal_reach, temporal_reach), (0, 0), (0, 0)),
    )
    grad_pad = jnp.pad(
        grad_part.reshape(frame_count, item_count, channels),
        ((temporal_reach, temporal_reach), (0, 0), (0, 0)),
    )
    mixed = temporal_taps(act_pad, temporal_weight, frame_count, False)
    out_part = (feat_part.reshape(-1, channels).astype(jnp.float32) + mixed).astype(jnp.bfloat16)
    back_part = temporal_taps(grad_pad, temporal_back, frame_count, True).astype(jnp.bfloat16)
    out_part = out_part.reshape(frame_count, 1, item_count, channels)
    back_part = back_part.reshape(frame_count, 1, item_count, channels)
    out_slab = lax.all_to_all(out_part, "frame", split_axis=0, concat_axis=1, tiled=True)
    grad_slab = lax.all_to_all(back_part, "frame", split_axis=0, concat_axis=1, tiled=True)
    act_grad = grad_slab.reshape(row_count, channels)
    sig = jax.nn.sigmoid(pre)
    pre_grad = (act_grad.astype(jnp.float32) * (sig * (1.0 + pre * (1.0 - sig)))).astype(
        jnp.bfloat16
    )
    full_term = lax.dot_general(
        feat_columns, pre_grad, (((0,), (0,)), ((), ())), preferred_element_type=jnp.float32
    )
    summed = lax.psum_scatter(full_term, ("frame", "tile"), scatter_dimension=0, tiled=True)
    weight_grad = summed * grad_scale
    grad_ext = padded_2(
        pre_grad.reshape(slab_frames, tile_rows, width_cells, channels), (("tile", 1),), 1
    )
    grad_columns = tile_columns(grad_ext, tile_rows, width_cells, True)
    local_back = jnp.dot(grad_columns, spatial_back, preferred_element_type=jnp.float32)
    input_grad = (out_grad.reshape(row_count, channels).astype(jnp.float32) + local_back).astype(
        jnp.bfloat16
    )
    input_grad = input_grad.reshape(slab_frames, tile_rows, width_cells, channels)
    return (out_slab, input_grad, weight_grad)


def kernel_call(body, outs, scratch, flops, *args, anywhere=0):
    moved = sum(a.size * a.dtype.itemsize for a in args)
    moved += sum(math.prod(shape) * jnp.dtype(kind).itemsize for shape, kind in outs)
    return pl.pallas_call(
        body,
        out_shape=tuple(jax.ShapeDtypeStruct(shape, kind) for shape, kind in outs),
        in_specs=[pl.BlockSpec(memory_space=pltpu.VMEM)] * (len(args) - anywhere)
        + [pl.BlockSpec(memory_space=pl.ANY)] * anywhere,
        out_specs=tuple(pl.BlockSpec(memory_space=pltpu.VMEM) for _ in outs),
        scratch_shapes=[pltpu.VMEM(shape, kind) for shape, kind in scratch],
        compiler_params=pltpu.CompilerParams(vmem_limit_bytes=VMEM_LIMIT),
        cost_estimate=pl.CostEstimate(flops=flops, bytes_accessed=moved, transcendentals=0),
    )(*args)


def shifted(values, width, step):
    rows = values.shape[0]
    at = lax.broadcasted_iota(jnp.int32, values.shape, 0) % width
    moved = pltpu.roll(values, step % rows, 0)
    inside = at >= step if step > 0 else at < width + step
    return jnp.where(inside, moved, 0.0)


def column_shifts(values, width):
    wide = values.astype(jnp.float32)
    return (
        shifted(wide, width, 1).astype(values.dtype),
        values,
        shifted(wide, width, -1).astype(values.dtype),
    )


def with_edges(own, other, ext):
    rows = own.shape[1]
    tile = lax.axis_index("tile")
    ext[:, 1 : rows + 1] = own[...]
    above, below = other[:, rows - 1], other[:, 0]
    ext[:, 0] = jnp.where(tile == 1, above, jnp.zeros_like(above))
    ext[:, rows + 1] = jnp.where(tile == 0, below, jnp.zeros_like(below))


def whole_image(own, other, image):
    rows = own.shape[1]
    tile = lax.axis_index("tile")
    image[:, 0] = jnp.zeros_like(image[:, 0])
    image[:, 2 * rows + 1] = jnp.zeros_like(image[:, 2 * rows + 1])
    image[:, pl.ds(1 + tile * rows, rows)] = own[...]
    image[:, pl.ds(1 + (1 - tile) * rows, rows)] = other[...]


def spatial_kernel(own, other, weight, pre_ref, act_ref, image, pre_all):
    frames, rows, width, channels = own.shape
    whole_image(own, other, image)
    shifts = column_shifts(image[...].reshape(-1, channels), width)
    shifts = [piece.reshape(image.shape) for piece in shifts]
    for half in range(2):
        columns = jnp.concatenate(
            [
                shifts[s][:, half * rows + r : half * rows + r + rows].reshape(-1, channels)
                for r in range(3)
                for s in range(3)
            ],
            axis=1,
        )
        pre = jnp.dot(columns, weight[...], preferred_element_type=jnp.float32)
        pre_all[half] = pre
        act_ref[half] = (pre * jax.nn.sigmoid(pre)).astype(jnp.bfloat16)
    pre_ref[...] = pre_all[lax.axis_index("tile")]


def split_kernel(arrived, _, mine_ref, other_ref):
    tile = lax.axis_index("tile")
    mine_ref[...] = arrived[tile]
    other_ref[...] = arrived[1 - tile]


def forward_sum_kernel(partial, arrived, _, out_ref):
    out_ref[...] = (partial[...] + arrived[...].astype(jnp.float32)).astype(out_ref.dtype)


def transpose_kernel(own, other, out_ref, image):
    frames, rows, width, channels = own.shape
    tile = lax.axis_index("tile")
    image[:, pl.ds(tile * rows, rows)] = own[...]
    image[:, pl.ds((1 - tile) * rows, rows)] = other[...]
    out_ref[...] = image[...].reshape(-1, channels).T


def slabs(own, first, second, ext):
    tile = lax.axis_index("tile")
    ext[2 * tile] = first[...]
    ext[1] = own[...]
    ext[2 - 2 * tile] = second[...]
    return ext[...].reshape(-1, own.shape[1])


def act_grad_kernel(own, first_in, second_in, weight, pre_ref, out_ref, ext):
    count, channels = own.shape
    frames = slabs(own, first_in, second_in, ext)
    hop = count // 4
    total = None
    for k in range(9):
        first = (8 - k) * hop
        term = lax.dot_general(
            frames[first : first + count],
            weight[k * channels : (k + 1) * channels],
            (((1,), (1,)), ((), ())),
            preferred_element_type=jnp.float32,
        )
        total = term if total is None else total + term
    act_grad = total.astype(jnp.bfloat16).astype(jnp.float32)
    pre = pre_ref[...]
    sig = jax.nn.sigmoid(pre)
    out_ref[...] = (act_grad * (sig * (1.0 + pre * (1.0 - sig)))).astype(jnp.bfloat16)


def temporal_kernel(feats, act, first_in, second_in, weight, out_ref, ext):
    count, channels = feats.shape
    own = act.at[lax.axis_index("tile")]
    frames = slabs(own, first_in, second_in, ext)
    hop = count // 4
    columns = jnp.concatenate([frames[k * hop : k * hop + count] for k in range(9)], axis=1)
    mixed = jnp.dot(columns, weight[...], preferred_element_type=jnp.float32)
    out_ref[...] = (feats[...].astype(jnp.float32) + mixed).astype(jnp.bfloat16)


def kernel_grad_kernel(feats_t, own, other, far_ref, pass_ref, near_ref, keep_ref, image, total):
    frames, rows, width, channels = own.shape
    tile = lax.axis_index("tile")
    chip = lax.axis_index("frame")
    whole_image(own, other, image)
    after, same, before = column_shifts(image[...].reshape(-1, channels), width)
    shifts = [piece.reshape(image.shape) for piece in (before, same, after)]
    left = feats_t[...]
    for r in range(3):
        for s in range(3):
            right = shifts[s][:, 2 - r : 2 - r + 2 * rows].reshape(-1, channels)
            tap = 3 * r + s
            total[tap * channels : (tap + 1) * channels] = jnp.dot(
                left, right, preferred_element_type=jnp.float32
            )
    share = keep_ref.shape[0]
    for distance, ref in ((3, far_ref), (2, pass_ref), (1, near_ref), (0, keep_ref)):
        first = (2 * (chip ^ distance) + tile) * share
        ref[...] = total[pl.ds(pl.multiple_of(first, 32), share)].astype(ref.dtype)


def input_grad_kernel(out_grad, own, other, weight, out_ref, ext):
    frames, rows, width, channels = own.shape
    with_edges(own, other, ext)
    after, same, before = column_shifts(ext[...].reshape(-1, channels), width)
    shifts = [piece.reshape(ext.shape) for piece in (before, same, after)]
    total = out_grad[...].astype(jnp.float32)
    for r in range(3):
        for s in range(3):
            tap = 3 * r + s
            total = total + lax.dot_general(
                shifts[s][:, 2 - r : 2 - r + rows].reshape(-1, channels),
                weight[tap * channels : (tap + 1) * channels],
                (((1,), (1,)), ((), ())),
                preferred_element_type=jnp.float32,
            )
    out_ref[...] = total.astype(jnp.bfloat16)


def per_device_pair(clip_feats, out_grad, spatial_weight, temporal_weight):
    frames, rows, width, channels = clip_feats.shape
    count = frames * rows * width
    chips = lax.axis_size("frame")
    cores = lax.axis_size("tile")
    scale = jnp.float32(1.0 / math.sqrt(frames * chips * rows * cores * width))
    outward = [(2 * z, 2 * z + 2) for z in range(chips - 1)]
    outward += [(2 * z + 3, 2 * z + 1) for z in range(chips - 1)]
    inward = [(target, source) for source, target in outward]
    both = ("frame", "tile")
    swap = [(0, 1), (1, 0)]
    bf16, f32 = jnp.bfloat16, jnp.float32
    product = 2 * count * 9 * channels * channels
    flat = (count, channels)
    ext = ((frames, rows + 2, width, channels), bf16)
    image = ((frames, 2 * rows + 2, width, channels), bf16)
    three = ((3, count, channels), bf16)

    grad_flat = out_grad.reshape(flat)
    feat_flat = clip_feats.reshape(flat)
    grad_first = lax.ppermute(grad_flat, both, outward)
    grad_second = lax.ppermute(grad_flat, both, inward)
    feat_other = lax.ppermute(clip_feats, "tile", swap)

    pre, act = kernel_call(
        spatial_kernel,
        [(flat, f32), ((2, *flat), bf16)],
        [image, ((2, *flat), f32)],
        2 * product,
        clip_feats, feat_other, spatial_weight,
    )
    act_in = lax.ppermute(act, both, outward)
    (feats_t,) = kernel_call(
        transpose_kernel,
        [((channels, 2 * count), bf16)],
        [((frames, 2 * rows, width, channels), bf16)],
        0,
        clip_feats, feat_other,
    )
    (pre_grad,) = kernel_call(
        act_grad_kernel,
        [(flat, bf16)],
        [three],
        product,
        grad_flat, grad_first, grad_second, temporal_weight, pre,
    )
    pre_grad = pre_grad.reshape(clip_feats.shape)
    pre_other = lax.ppermute(pre_grad, "tile", swap)

    share = (9 * channels // (chips * cores), channels)
    far, onward, near, keep = kernel_call(
        kernel_grad_kernel,
        [(share, bf16), (share, f32), (share, bf16), (share, f32)],
        [image, ((9 * channels, channels), f32)],
        2 * product,
        feats_t, pre_grad, pre_other,
    )
    act_first, act_pass = kernel_call(
        split_kernel, [(flat, bf16), (flat, bf16)], [], 0, act_in, keep, anywhere=1
    )
    act_second = lax.ppermute(act_pass, "tile", swap)
    beside = [(z, z ^ 1) for z in range(chips)]
    across = [(z, z ^ 2) for z in range(chips)]
    far_in = lax.ppermute(far, "frame", beside)
    near_in = lax.ppermute(near, "frame", beside)
    (onward,) = kernel_call(
        forward_sum_kernel, [(share, bf16)], [], 0, onward, far_in, act_second, anywhere=1
    )
    last_in = lax.ppermute(onward, "frame", across)

    (input_grad,) = kernel_call(
        input_grad_kernel,
        [(flat, bf16)],
        [ext],
        product,
        grad_flat, pre_grad, pre_other, spatial_weight,
    )
    (block_out,) = kernel_call(
        temporal_kernel,
        [(flat, bf16)],
        [three],
        product,
        feat_flat, act, act_first, act_second, temporal_weight,
    )
    weight_grad = (keep + near_in.astype(f32) + last_in.astype(f32)) * scale
    return (
        block_out.reshape(clip_feats.shape),
        input_grad.reshape(clip_feats.shape),
        weight_grad,
    )


def per_device(clip_feats, *rest):
    pairs = lax.axis_size("tile") == 2 and lax.axis_size("frame") == 4
    if pairs and clip_feats.shape[0] == 4 * TAP_DILATION:
        return per_device_pair(clip_feats, *rest)
    return per_device_any(clip_feats, *rest)


def solution(mesh):
    return jax.shard_map(
        per_device,
        mesh=mesh,
        in_specs=(
            P(("clip", "frame"), "tile", None, None),
            P(("clip", "frame"), "tile", None, None),
            P(),
            P(),
        ),
        out_specs=(
            P(("clip", "frame"), "tile", None, None),
            P(("clip", "frame"), "tile", None, None),
            P(("clip", "frame", "tile"), None),
        ),
        check_vma=False,
    )
```

```python
import functools
import math

import jax
import jax.numpy as jnp
from jax import lax
from jax.experimental import pallas as pl
from jax.experimental.pallas import tpu as pltpu
from jax.sharding import PartitionSpec as P

TAP_DILATION = 2
VMEM_LIMIT = 32 * 1024 * 1024
COPYING_LIMIT = 52 * 1024 * 1024


def padded_2(block, sides, width):
    for axis, dim in sides:
        count = lax.axis_size(axis)
        forward = [(i, i + 1) for i in range(count - 1)]
        backward = [(target, source) for source, target in forward]
        low = lax.ppermute(
            lax.slice_in_dim(block, block.shape[dim] - width, None, axis=dim), axis, forward
        )
        high = lax.ppermute(lax.slice_in_dim(block, 0, width, axis=dim), axis, backward)
        block = jnp.concatenate([low, block, high], axis=dim)
    return block


def tile_columns(extended, tile_rows, width_cells, backward_pass):
    padded = jnp.pad(extended, ((0, 0), (0, 0), (1, 1), (0, 0)))
    pieces = []
    for row_shift in range(3):
        for col_shift in range(3):
            row_start = 2 - row_shift if backward_pass else row_shift
            col_start = 2 - col_shift if backward_pass else col_shift
            pieces.append(
                padded[:, row_start : row_start + tile_rows, col_start : col_start + width_cells, :]
            )
    channels = extended.shape[3]
    return jnp.concatenate(pieces, axis=-1).reshape(-1, 9 * channels)


def temporal_taps(padded_seq, weight, frame_count, backward_pass):
    pieces = []
    for temporal_tap_index in range(9):
        first_frame_index = (
            (8 - temporal_tap_index) * TAP_DILATION
            if backward_pass
            else temporal_tap_index * TAP_DILATION
        )
        pieces.append(padded_seq[first_frame_index : first_frame_index + frame_count])
    channels = padded_seq.shape[2]
    columns = jnp.concatenate(pieces, axis=-1).reshape(-1, 9 * channels)
    return jnp.dot(columns, weight, preferred_element_type=jnp.float32)


def per_device_any(clip_feats, out_grad, spatial_weight, temporal_weight):
    slab_frames, tile_rows, width_cells, channels = clip_feats.shape
    row_count = slab_frames * tile_rows * width_cells
    frame_devs = lax.axis_size("frame")
    tile_devs = lax.axis_size("tile")
    grad_scale = jnp.float32(
        1.0 / math.sqrt(slab_frames * frame_devs * tile_rows * tile_devs * width_cells)
    )
    spatial_back = (
        spatial_weight.reshape(9, channels, channels)
        .transpose(0, 2, 1)
        .reshape(9 * channels, channels)
    )
    temporal_back = (
        temporal_weight.reshape(9, channels, channels)
        .transpose(0, 2, 1)
        .reshape(9 * channels, channels)
    )
    feat_ext = padded_2(clip_feats, (("tile", 1),), 1)
    feat_columns = tile_columns(feat_ext, tile_rows, width_cells, False)
    pre = jnp.dot(feat_columns, spatial_weight, preferred_element_type=jnp.float32)
    act = jax.nn.silu(pre).astype(jnp.bfloat16)
    temporal_reach = 4 * TAP_DILATION
    per_group = tile_rows * width_cells // frame_devs
    grouped = (slab_frames, frame_devs, per_group, channels)
    act_part = lax.all_to_all(
        act.reshape(grouped), "frame", split_axis=1, concat_axis=0, tiled=True
    )
    grad_part = lax.all_to_all(out_grad, "frame", split_axis=1, concat_axis=0, tiled=True)
    feat_part = lax.all_to_all(clip_feats, "frame", split_axis=1, concat_axis=0, tiled=True)
    frame_count = act_part.shape[0]
    item_count = act_part.shape[2]
    act_pad = jnp.pad(
        act_part.reshape(frame_count, item_count, channels),
        ((temporal_reach, temporal_reach), (0, 0), (0, 0)),
    )
    grad_pad = jnp.pad(
        grad_part.reshape(frame_count, item_count, channels),
        ((temporal_reach, temporal_reach), (0, 0), (0, 0)),
    )
    mixed = temporal_taps(act_pad, temporal_weight, frame_count, False)
    out_part = (feat_part.reshape(-1, channels).astype(jnp.float32) + mixed).astype(jnp.bfloat16)
    back_part = temporal_taps(grad_pad, temporal_back, frame_count, True).astype(jnp.bfloat16)
    out_part = out_part.reshape(frame_count, 1, item_count, channels)
    back_part = back_part.reshape(frame_count, 1, item_count, channels)
    out_slab = lax.all_to_all(out_part, "frame", split_axis=0, concat_axis=1, tiled=True)
    grad_slab = lax.all_to_all(back_part, "frame", split_axis=0, concat_axis=1, tiled=True)
    act_grad = grad_slab.reshape(row_count, channels)
    sig = jax.nn.sigmoid(pre)
    pre_grad = (act_grad.astype(jnp.float32) * (sig * (1.0 + pre * (1.0 - sig)))).astype(
        jnp.bfloat16
    )
    full_term = lax.dot_general(
        feat_columns, pre_grad, (((0,), (0,)), ((), ())), preferred_element_type=jnp.float32
    )
    summed = lax.psum_scatter(full_term, ("frame", "tile"), scatter_dimension=0, tiled=True)
    weight_grad = summed * grad_scale
    grad_ext = padded_2(
        pre_grad.reshape(slab_frames, tile_rows, width_cells, channels), (("tile", 1),), 1
    )
    grad_columns = tile_columns(grad_ext, tile_rows, width_cells, True)
    local_back = jnp.dot(grad_columns, spatial_back, preferred_element_type=jnp.float32)
    input_grad = (out_grad.reshape(row_count, channels).astype(jnp.float32) + local_back).astype(
        jnp.bfloat16
    )
    input_grad = input_grad.reshape(slab_frames, tile_rows, width_cells, channels)
    return (out_slab, input_grad, weight_grad)


def kernel_call(body, outs, scratch, flops, *args, copied=0, anywhere=0, room=VMEM_LIMIT):
    moved = sum(a.size * a.dtype.itemsize for a in args)
    moved += sum(math.prod(shape) * jnp.dtype(kind).itemsize for shape, kind in outs)
    spaces = [pltpu.HBM] * copied + [pltpu.VMEM] * (len(args) - copied - anywhere) + [pl.ANY] * anywhere
    semaphores = [pltpu.SemaphoreType.DMA((copied,))] if copied else []
    return pl.pallas_call(
        body,
        out_shape=tuple(jax.ShapeDtypeStruct(shape, kind) for shape, kind in outs),
        in_specs=[pl.BlockSpec(memory_space=space) for space in spaces],
        out_specs=tuple(pl.BlockSpec(memory_space=pltpu.VMEM) for _ in outs),
        scratch_shapes=[pltpu.VMEM(shape, kind) for shape, kind in scratch] + semaphores,
        compiler_params=pltpu.CompilerParams(vmem_limit_bytes=room),
        cost_estimate=pl.CostEstimate(flops=flops, bytes_accessed=moved, transcendentals=0),
    )(*args)


def shifted(values, width, step):
    rows = values.shape[0]
    at = lax.broadcasted_iota(jnp.int32, values.shape, 0) % width
    moved = pltpu.roll(values, step % rows, 0)
    inside = at >= step if step > 0 else at < width + step
    return jnp.where(inside, moved, 0.0)


def column_shifts(values, width):
    wide = values.astype(jnp.float32)
    return (
        shifted(wide, width, 1).astype(values.dtype),
        values,
        shifted(wide, width, -1).astype(values.dtype),
    )


def with_edges(own, other, ext):
    rows = own.shape[1]
    tile = lax.axis_index("tile")
    ext[:, 1 : rows + 1] = own[...]
    above, below = other[:, rows - 1], other[:, 0]
    ext[:, 0] = jnp.where(tile == 1, above, jnp.zeros_like(above))
    ext[:, rows + 1] = jnp.where(tile == 0, below, jnp.zeros_like(below))


def whole_image(own, other, image):
    rows = own.shape[1]
    tile = lax.axis_index("tile")
    image[:, 0] = jnp.zeros_like(image[:, 0])
    image[:, 2 * rows + 1] = jnp.zeros_like(image[:, 2 * rows + 1])
    image[:, pl.ds(1 + tile * rows, rows)] = own[...]
    image[:, pl.ds(1 + (1 - tile) * rows, rows)] = other[...]


def spatial_kernel(own_hbm, weight_hbm, other, pre_ref, act_ref, image, weight, pre_all, sems):
    frames, rows, width, channels = other.shape
    tile = lax.axis_index("tile")
    copies = (
        pltpu.make_async_copy(own_hbm, image.at[:, pl.ds(1 + tile * rows, rows)], sems.at[0]),
        pltpu.make_async_copy(weight_hbm, weight, sems.at[1]),
    )
    for copy in copies:
        copy.start()
    image[:, 0] = jnp.zeros_like(image[:, 0])
    image[:, 2 * rows + 1] = jnp.zeros_like(image[:, 2 * rows + 1])
    image[:, pl.ds(1 + (1 - tile) * rows, rows)] = other[...]
    copies[0].wait()
    shifts = column_shifts(image[...].reshape(-1, channels), width)
    shifts = [piece.reshape(image.shape) for piece in shifts]
    copies[1].wait()
    for half in range(2):
        columns = jnp.concatenate(
            [
                shifts[s][:, half * rows + r : half * rows + r + rows].reshape(-1, channels)
                for r in range(3)
                for s in range(3)
            ],
            axis=1,
        )
        pre = jnp.dot(columns, weight[...], preferred_element_type=jnp.float32)
        pre_all[half] = pre
        act_ref[half] = (pre * jax.nn.sigmoid(pre)).astype(jnp.bfloat16)
    pre_ref[...] = pre_all[tile]


def split_kernel(arrived, near, _, mine_ref, other_ref, near_ref):
    tile = lax.axis_index("tile")
    near_ref[...] = near[...]
    mine_ref[...] = arrived[tile]
    other_ref[...] = arrived[1 - tile]


def forward_sum_kernel(partial, arrived, sum_ref):
    sum_ref[...] = (partial[...] + arrived[...].astype(jnp.float32)).astype(sum_ref.dtype)


def last_sum_kernel(keep, near, last, _, out_ref, *, scale):
    total = keep[...] + near[...].astype(jnp.float32) + last[...].astype(jnp.float32)
    out_ref[...] = total * scale


def transpose_kernel(own, other, out_ref, image):
    frames, rows, width, channels = own.shape
    tile = lax.axis_index("tile")
    whole_image(own, other, image)
    for which, first in enumerate((tile * rows, (1 - tile) * rows)):
        for r in range(3):
            block = image[:, pl.ds(first + r, rows)].reshape(-1, channels)
            out_ref[which, r * channels : (r + 1) * channels] = block.T


def slabs(own, first, second, ext):
    tile = lax.axis_index("tile")
    ext[2 * tile] = first[...]
    ext[1] = own[...]
    ext[2 - 2 * tile] = second[...]
    return ext[...].reshape(-1, own.shape[1])


def act_grad_kernel(own, first_in, second_in, weight, pre_ref, out_ref, ext):
    count, channels = own.shape
    frames = slabs(own, first_in, second_in, ext)
    hop = count // 4
    total = None
    for k in range(9):
        first = (8 - k) * hop
        term = lax.dot_general(
            frames[first : first + count],
            weight[k * channels : (k + 1) * channels],
            (((1,), (1,)), ((), ())),
            preferred_element_type=jnp.float32,
        )
        total = term if total is None else total + term
    act_grad = total.astype(jnp.bfloat16).astype(jnp.float32)
    pre = pre_ref[...]
    sig = jax.nn.sigmoid(pre)
    out_ref[...] = (act_grad * (sig * (1.0 + pre * (1.0 - sig)))).astype(jnp.bfloat16)


def temporal_kernel(feats, act, first_in, second_in, weight, out_ref, done_ref, ext):
    count, channels = feats.shape
    own = act.at[lax.axis_index("tile")]
    frames = slabs(own, first_in, second_in, ext)
    hop = count // 4
    columns = jnp.concatenate([frames[k * hop : k * hop + count] for k in range(9)], axis=1)
    mixed = jnp.dot(columns, weight[...], preferred_element_type=jnp.float32)
    out_ref[...] = (feats[...].astype(jnp.float32) + mixed).astype(jnp.bfloat16)
    done_ref[...] = jnp.zeros_like(done_ref)


def own_term_kernel(feats_t, own, total_ref):
    channels = own.shape[3]
    after, same, before = column_shifts(own[...].reshape(-1, channels), own.shape[2])
    left = feats_t[0]
    for s, right in enumerate((before, same, after)):
        total_ref[s] = jnp.dot(left, right, preferred_element_type=jnp.float32)


def kernel_grad_kernel(feats_t, other, term, far_ref, pass_ref, near_ref, keep_ref, total):
    frames, rows, width, channels = other.shape
    tile = lax.axis_index("tile")
    chip = lax.axis_index("frame")
    after, same, before = column_shifts(other[...].reshape(-1, channels), width)
    left = feats_t[1]
    for s, right in enumerate((before, same, after)):
        both = term[s] + jnp.dot(left, right, preferred_element_type=jnp.float32)
        for r in range(3):
            tap = 3 * r + s
            total[tap * channels : (tap + 1) * channels] = both[r * channels : (r + 1) * channels]
    share = keep_ref.shape[0]
    for distance, ref in ((3, far_ref), (2, pass_ref), (1, near_ref), (0, keep_ref)):
        first = (2 * (chip ^ distance) + tile) * share
        ref[...] = total[pl.ds(pl.multiple_of(first, 32), share)].astype(ref.dtype)


def input_grad_kernel(out_grad, own, other, weight, out_ref, ext):
    frames, rows, width, channels = own.shape
    with_edges(own, other, ext)
    after, same, before = column_shifts(ext[...].reshape(-1, channels), width)
    shifts = [piece.reshape(ext.shape) for piece in (before, same, after)]
    total = out_grad[...].astype(jnp.float32)
    for r in range(3):
        for s in range(3):
            tap = 3 * r + s
            total = total + lax.dot_general(
                shifts[s][:, 2 - r : 2 - r + rows].reshape(-1, channels),
                weight[tap * channels : (tap + 1) * channels],
                (((1,), (1,)), ((), ())),
                preferred_element_type=jnp.float32,
            )
    out_ref[...] = total.astype(jnp.bfloat16)


def per_device_pair(clip_feats, out_grad, spatial_weight, temporal_weight):
    frames, rows, width, channels = clip_feats.shape
    count = frames * rows * width
    chips = lax.axis_size("frame")
    cores = lax.axis_size("tile")
    scale = 1.0 / math.sqrt(frames * chips * rows * cores * width)
    outward = [(2 * z, 2 * z + 2) for z in range(chips - 1)]
    outward += [(2 * z + 3, 2 * z + 1) for z in range(chips - 1)]
    inward = [(target, source) for source, target in outward]
    both = ("frame", "tile")
    swap = [(0, 1), (1, 0)]
    bf16, f32 = jnp.bfloat16, jnp.float32
    product = 2 * count * 9 * channels * channels
    flat = (count, channels)
    ext = ((frames, rows + 2, width, channels), bf16)
    image = ((frames, 2 * rows + 2, width, channels), bf16)
    three = ((3, count, channels), bf16)

    grad_flat = out_grad.reshape(flat)
    feat_flat = clip_feats.reshape(flat)
    grad_first = lax.ppermute(grad_flat, both, outward)
    grad_second = lax.ppermute(grad_flat, both, inward)
    feat_other = lax.ppermute(clip_feats, "tile", swap)

    pre, act = kernel_call(
        spatial_kernel,
        [(flat, f32), ((2, *flat), bf16)],
        [image, (spatial_weight.shape, bf16), ((2, *flat), f32)],
        2 * product,
        clip_feats, spatial_weight, feat_other, copied=2, room=COPYING_LIMIT,
    )
    act_in = lax.ppermute(act, both, outward)
    (feats_t,) = kernel_call(
        transpose_kernel,
        [((2, 3 * channels, count), bf16)],
        [image],
        0,
        clip_feats, feat_other,
    )
    (pre_grad,) = kernel_call(
        act_grad_kernel,
        [(flat, bf16)],
        [three],
        product,
        grad_flat, grad_first, grad_second, temporal_weight, pre,
    )
    pre_grad = pre_grad.reshape(clip_feats.shape)
    pre_other = lax.ppermute(pre_grad, "tile", swap)

    share = (9 * channels // (chips * cores), channels)
    (term,) = kernel_call(
        own_term_kernel,
        [((3, 3 * channels, channels), f32)],
        [],
        product,
        feats_t, pre_grad,
    )
    far, onward, near, keep = kernel_call(
        kernel_grad_kernel,
        [(share, bf16), (share, f32), (share, bf16), (share, f32)],
        [((9 * channels, channels), f32)],
        product,
        feats_t, pre_other, term,
    )
    beside = [(z, z ^ 1) for z in range(chips)]
    across = [(z, z ^ 2) for z in range(chips)]
    far_in = lax.ppermute(far, "frame", beside)
    (onward,) = kernel_call(forward_sum_kernel, [(share, bf16)], [], 0, onward, far_in)
    last_in = lax.ppermute(onward, "frame", across)
    act_first, act_pass, near = kernel_call(
        split_kernel,
        [(flat, bf16), (flat, bf16), (share, bf16)],
        [],
        0,
        act_in, near, onward, anywhere=1,
    )
    near_in = lax.ppermute(near, "frame", beside)
    act_second = lax.ppermute(act_pass, "tile", swap)

    (input_grad,) = kernel_call(
        input_grad_kernel,
        [(flat, bf16)],
        [ext],
        product,
        grad_flat, pre_grad, pre_other, spatial_weight,
    )
    block_out, done = kernel_call(
        temporal_kernel,
        [(flat, bf16), ((8, 128), f32)],
        [three],
        product,
        feat_flat, act, act_first, act_second, temporal_weight,
    )
    (weight_grad,) = kernel_call(
        functools.partial(last_sum_kernel, scale=scale),
        [(share, f32)],
        [],
        0,
        keep, near_in, last_in, done, anywhere=1,
    )
    return (
        block_out.reshape(clip_feats.shape),
        input_grad.reshape(clip_feats.shape),
        weight_grad,
    )


def per_device(clip_feats, *rest):
    pairs = lax.axis_size("tile") == 2 and lax.axis_size("frame") == 4
    if pairs and clip_feats.shape[0] == 4 * TAP_DILATION:
        return per_device_pair(clip_feats, *rest)
    return per_device_any(clip_feats, *rest)


def solution(mesh):
    return jax.shard_map(
        per_device,
        mesh=mesh,
        in_specs=(
            P(("clip", "frame"), "tile", None, None),
            P(("clip", "frame"), "tile", None, None),
            P(),
            P(),
        ),
        out_specs=(
            P(("clip", "frame"), "tile", None, None),
            P(("clip", "frame"), "tile", None, None),
            P(("clip", "frame", "tile"), None),
        ),
        check_vma=False,
    )
```

```python
import functools
import math

import jax
import jax.numpy as jnp
from jax import lax
from jax.experimental import pallas as pl
from jax.experimental.pallas import tpu as pltpu
from jax.sharding import PartitionSpec as P

TAP_DILATION = 2
VMEM_LIMIT = 32 * 1024 * 1024


def padded_2(block, sides, width):
    for axis, dim in sides:
        count = lax.axis_size(axis)
        forward = [(i, i + 1) for i in range(count - 1)]
        backward = [(target, source) for source, target in forward]
        low = lax.ppermute(
            lax.slice_in_dim(block, block.shape[dim] - width, None, axis=dim), axis, forward
        )
        high = lax.ppermute(lax.slice_in_dim(block, 0, width, axis=dim), axis, backward)
        block = jnp.concatenate([low, block, high], axis=dim)
    return block


def tile_columns(extended, tile_rows, width_cells, backward_pass):
    padded = jnp.pad(extended, ((0, 0), (0, 0), (1, 1), (0, 0)))
    pieces = []
    for row_shift in range(3):
        for col_shift in range(3):
            row_start = 2 - row_shift if backward_pass else row_shift
            col_start = 2 - col_shift if backward_pass else col_shift
            pieces.append(
                padded[:, row_start : row_start + tile_rows, col_start : col_start + width_cells, :]
            )
    channels = extended.shape[3]
    return jnp.concatenate(pieces, axis=-1).reshape(-1, 9 * channels)


def temporal_taps(padded_seq, weight, frame_count, backward_pass):
    pieces = []
    for temporal_tap_index in range(9):
        first_frame_index = (
            (8 - temporal_tap_index) * TAP_DILATION
            if backward_pass
            else temporal_tap_index * TAP_DILATION
        )
        pieces.append(padded_seq[first_frame_index : first_frame_index + frame_count])
    channels = padded_seq.shape[2]
    columns = jnp.concatenate(pieces, axis=-1).reshape(-1, 9 * channels)
    return jnp.dot(columns, weight, preferred_element_type=jnp.float32)


def per_device_any(clip_feats, out_grad, spatial_weight, temporal_weight):
    slab_frames, tile_rows, width_cells, channels = clip_feats.shape
    row_count = slab_frames * tile_rows * width_cells
    frame_devs = lax.axis_size("frame")
    tile_devs = lax.axis_size("tile")
    grad_scale = jnp.float32(
        1.0 / math.sqrt(slab_frames * frame_devs * tile_rows * tile_devs * width_cells)
    )
    spatial_back = (
        spatial_weight.reshape(9, channels, channels)
        .transpose(0, 2, 1)
        .reshape(9 * channels, channels)
    )
    temporal_back = (
        temporal_weight.reshape(9, channels, channels)
        .transpose(0, 2, 1)
        .reshape(9 * channels, channels)
    )
    feat_ext = padded_2(clip_feats, (("tile", 1),), 1)
    feat_columns = tile_columns(feat_ext, tile_rows, width_cells, False)
    pre = jnp.dot(feat_columns, spatial_weight, preferred_element_type=jnp.float32)
    act = jax.nn.silu(pre).astype(jnp.bfloat16)
    temporal_reach = 4 * TAP_DILATION
    per_group = tile_rows * width_cells // frame_devs
    grouped = (slab_frames, frame_devs, per_group, channels)
    act_part = lax.all_to_all(
        act.reshape(grouped), "frame", split_axis=1, concat_axis=0, tiled=True
    )
    grad_part = lax.all_to_all(out_grad, "frame", split_axis=1, concat_axis=0, tiled=True)
    feat_part = lax.all_to_all(clip_feats, "frame", split_axis=1, concat_axis=0, tiled=True)
    frame_count = act_part.shape[0]
    item_count = act_part.shape[2]
    act_pad = jnp.pad(
        act_part.reshape(frame_count, item_count, channels),
        ((temporal_reach, temporal_reach), (0, 0), (0, 0)),
    )
    grad_pad = jnp.pad(
        grad_part.reshape(frame_count, item_count, channels),
        ((temporal_reach, temporal_reach), (0, 0), (0, 0)),
    )
    mixed = temporal_taps(act_pad, temporal_weight, frame_count, False)
    out_part = (feat_part.reshape(-1, channels).astype(jnp.float32) + mixed).astype(jnp.bfloat16)
    back_part = temporal_taps(grad_pad, temporal_back, frame_count, True).astype(jnp.bfloat16)
    out_part = out_part.reshape(frame_count, 1, item_count, channels)
    back_part = back_part.reshape(frame_count, 1, item_count, channels)
    out_slab = lax.all_to_all(out_part, "frame", split_axis=0, concat_axis=1, tiled=True)
    grad_slab = lax.all_to_all(back_part, "frame", split_axis=0, concat_axis=1, tiled=True)
    act_grad = grad_slab.reshape(row_count, channels)
    sig = jax.nn.sigmoid(pre)
    pre_grad = (act_grad.astype(jnp.float32) * (sig * (1.0 + pre * (1.0 - sig)))).astype(
        jnp.bfloat16
    )
    full_term = lax.dot_general(
        feat_columns, pre_grad, (((0,), (0,)), ((), ())), preferred_element_type=jnp.float32
    )
    summed = lax.psum_scatter(full_term, ("frame", "tile"), scatter_dimension=0, tiled=True)
    weight_grad = summed * grad_scale
    grad_ext = padded_2(
        pre_grad.reshape(slab_frames, tile_rows, width_cells, channels), (("tile", 1),), 1
    )
    grad_columns = tile_columns(grad_ext, tile_rows, width_cells, True)
    local_back = jnp.dot(grad_columns, spatial_back, preferred_element_type=jnp.float32)
    input_grad = (out_grad.reshape(row_count, channels).astype(jnp.float32) + local_back).astype(
        jnp.bfloat16
    )
    input_grad = input_grad.reshape(slab_frames, tile_rows, width_cells, channels)
    return (out_slab, input_grad, weight_grad)


def kernel_call(body, outs, scratch, flops, *args, anywhere=0):
    moved = sum(a.size * a.dtype.itemsize for a in args)
    moved += sum(math.prod(shape) * jnp.dtype(kind).itemsize for shape, kind in outs)
    spaces = [pltpu.VMEM] * (len(args) - anywhere) + [pl.ANY] * anywhere
    return pl.pallas_call(
        body,
        out_shape=tuple(jax.ShapeDtypeStruct(shape, kind) for shape, kind in outs),
        in_specs=[pl.BlockSpec(memory_space=space) for space in spaces],
        out_specs=tuple(pl.BlockSpec(memory_space=pltpu.VMEM) for _ in outs),
        scratch_shapes=[pltpu.VMEM(shape, kind) for shape, kind in scratch],
        compiler_params=pltpu.CompilerParams(vmem_limit_bytes=VMEM_LIMIT),
        cost_estimate=pl.CostEstimate(flops=flops, bytes_accessed=moved, transcendentals=0),
    )(*args)


def shifted(values, width, step):
    rows = values.shape[0]
    at = lax.broadcasted_iota(jnp.int32, values.shape, 0) % width
    moved = pltpu.roll(values, step % rows, 0)
    inside = at >= step if step > 0 else at < width + step
    return jnp.where(inside, moved, 0.0)


def column_shifts(values, width):
    wide = values.astype(jnp.float32)
    return (
        shifted(wide, width, 1).astype(values.dtype),
        values,
        shifted(wide, width, -1).astype(values.dtype),
    )


def with_edges(own, other, ext):
    rows = own.shape[1]
    tile = lax.axis_index("tile")
    ext[:, 1 : rows + 1] = own[...]
    above, below = other[:, rows - 1], other[:, 0]
    ext[:, 0] = jnp.where(tile == 1, above, jnp.zeros_like(above))
    ext[:, rows + 1] = jnp.where(tile == 0, below, jnp.zeros_like(below))


def whole_image(own, other, image):
    rows = own.shape[1]
    tile = lax.axis_index("tile")
    image[:, 0] = jnp.zeros_like(image[:, 0])
    image[:, 2 * rows + 1] = jnp.zeros_like(image[:, 2 * rows + 1])
    image[:, pl.ds(1 + tile * rows, rows)] = own[...]
    image[:, pl.ds(1 + (1 - tile) * rows, rows)] = other[...]


def first_kernel(out_ref):
    out_ref[...] = jnp.zeros_like(out_ref)


def spatial_kernel(own, weight, other, _, pre_ref, act_ref, image, pre_all):
    frames, rows, width, channels = own.shape
    whole_image(own, other, image)
    shifts = column_shifts(image[...].reshape(-1, channels), width)
    shifts = [piece.reshape(image.shape) for piece in shifts]
    for half in range(2):
        columns = jnp.concatenate(
            [
                shifts[s][:, half * rows + r : half * rows + r + rows].reshape(-1, channels)
                for r in range(3)
                for s in range(3)
            ],
            axis=1,
        )
        pre = jnp.dot(columns, weight[...], preferred_element_type=jnp.float32)
        pre_all[half] = pre
        act_ref[half] = (pre * jax.nn.sigmoid(pre)).astype(jnp.bfloat16)
    pre_ref[...] = pre_all[lax.axis_index("tile")]


def split_kernel(arrived, near, _, mine_ref, other_ref, near_ref):
    tile = lax.axis_index("tile")
    near_ref[...] = near[...]
    mine_ref[...] = arrived[tile]
    other_ref[...] = arrived[1 - tile]


def forward_sum_kernel(partial, arrived, sum_ref):
    sum_ref[...] = (partial[...] + arrived[...].astype(jnp.float32)).astype(sum_ref.dtype)


def last_sum_kernel(keep, near, last, _, out_ref, *, scale):
    total = keep[...] + near[...].astype(jnp.float32) + last[...].astype(jnp.float32)
    out_ref[...] = total * scale


def transpose_kernel(own, other, out_ref, image):
    frames, rows, width, channels = own.shape
    tile = lax.axis_index("tile")
    whole_image(own, other, image)
    for which, first in enumerate((tile * rows, (1 - tile) * rows)):
        for r in range(3):
            block = image[:, pl.ds(first + r, rows)].reshape(-1, channels)
            out_ref[which, r * channels : (r + 1) * channels] = block.T


def slabs(own, first, second, ext):
    tile = lax.axis_index("tile")
    ext[2 * tile] = first[...]
    ext[1] = own[...]
    ext[2 - 2 * tile] = second[...]
    return ext[...].reshape(-1, own.shape[1])


def act_grad_kernel(own, first_in, second_in, weight, pre_ref, out_ref, ext):
    count, channels = own.shape
    frames = slabs(own, first_in, second_in, ext)
    hop = count // 4
    total = None
    for k in range(9):
        first = (8 - k) * hop
        term = lax.dot_general(
            frames[first : first + count],
            weight[k * channels : (k + 1) * channels],
            (((1,), (1,)), ((), ())),
            preferred_element_type=jnp.float32,
        )
        total = term if total is None else total + term
    act_grad = total.astype(jnp.bfloat16).astype(jnp.float32)
    pre = pre_ref[...]
    sig = jax.nn.sigmoid(pre)
    out_ref[...] = (act_grad * (sig * (1.0 + pre * (1.0 - sig)))).astype(jnp.bfloat16)


def temporal_kernel(feats, act, first_in, second_in, weight, out_ref, done_ref, ext):
    count, channels = feats.shape
    own = act.at[lax.axis_index("tile")]
    frames = slabs(own, first_in, second_in, ext)
    hop = count // 4
    columns = jnp.concatenate([frames[k * hop : k * hop + count] for k in range(9)], axis=1)
    mixed = jnp.dot(columns, weight[...], preferred_element_type=jnp.float32)
    out_ref[...] = (feats[...].astype(jnp.float32) + mixed).astype(jnp.bfloat16)
    done_ref[...] = jnp.zeros_like(done_ref)


def own_term_kernel(feats_t, own, total_ref):
    channels = own.shape[3]
    after, same, before = column_shifts(own[...].reshape(-1, channels), own.shape[2])
    left = feats_t[0]
    for s, right in enumerate((before, same, after)):
        total_ref[s] = jnp.dot(left, right, preferred_element_type=jnp.float32)


def kernel_grad_kernel(feats_t, other, term, far_ref, pass_ref, near_ref, keep_ref, total):
    frames, rows, width, channels = other.shape
    tile = lax.axis_index("tile")
    chip = lax.axis_index("frame")
    after, same, before = column_shifts(other[...].reshape(-1, channels), width)
    left = feats_t[1]
    for s, right in enumerate((before, same, after)):
        both = term[s] + jnp.dot(left, right, preferred_element_type=jnp.float32)
        for r in range(3):
            tap = 3 * r + s
            total[tap * channels : (tap + 1) * channels] = both[r * channels : (r + 1) * channels]
    share = keep_ref.shape[0]
    for distance, ref in ((3, far_ref), (2, pass_ref), (1, near_ref), (0, keep_ref)):
        first = (2 * (chip ^ distance) + tile) * share
        ref[...] = total[pl.ds(pl.multiple_of(first, 32), share)].astype(ref.dtype)


def input_grad_kernel(out_grad, own, other, weight, out_ref, ext):
    frames, rows, width, channels = own.shape
    with_edges(own, other, ext)
    after, same, before = column_shifts(ext[...].reshape(-1, channels), width)
    shifts = [piece.reshape(ext.shape) for piece in (before, same, after)]
    total = out_grad[...].astype(jnp.float32)
    for r in range(3):
        for s in range(3):
            tap = 3 * r + s
            total = total + lax.dot_general(
                shifts[s][:, 2 - r : 2 - r + rows].reshape(-1, channels),
                weight[tap * channels : (tap + 1) * channels],
                (((1,), (1,)), ((), ())),
                preferred_element_type=jnp.float32,
            )
    out_ref[...] = total.astype(jnp.bfloat16)


def per_device_pair(clip_feats, out_grad, spatial_weight, temporal_weight):
    frames, rows, width, channels = clip_feats.shape
    count = frames * rows * width
    chips = lax.axis_size("frame")
    cores = lax.axis_size("tile")
    scale = 1.0 / math.sqrt(frames * chips * rows * cores * width)
    outward = [(2 * z, 2 * z + 2) for z in range(chips - 1)]
    outward += [(2 * z + 3, 2 * z + 1) for z in range(chips - 1)]
    inward = [(target, source) for source, target in outward]
    both = ("frame", "tile")
    swap = [(0, 1), (1, 0)]
    bf16, f32 = jnp.bfloat16, jnp.float32
    product = 2 * count * 9 * channels * channels
    flat = (count, channels)
    ext = ((frames, rows + 2, width, channels), bf16)
    image = ((frames, 2 * rows + 2, width, channels), bf16)
    three = ((3, count, channels), bf16)

    grad_flat = out_grad.reshape(flat)
    feat_flat = clip_feats.reshape(flat)
    grad_first = lax.ppermute(grad_flat, both, outward)
    grad_second = lax.ppermute(grad_flat, both, inward)
    feat_other = lax.ppermute(clip_feats, "tile", swap)

    (first,) = kernel_call(first_kernel, [((8, 128), f32)], [], 5 * product)
    pre, act = kernel_call(
        spatial_kernel,
        [(flat, f32), ((2, *flat), bf16)],
        [image, ((2, *flat), f32)],
        2 * product,
        clip_feats, spatial_weight, feat_other, first, anywhere=1,
    )
    act_in = lax.ppermute(act, both, outward)
    (feats_t,) = kernel_call(
        transpose_kernel,
        [((2, 3 * channels, count), bf16)],
        [image],
        0,
        clip_feats, feat_other,
    )
    (pre_grad,) = kernel_call(
        act_grad_kernel,
        [(flat, bf16)],
        [three],
        product,
        grad_flat, grad_first, grad_second, temporal_weight, pre,
    )
    pre_grad = pre_grad.reshape(clip_feats.shape)
    pre_other = lax.ppermute(pre_grad, "tile", swap)

    share = (9 * channels // (chips * cores), channels)
    (term,) = kernel_call(
        own_term_kernel,
        [((3, 3 * channels, channels), f32)],
        [],
        product,
        feats_t, pre_grad,
    )
    far, onward, near, keep = kernel_call(
        kernel_grad_kernel,
        [(share, bf16), (share, f32), (share, bf16), (share, f32)],
        [((9 * channels, channels), f32)],
        product,
        feats_t, pre_other, term,
    )
    beside = [(z, z ^ 1) for z in range(chips)]
    across = [(z, z ^ 2) for z in range(chips)]
    far_in = lax.ppermute(far, "frame", beside)
    (onward,) = kernel_call(forward_sum_kernel, [(share, bf16)], [], 0, onward, far_in)
    last_in = lax.ppermute(onward, "frame", across)
    act_first, act_pass, near = kernel_call(
        split_kernel,
        [(flat, bf16), (flat, bf16), (share, bf16)],
        [],
        0,
        act_in, near, onward, anywhere=1,
    )
    near_in = lax.ppermute(near, "frame", beside)
    act_second = lax.ppermute(act_pass, "tile", swap)

    (input_grad,) = kernel_call(
        input_grad_kernel,
        [(flat, bf16)],
        [ext],
        product,
        grad_flat, pre_grad, pre_other, spatial_weight,
    )
    block_out, done = kernel_call(
        temporal_kernel,
        [(flat, bf16), ((8, 128), f32)],
        [three],
        product,
        feat_flat, act, act_first, act_second, temporal_weight,
    )
    (weight_grad,) = kernel_call(
        functools.partial(last_sum_kernel, scale=scale),
        [(share, f32)],
        [],
        0,
        keep, near_in, last_in, done, anywhere=1,
    )
    return (
        block_out.reshape(clip_feats.shape),
        input_grad.reshape(clip_feats.shape),
        weight_grad,
    )


def per_device(clip_feats, *rest):
    pairs = lax.axis_size("tile") == 2 and lax.axis_size("frame") == 4
    if pairs and clip_feats.shape[0] == 4 * TAP_DILATION:
        return per_device_pair(clip_feats, *rest)
    return per_device_any(clip_feats, *rest)


def solution(mesh):
    return jax.shard_map(
        per_device,
        mesh=mesh,
        in_specs=(
            P(("clip", "frame"), "tile", None, None),
            P(("clip", "frame"), "tile", None, None),
            P(),
            P(),
        ),
        out_specs=(
            P(("clip", "frame"), "tile", None, None),
            P(("clip", "frame"), "tile", None, None),
            P(("clip", "frame", "tile"), None),
        ),
        check_vma=False,
    )
```

```python
import functools
import math

import jax
import jax.numpy as jnp
from jax import lax
from jax.experimental import pallas as pl
from jax.experimental.pallas import tpu as pltpu
from jax.sharding import PartitionSpec as P

TAP_DILATION = 2
VMEM_LIMIT = 32 * 1024 * 1024


def padded_2(block, sides, width):
    for axis, dim in sides:
        count = lax.axis_size(axis)
        forward = [(i, i + 1) for i in range(count - 1)]
        backward = [(target, source) for source, target in forward]
        low = lax.ppermute(
            lax.slice_in_dim(block, block.shape[dim] - width, None, axis=dim), axis, forward
        )
        high = lax.ppermute(lax.slice_in_dim(block, 0, width, axis=dim), axis, backward)
        block = jnp.concatenate([low, block, high], axis=dim)
    return block


def tile_columns(extended, tile_rows, width_cells, backward_pass):
    padded = jnp.pad(extended, ((0, 0), (0, 0), (1, 1), (0, 0)))
    pieces = []
    for row_shift in range(3):
        for col_shift in range(3):
            row_start = 2 - row_shift if backward_pass else row_shift
            col_start = 2 - col_shift if backward_pass else col_shift
            pieces.append(
                padded[:, row_start : row_start + tile_rows, col_start : col_start + width_cells, :]
            )
    channels = extended.shape[3]
    return jnp.concatenate(pieces, axis=-1).reshape(-1, 9 * channels)


def temporal_taps(padded_seq, weight, frame_count, backward_pass):
    pieces = []
    for temporal_tap_index in range(9):
        first_frame_index = (
            (8 - temporal_tap_index) * TAP_DILATION
            if backward_pass
            else temporal_tap_index * TAP_DILATION
        )
        pieces.append(padded_seq[first_frame_index : first_frame_index + frame_count])
    channels = padded_seq.shape[2]
    columns = jnp.concatenate(pieces, axis=-1).reshape(-1, 9 * channels)
    return jnp.dot(columns, weight, preferred_element_type=jnp.float32)


def per_device_any(clip_feats, out_grad, spatial_weight, temporal_weight):
    slab_frames, tile_rows, width_cells, channels = clip_feats.shape
    row_count = slab_frames * tile_rows * width_cells
    frame_devs = lax.axis_size("frame")
    tile_devs = lax.axis_size("tile")
    grad_scale = jnp.float32(
        1.0 / math.sqrt(slab_frames * frame_devs * tile_rows * tile_devs * width_cells)
    )
    spatial_back = (
        spatial_weight.reshape(9, channels, channels)
        .transpose(0, 2, 1)
        .reshape(9 * channels, channels)
    )
    temporal_back = (
        temporal_weight.reshape(9, channels, channels)
        .transpose(0, 2, 1)
        .reshape(9 * channels, channels)
    )
    feat_ext = padded_2(clip_feats, (("tile", 1),), 1)
    feat_columns = tile_columns(feat_ext, tile_rows, width_cells, False)
    pre = jnp.dot(feat_columns, spatial_weight, preferred_element_type=jnp.float32)
    act = jax.nn.silu(pre).astype(jnp.bfloat16)
    temporal_reach = 4 * TAP_DILATION
    per_group = tile_rows * width_cells // frame_devs
    grouped = (slab_frames, frame_devs, per_group, channels)
    act_part = lax.all_to_all(
        act.reshape(grouped), "frame", split_axis=1, concat_axis=0, tiled=True
    )
    grad_part = lax.all_to_all(out_grad, "frame", split_axis=1, concat_axis=0, tiled=True)
    feat_part = lax.all_to_all(clip_feats, "frame", split_axis=1, concat_axis=0, tiled=True)
    frame_count = act_part.shape[0]
    item_count = act_part.shape[2]
    act_pad = jnp.pad(
        act_part.reshape(frame_count, item_count, channels),
        ((temporal_reach, temporal_reach), (0, 0), (0, 0)),
    )
    grad_pad = jnp.pad(
        grad_part.reshape(frame_count, item_count, channels),
        ((temporal_reach, temporal_reach), (0, 0), (0, 0)),
    )
    mixed = temporal_taps(act_pad, temporal_weight, frame_count, False)
    out_part = (feat_part.reshape(-1, channels).astype(jnp.float32) + mixed).astype(jnp.bfloat16)
    back_part = temporal_taps(grad_pad, temporal_back, frame_count, True).astype(jnp.bfloat16)
    out_part = out_part.reshape(frame_count, 1, item_count, channels)
    back_part = back_part.reshape(frame_count, 1, item_count, channels)
    out_slab = lax.all_to_all(out_part, "frame", split_axis=0, concat_axis=1, tiled=True)
    grad_slab = lax.all_to_all(back_part, "frame", split_axis=0, concat_axis=1, tiled=True)
    act_grad = grad_slab.reshape(row_count, channels)
    sig = jax.nn.sigmoid(pre)
    pre_grad = (act_grad.astype(jnp.float32) * (sig * (1.0 + pre * (1.0 - sig)))).astype(
        jnp.bfloat16
    )
    full_term = lax.dot_general(
        feat_columns, pre_grad, (((0,), (0,)), ((), ())), preferred_element_type=jnp.float32
    )
    summed = lax.psum_scatter(full_term, ("frame", "tile"), scatter_dimension=0, tiled=True)
    weight_grad = summed * grad_scale
    grad_ext = padded_2(
        pre_grad.reshape(slab_frames, tile_rows, width_cells, channels), (("tile", 1),), 1
    )
    grad_columns = tile_columns(grad_ext, tile_rows, width_cells, True)
    local_back = jnp.dot(grad_columns, spatial_back, preferred_element_type=jnp.float32)
    input_grad = (out_grad.reshape(row_count, channels).astype(jnp.float32) + local_back).astype(
        jnp.bfloat16
    )
    input_grad = input_grad.reshape(slab_frames, tile_rows, width_cells, channels)
    return (out_slab, input_grad, weight_grad)


def kernel_call(body, outs, scratch, flops, *args, anywhere=0):
    moved = sum(a.size * a.dtype.itemsize for a in args)
    moved += sum(math.prod(shape) * jnp.dtype(kind).itemsize for shape, kind in outs)
    spaces = [pltpu.VMEM] * (len(args) - anywhere) + [pl.ANY] * anywhere
    return pl.pallas_call(
        body,
        out_shape=tuple(jax.ShapeDtypeStruct(shape, kind) for shape, kind in outs),
        in_specs=[pl.BlockSpec(memory_space=space) for space in spaces],
        out_specs=tuple(pl.BlockSpec(memory_space=pltpu.VMEM) for _ in outs),
        scratch_shapes=[pltpu.VMEM(shape, kind) for shape, kind in scratch],
        compiler_params=pltpu.CompilerParams(vmem_limit_bytes=VMEM_LIMIT),
        cost_estimate=pl.CostEstimate(flops=flops, bytes_accessed=moved, transcendentals=0),
    )(*args)


def shifted(values, width, step):
    rows = values.shape[0]
    at = lax.broadcasted_iota(jnp.int32, values.shape, 0) % width
    moved = pltpu.roll(values, step % rows, 0)
    inside = at >= step if step > 0 else at < width + step
    return jnp.where(inside, moved, 0.0)


def column_shifts(values, width):
    wide = values.astype(jnp.float32)
    return (
        shifted(wide, width, 1).astype(values.dtype),
        values,
        shifted(wide, width, -1).astype(values.dtype),
    )


def with_edges(own, other, ext):
    rows = own.shape[1]
    tile = lax.axis_index("tile")
    ext[:, 1 : rows + 1] = own[...]
    above, below = other[:, rows - 1], other[:, 0]
    ext[:, 0] = jnp.where(tile == 1, above, jnp.zeros_like(above))
    ext[:, rows + 1] = jnp.where(tile == 0, below, jnp.zeros_like(below))


def whole_image(own, other, image):
    rows = own.shape[1]
    tile = lax.axis_index("tile")
    image[:, 0] = jnp.zeros_like(image[:, 0])
    image[:, 2 * rows + 1] = jnp.zeros_like(image[:, 2 * rows + 1])
    image[:, pl.ds(1 + tile * rows, rows)] = own[...]
    image[:, pl.ds(1 + (1 - tile) * rows, rows)] = other[...]


def first_kernel(out_ref):
    out_ref[...] = jnp.zeros_like(out_ref)


def spatial_kernel(own, weight, other, _, pre_ref, act_ref, image, pre_all):
    frames, rows, width, channels = own.shape
    whole_image(own, other, image)
    shifts = column_shifts(image[...].reshape(-1, channels), width)
    shifts = [piece.reshape(image.shape) for piece in shifts]
    for half in range(2):
        columns = jnp.concatenate(
            [
                shifts[s][:, half * rows + r : half * rows + r + rows].reshape(-1, channels)
                for r in range(3)
                for s in range(3)
            ],
            axis=1,
        )
        pre = jnp.dot(columns, weight[...], preferred_element_type=jnp.float32)
        pre_all[half] = pre
        act_ref[half] = (pre * jax.nn.sigmoid(pre)).astype(jnp.bfloat16)
    pre_ref[...] = pre_all[lax.axis_index("tile")]


def split_kernel(arrived, near, _, mine_ref, other_ref, near_ref):
    tile = lax.axis_index("tile")
    near_ref[...] = near[...]
    mine_ref[...] = arrived[tile]
    other_ref[...] = arrived[1 - tile]


def forward_sum_kernel(partial, arrived, *rest, first):
    sum_ref = rest[-1]
    rows = partial[first : first + sum_ref.shape[0]]
    sum_ref[...] = (rows + arrived[...].astype(jnp.float32)).astype(sum_ref.dtype)


def last_sum_kernel(keep, near, last_a, last_b, _, out_ref, *, scale):
    half = last_a.shape[0]
    for first, last in ((0, last_a), (half, last_b)):
        total = keep[first : first + half] + near[first : first + half].astype(jnp.float32)
        out_ref[first : first + half] = (total + last[...].astype(jnp.float32)) * scale


def transpose_kernel(own, other, out_ref, image):
    frames, rows, width, channels = own.shape
    tile = lax.axis_index("tile")
    whole_image(own, other, image)
    for which, first in enumerate((tile * rows, (1 - tile) * rows)):
        for r in range(3):
            block = image[:, pl.ds(first + r, rows)].reshape(-1, channels)
            out_ref[which, r * channels : (r + 1) * channels] = block.T


def slabs(own, first, second, ext):
    tile = lax.axis_index("tile")
    ext[2 * tile] = first[...]
    ext[1] = own[...]
    ext[2 - 2 * tile] = second[...]
    return ext[...].reshape(-1, own.shape[1])


def act_grad_kernel(own, first_in, second_in, weight, pre_ref, out_ref, ext):
    count, channels = own.shape
    frames = slabs(own, first_in, second_in, ext)
    hop = count // 4
    total = None
    for k in range(9):
        first = (8 - k) * hop
        term = lax.dot_general(
            frames[first : first + count],
            weight[k * channels : (k + 1) * channels],
            (((1,), (1,)), ((), ())),
            preferred_element_type=jnp.float32,
        )
        total = term if total is None else total + term
    act_grad = total.astype(jnp.bfloat16).astype(jnp.float32)
    pre = pre_ref[...]
    sig = jax.nn.sigmoid(pre)
    out_ref[...] = (act_grad * (sig * (1.0 + pre * (1.0 - sig)))).astype(jnp.bfloat16)


def temporal_kernel(feats, act, first_in, second_in, weight, out_ref, done_ref, ext):
    count, channels = feats.shape
    own = act.at[lax.axis_index("tile")]
    frames = slabs(own, first_in, second_in, ext)
    hop = count // 4
    columns = jnp.concatenate([frames[k * hop : k * hop + count] for k in range(9)], axis=1)
    mixed = jnp.dot(columns, weight[...], preferred_element_type=jnp.float32)
    out_ref[...] = (feats[...].astype(jnp.float32) + mixed).astype(jnp.bfloat16)
    done_ref[...] = jnp.zeros_like(done_ref)


def own_term_kernel(feats_t, own, total_ref):
    channels = own.shape[3]
    after, same, before = column_shifts(own[...].reshape(-1, channels), own.shape[2])
    left = feats_t[0]
    for s, right in enumerate((before, same, after)):
        total_ref[s] = jnp.dot(left, right, preferred_element_type=jnp.float32)


def kernel_grad_kernel(
    feats_t, other, term, far_a_ref, far_b_ref, pass_ref, near_ref, keep_ref, total
):
    frames, rows, width, channels = other.shape
    tile = lax.axis_index("tile")
    chip = lax.axis_index("frame")
    after, same, before = column_shifts(other[...].reshape(-1, channels), width)
    left = feats_t[1]
    for s, right in enumerate((before, same, after)):
        both = term[s] + jnp.dot(left, right, preferred_element_type=jnp.float32)
        for r in range(3):
            tap = 3 * r + s
            total[tap * channels : (tap + 1) * channels] = both[r * channels : (r + 1) * channels]
    share = keep_ref.shape[0]
    half = share // 2
    for distance, skip, ref in (
        (3, 0, far_a_ref),
        (3, half, far_b_ref),
        (2, 0, pass_ref),
        (1, 0, near_ref),
        (0, 0, keep_ref),
    ):
        first = (2 * (chip ^ distance) + tile) * share + skip
        ref[...] = total[pl.ds(pl.multiple_of(first, 16), ref.shape[0])].astype(ref.dtype)


def input_grad_kernel(out_grad, own, other, weight, _, out_ref, ext):
    frames, rows, width, channels = own.shape
    with_edges(own, other, ext)
    after, same, before = column_shifts(ext[...].reshape(-1, channels), width)
    shifts = [piece.reshape(ext.shape) for piece in (before, same, after)]
    total = out_grad[...].astype(jnp.float32)
    for r in range(3):
        for s in range(3):
            tap = 3 * r + s
            total = total + lax.dot_general(
                shifts[s][:, 2 - r : 2 - r + rows].reshape(-1, channels),
                weight[tap * channels : (tap + 1) * channels],
                (((1,), (1,)), ((), ())),
                preferred_element_type=jnp.float32,
            )
    out_ref[...] = total.astype(jnp.bfloat16)


def per_device_pair(clip_feats, out_grad, spatial_weight, temporal_weight):
    frames, rows, width, channels = clip_feats.shape
    count = frames * rows * width
    chips = lax.axis_size("frame")
    cores = lax.axis_size("tile")
    scale = 1.0 / math.sqrt(frames * chips * rows * cores * width)
    outward = [(2 * z, 2 * z + 2) for z in range(chips - 1)]
    outward += [(2 * z + 3, 2 * z + 1) for z in range(chips - 1)]
    inward = [(target, source) for source, target in outward]
    both = ("frame", "tile")
    swap = [(0, 1), (1, 0)]
    bf16, f32 = jnp.bfloat16, jnp.float32
    product = 2 * count * 9 * channels * channels
    flat = (count, channels)
    ext = ((frames, rows + 2, width, channels), bf16)
    image = ((frames, 2 * rows + 2, width, channels), bf16)
    three = ((3, count, channels), bf16)

    grad_flat = out_grad.reshape(flat)
    feat_flat = clip_feats.reshape(flat)
    grad_first = lax.ppermute(grad_flat, both, outward)
    grad_second = lax.ppermute(grad_flat, both, inward)
    feat_other = lax.ppermute(clip_feats, "tile", swap)

    (first,) = kernel_call(first_kernel, [((8, 128), f32)], [], 2 * product)
    pre, act = kernel_call(
        spatial_kernel,
        [(flat, f32), ((2, *flat), bf16)],
        [image, ((2, *flat), f32)],
        2 * product,
        clip_feats, spatial_weight, feat_other, first, anywhere=1,
    )
    act_in = lax.ppermute(act, both, outward)
    (feats_t,) = kernel_call(
        transpose_kernel,
        [((2, 3 * channels, count), bf16)],
        [image],
        0,
        clip_feats, feat_other,
    )
    (pre_grad,) = kernel_call(
        act_grad_kernel,
        [(flat, bf16)],
        [three],
        product,
        grad_flat, grad_first, grad_second, temporal_weight, pre,
    )
    pre_grad = pre_grad.reshape(clip_feats.shape)
    pre_other = lax.ppermute(pre_grad, "tile", swap)

    share = (9 * channels // (chips * cores), channels)
    (term,) = kernel_call(
        own_term_kernel,
        [((3, 3 * channels, channels), f32)],
        [],
        product,
        feats_t, pre_grad,
    )
    half = (share[0] // 2, channels)
    far_a, far_b, onward, near, keep = kernel_call(
        kernel_grad_kernel,
        [(half, bf16), (half, bf16), (share, f32), (share, bf16), (share, f32)],
        [((9 * channels, channels), f32)],
        product,
        feats_t, pre_other, term,
    )
    beside = [(z, z ^ 1) for z in range(chips)]
    across = [(z, z ^ 2) for z in range(chips)]
    far_in_a = lax.ppermute(far_a, "frame", beside)
    far_in_b = lax.ppermute(far_b, "frame", beside)
    (sum_a,) = kernel_call(
        functools.partial(forward_sum_kernel, first=0), [(half, bf16)], [], 0, onward, far_in_a
    )
    last_a = lax.ppermute(sum_a, "frame", across)
    (sum_b,) = kernel_call(
        functools.partial(forward_sum_kernel, first=half[0]),
        [(half, bf16)],
        [],
        0,
        onward, far_in_b, sum_a, anywhere=1,
    )
    last_b = lax.ppermute(sum_b, "frame", across)
    act_first, act_pass, near = kernel_call(
        split_kernel,
        [(flat, bf16), (flat, bf16), (share, bf16)],
        [],
        0,
        act_in, near, sum_b, anywhere=1,
    )
    near_in = lax.ppermute(near, "frame", beside)
    act_second = lax.ppermute(act_pass, "tile", swap)

    (input_grad,) = kernel_call(
        input_grad_kernel,
        [(flat, bf16)],
        [ext],
        20 * product,
        grad_flat, pre_grad, pre_other, spatial_weight, last_a, anywhere=1,
    )
    block_out, done = kernel_call(
        temporal_kernel,
        [(flat, bf16), ((8, 128), f32)],
        [three],
        product,
        feat_flat, act, act_first, act_second, temporal_weight,
    )
    (weight_grad,) = kernel_call(
        functools.partial(last_sum_kernel, scale=scale),
        [(share, f32)],
        [],
        0,
        keep, near_in, last_a, last_b, done, anywhere=1,
    )
    return (
        block_out.reshape(clip_feats.shape),
        input_grad.reshape(clip_feats.shape),
        weight_grad,
    )


def per_device(clip_feats, *rest):
    pairs = lax.axis_size("tile") == 2 and lax.axis_size("frame") == 4
    if pairs and clip_feats.shape[0] == 4 * TAP_DILATION:
        return per_device_pair(clip_feats, *rest)
    return per_device_any(clip_feats, *rest)


def solution(mesh):
    return jax.shard_map(
        per_device,
        mesh=mesh,
        in_specs=(
            P(("clip", "frame"), "tile", None, None),
            P(("clip", "frame"), "tile", None, None),
            P(),
            P(),
        ),
        out_specs=(
            P(("clip", "frame"), "tile", None, None),
            P(("clip", "frame"), "tile", None, None),
            P(("clip", "frame", "tile"), None),
        ),
        check_vma=False,
    )
```

```python
import functools
import math

import jax
import jax.numpy as jnp
from jax import lax
from jax.experimental import pallas as pl
from jax.experimental.pallas import tpu as pltpu
from jax.sharding import PartitionSpec as P

TAP_DILATION = 2
VMEM_LIMIT = 32 * 1024 * 1024


def padded_2(block, sides, width):
    for axis, dim in sides:
        count = lax.axis_size(axis)
        forward = [(i, i + 1) for i in range(count - 1)]
        backward = [(target, source) for source, target in forward]
        low = lax.ppermute(
            lax.slice_in_dim(block, block.shape[dim] - width, None, axis=dim), axis, forward
        )
        high = lax.ppermute(lax.slice_in_dim(block, 0, width, axis=dim), axis, backward)
        block = jnp.concatenate([low, block, high], axis=dim)
    return block


def tile_columns(extended, tile_rows, width_cells, backward_pass):
    padded = jnp.pad(extended, ((0, 0), (0, 0), (1, 1), (0, 0)))
    pieces = []
    for row_shift in range(3):
        for col_shift in range(3):
            row_start = 2 - row_shift if backward_pass else row_shift
            col_start = 2 - col_shift if backward_pass else col_shift
            pieces.append(
                padded[:, row_start : row_start + tile_rows, col_start : col_start + width_cells, :]
            )
    channels = extended.shape[3]
    return jnp.concatenate(pieces, axis=-1).reshape(-1, 9 * channels)


def temporal_taps(padded_seq, weight, frame_count, backward_pass):
    pieces = []
    for temporal_tap_index in range(9):
        first_frame_index = (
            (8 - temporal_tap_index) * TAP_DILATION
            if backward_pass
            else temporal_tap_index * TAP_DILATION
        )
        pieces.append(padded_seq[first_frame_index : first_frame_index + frame_count])
    channels = padded_seq.shape[2]
    columns = jnp.concatenate(pieces, axis=-1).reshape(-1, 9 * channels)
    return jnp.dot(columns, weight, preferred_element_type=jnp.float32)


def per_device_any(clip_feats, out_grad, spatial_weight, temporal_weight):
    slab_frames, tile_rows, width_cells, channels = clip_feats.shape
    row_count = slab_frames * tile_rows * width_cells
    frame_devs = lax.axis_size("frame")
    tile_devs = lax.axis_size("tile")
    grad_scale = jnp.float32(
        1.0 / math.sqrt(slab_frames * frame_devs * tile_rows * tile_devs * width_cells)
    )
    spatial_back = (
        spatial_weight.reshape(9, channels, channels)
        .transpose(0, 2, 1)
        .reshape(9 * channels, channels)
    )
    temporal_back = (
        temporal_weight.reshape(9, channels, channels)
        .transpose(0, 2, 1)
        .reshape(9 * channels, channels)
    )
    feat_ext = padded_2(clip_feats, (("tile", 1),), 1)
    feat_columns = tile_columns(feat_ext, tile_rows, width_cells, False)
    pre = jnp.dot(feat_columns, spatial_weight, preferred_element_type=jnp.float32)
    act = jax.nn.silu(pre).astype(jnp.bfloat16)
    temporal_reach = 4 * TAP_DILATION
    per_group = tile_rows * width_cells // frame_devs
    grouped = (slab_frames, frame_devs, per_group, channels)
    act_part = lax.all_to_all(
        act.reshape(grouped), "frame", split_axis=1, concat_axis=0, tiled=True
    )
    grad_part = lax.all_to_all(out_grad, "frame", split_axis=1, concat_axis=0, tiled=True)
    feat_part = lax.all_to_all(clip_feats, "frame", split_axis=1, concat_axis=0, tiled=True)
    frame_count = act_part.shape[0]
    item_count = act_part.shape[2]
    act_pad = jnp.pad(
        act_part.reshape(frame_count, item_count, channels),
        ((temporal_reach, temporal_reach), (0, 0), (0, 0)),
    )
    grad_pad = jnp.pad(
        grad_part.reshape(frame_count, item_count, channels),
        ((temporal_reach, temporal_reach), (0, 0), (0, 0)),
    )
    mixed = temporal_taps(act_pad, temporal_weight, frame_count, False)
    out_part = (feat_part.reshape(-1, channels).astype(jnp.float32) + mixed).astype(jnp.bfloat16)
    back_part = temporal_taps(grad_pad, temporal_back, frame_count, True).astype(jnp.bfloat16)
    out_part = out_part.reshape(frame_count, 1, item_count, channels)
    back_part = back_part.reshape(frame_count, 1, item_count, channels)
    out_slab = lax.all_to_all(out_part, "frame", split_axis=0, concat_axis=1, tiled=True)
    grad_slab = lax.all_to_all(back_part, "frame", split_axis=0, concat_axis=1, tiled=True)
    act_grad = grad_slab.reshape(row_count, channels)
    sig = jax.nn.sigmoid(pre)
    pre_grad = (act_grad.astype(jnp.float32) * (sig * (1.0 + pre * (1.0 - sig)))).astype(
        jnp.bfloat16
    )
    full_term = lax.dot_general(
        feat_columns, pre_grad, (((0,), (0,)), ((), ())), preferred_element_type=jnp.float32
    )
    summed = lax.psum_scatter(full_term, ("frame", "tile"), scatter_dimension=0, tiled=True)
    weight_grad = summed * grad_scale
    grad_ext = padded_2(
        pre_grad.reshape(slab_frames, tile_rows, width_cells, channels), (("tile", 1),), 1
    )
    grad_columns = tile_columns(grad_ext, tile_rows, width_cells, True)
    local_back = jnp.dot(grad_columns, spatial_back, preferred_element_type=jnp.float32)
    input_grad = (out_grad.reshape(row_count, channels).astype(jnp.float32) + local_back).astype(
        jnp.bfloat16
    )
    input_grad = input_grad.reshape(slab_frames, tile_rows, width_cells, channels)
    return (out_slab, input_grad, weight_grad)


def kernel_call(body, outs, scratch, flops, *args, anywhere=0):
    moved = sum(a.size * a.dtype.itemsize for a in args)
    moved += sum(math.prod(shape) * jnp.dtype(kind).itemsize for shape, kind in outs)
    spaces = [pltpu.VMEM] * (len(args) - anywhere) + [pl.ANY] * anywhere
    return pl.pallas_call(
        body,
        out_shape=tuple(jax.ShapeDtypeStruct(shape, kind) for shape, kind in outs),
        in_specs=[pl.BlockSpec(memory_space=space) for space in spaces],
        out_specs=tuple(pl.BlockSpec(memory_space=pltpu.VMEM) for _ in outs),
        scratch_shapes=[pltpu.VMEM(shape, kind) for shape, kind in scratch],
        compiler_params=pltpu.CompilerParams(vmem_limit_bytes=VMEM_LIMIT),
        cost_estimate=pl.CostEstimate(flops=flops, bytes_accessed=moved, transcendentals=0),
    )(*args)


def shifted(values, width, step):
    rows = values.shape[0]
    at = lax.broadcasted_iota(jnp.int32, values.shape, 0) % width
    moved = pltpu.roll(values, step % rows, 0)
    inside = at >= step if step > 0 else at < width + step
    return jnp.where(inside, moved, 0.0)


def column_shifts(values, width):
    wide = values.astype(jnp.float32)
    return (
        shifted(wide, width, 1).astype(values.dtype),
        values,
        shifted(wide, width, -1).astype(values.dtype),
    )


def with_edges(own, other, ext):
    rows = own.shape[1]
    tile = lax.axis_index("tile")
    ext[:, 1 : rows + 1] = own[...]
    above, below = other[:, rows - 1], other[:, 0]
    ext[:, 0] = jnp.where(tile == 1, above, jnp.zeros_like(above))
    ext[:, rows + 1] = jnp.where(tile == 0, below, jnp.zeros_like(below))


def whole_image(own, other, image):
    rows = own.shape[1]
    tile = lax.axis_index("tile")
    image[:, 0] = jnp.zeros_like(image[:, 0])
    image[:, 2 * rows + 1] = jnp.zeros_like(image[:, 2 * rows + 1])
    image[:, pl.ds(1 + tile * rows, rows)] = own[...]
    image[:, pl.ds(1 + (1 - tile) * rows, rows)] = other[...]


def order_kernel(*refs):
    refs[-1][...] = jnp.zeros_like(refs[-1])


def spatial_kernel(own, weight, other, _, pre_ref, act_ref, image, pre_all):
    frames, rows, width, channels = own.shape
    whole_image(own, other, image)
    shifts = column_shifts(image[...].reshape(-1, channels), width)
    shifts = [piece.reshape(image.shape) for piece in shifts]
    for half in range(2):
        columns = jnp.concatenate(
            [
                shifts[s][:, half * rows + r : half * rows + r + rows].reshape(-1, channels)
                for r in range(3)
                for s in range(3)
            ],
            axis=1,
        )
        pre = jnp.dot(columns, weight[...], preferred_element_type=jnp.float32)
        pre_all[half] = pre
        act_ref[half] = (pre * jax.nn.sigmoid(pre)).astype(jnp.bfloat16)
    pre_ref[...] = pre_all[lax.axis_index("tile")]


def split_kernel(arrived, _, mine_ref, other_ref):
    tile = lax.axis_index("tile")
    mine_ref[...] = arrived[tile]
    other_ref[...] = arrived[1 - tile]


def forward_sum_kernel(partial, arrived, *rest, first):
    sum_ref = rest[-1]
    rows = partial[first : first + sum_ref.shape[0]]
    came = arrived[: sum_ref.shape[0]].astype(jnp.float32)
    sum_ref[...] = (rows + came).astype(sum_ref.dtype)


def last_sum_kernel(keep, rest, last_a, last_b, _, out_ref, *, scale):
    half = last_a.shape[0]
    for first, last in ((0, last_a), (half, last_b)):
        near = rest[half + first : 2 * half + first].astype(jnp.float32)
        total = keep[first : first + half] + near
        out_ref[first : first + half] = (total + last[...].astype(jnp.float32)) * scale


def transpose_kernel(own, other, _, out_ref, image):
    frames, rows, width, channels = own.shape
    tile = lax.axis_index("tile")
    whole_image(own, other, image)
    for which, first in enumerate((tile * rows, (1 - tile) * rows)):
        for r in range(3):
            block = image[:, pl.ds(first + r, rows)].reshape(-1, channels)
            out_ref[which, r * channels : (r + 1) * channels] = block.T


def slabs(own, first, second, ext):
    tile = lax.axis_index("tile")
    ext[2 * tile] = first[...]
    ext[1] = own[...]
    ext[2 - 2 * tile] = second[...]
    chip = lax.axis_index("frame")

    @pl.when(chip == 0)
    def _():
        ext[0] = jnp.zeros_like(ext[0])

    @pl.when(chip == lax.axis_size("frame") - 1)
    def _():
        ext[2] = jnp.zeros_like(ext[2])

    return ext[...].reshape(-1, own.shape[1])


def act_grad_kernel(own, first_in, second_in, weight, pre_ref, _, out_ref, ext):
    count, channels = own.shape
    frames = slabs(own, first_in, second_in, ext)
    hop = count // 4
    total = None
    for k in range(9):
        first = (8 - k) * hop
        term = lax.dot_general(
            frames[first : first + count],
            weight[k * channels : (k + 1) * channels],
            (((1,), (1,)), ((), ())),
            preferred_element_type=jnp.float32,
        )
        total = term if total is None else total + term
    act_grad = total.astype(jnp.bfloat16).astype(jnp.float32)
    pre = pre_ref[...]
    sig = jax.nn.sigmoid(pre)
    out_ref[...] = (act_grad * (sig * (1.0 + pre * (1.0 - sig)))).astype(jnp.bfloat16)


def temporal_kernel(feats, act, first_in, second_in, weight, _, out_ref, done_ref, ext):
    count, channels = feats.shape
    own = act.at[lax.axis_index("tile")]
    frames = slabs(own, first_in, second_in, ext)
    hop = count // 4
    columns = jnp.concatenate([frames[k * hop : k * hop + count] for k in range(9)], axis=1)
    mixed = jnp.dot(columns, weight[...], preferred_element_type=jnp.float32)
    out_ref[...] = (feats[...].astype(jnp.float32) + mixed).astype(jnp.bfloat16)
    done_ref[...] = jnp.zeros_like(done_ref)


def own_term_kernel(feats_t, own, total_ref):
    channels = own.shape[3]
    after, same, before = column_shifts(own[...].reshape(-1, channels), own.shape[2])
    left = feats_t[0]
    for s, right in enumerate((before, same, after)):
        total_ref[s] = jnp.dot(left, right, preferred_element_type=jnp.float32)


def kernel_grad_kernel(
    feats_t, other, term, far_ref, rest_ref, pass_ref, keep_ref, total
):
    frames, rows, width, channels = other.shape
    tile = lax.axis_index("tile")
    chip = lax.axis_index("frame")
    after, same, before = column_shifts(other[...].reshape(-1, channels), width)
    left = feats_t[1]
    for s, right in enumerate((before, same, after)):
        both = term[s] + jnp.dot(left, right, preferred_element_type=jnp.float32)
        for r in range(3):
            tap = 3 * r + s
            total[tap * channels : (tap + 1) * channels] = both[r * channels : (r + 1) * channels]
    share = keep_ref.shape[0]
    half = share // 2
    for distance, skip, ref, at, count in (
        (3, 0, far_ref, 0, half),
        (3, half, rest_ref, 0, half),
        (1, 0, rest_ref, half, share),
        (2, 0, pass_ref, 0, share),
        (0, 0, keep_ref, 0, share),
    ):
        first = (2 * (chip ^ distance) + tile) * share + skip
        rows = total[pl.ds(pl.multiple_of(first, 16), count)]
        ref[at : at + count] = rows.astype(ref.dtype)


def input_grad_kernel(out_grad, own, other, weight, _, out_ref, done_ref, ext):
    frames, rows, width, channels = own.shape
    with_edges(own, other, ext)
    after, same, before = column_shifts(ext[...].reshape(-1, channels), width)
    shifts = [piece.reshape(ext.shape) for piece in (before, same, after)]
    total = out_grad[...].astype(jnp.float32)
    for r in range(3):
        for s in range(3):
            tap = 3 * r + s
            total = total + lax.dot_general(
                shifts[s][:, 2 - r : 2 - r + rows].reshape(-1, channels),
                weight[tap * channels : (tap + 1) * channels],
                (((1,), (1,)), ((), ())),
                preferred_element_type=jnp.float32,
            )
    out_ref[...] = total.astype(jnp.bfloat16)
    done_ref[...] = jnp.zeros_like(done_ref)


def per_device_pair(clip_feats, out_grad, spatial_weight, temporal_weight):
    frames, rows, width, channels = clip_feats.shape
    count = frames * rows * width
    chips = lax.axis_size("frame")
    cores = lax.axis_size("tile")
    scale = 1.0 / math.sqrt(frames * chips * rows * cores * width)
    outward = [(2 * z, 2 * z + 2) for z in range(chips - 1)]
    outward += [(2 * z + 3, 2 * z + 1) for z in range(chips - 1)]
    outward += [(2 * chips - 2, 2 * chips - 1), (1, 0)]
    inward = [(target, source) for source, target in outward]
    both = ("frame", "tile")
    swap = [(0, 1), (1, 0)]
    bf16, f32 = jnp.bfloat16, jnp.float32
    product = 2 * count * 9 * channels * channels
    flat = (count, channels)
    ext = ((frames, rows + 2, width, channels), bf16)
    image = ((frames, 2 * rows + 2, width, channels), bf16)
    three = ((3, count, channels), bf16)

    grad_flat = out_grad.reshape(flat)
    feat_flat = clip_feats.reshape(flat)
    grad_first = lax.ppermute(grad_flat, both, outward)
    grad_second = lax.ppermute(grad_flat, both, inward)
    feat_other = lax.ppermute(clip_feats, "tile", swap)

    (first,) = kernel_call(order_kernel, [((8, 128), f32)], [], 2 * product)
    pre, act = kernel_call(
        spatial_kernel,
        [(flat, f32), ((2, *flat), bf16)],
        [image, ((2, *flat), f32)],
        2 * product,
        clip_feats, spatial_weight, feat_other, first, anywhere=1,
    )
    act_in = lax.ppermute(act, both, outward)
    (feats_t,) = kernel_call(
        transpose_kernel,
        [((2, 3 * channels, count), bf16)],
        [image],
        0,
        clip_feats, feat_other, pre, anywhere=1,
    )
    (pre_grad,) = kernel_call(
        act_grad_kernel,
        [(flat, bf16)],
        [three],
        product,
        grad_flat, grad_first, grad_second, temporal_weight, pre, feats_t, anywhere=1,
    )
    pre_grad = pre_grad.reshape(clip_feats.shape)
    pre_other = lax.ppermute(pre_grad, "tile", swap)

    share = (9 * channels // (chips * cores), channels)
    (term,) = kernel_call(
        own_term_kernel,
        [((3, 3 * channels, channels), f32)],
        [],
        product,
        feats_t, pre_grad,
    )
    half = (share[0] // 2, channels)
    far, rest, onward, keep = kernel_call(
        kernel_grad_kernel,
        [(half, bf16), ((3 * half[0], channels), bf16), (share, f32), (share, f32)],
        [((9 * channels, channels), f32)],
        product,
        feats_t, pre_other, term,
    )
    beside = [(z, z ^ 1) for z in range(chips)]
    across = [(z, z ^ 2) for z in range(chips)]
    far_in = lax.ppermute(far, "frame", beside)
    rest_in = lax.ppermute(rest, "frame", beside)
    (sum_a,) = kernel_call(
        functools.partial(forward_sum_kernel, first=0),
        [(half, bf16)],
        [],
        4 * product,
        onward, far_in, act_in, anywhere=1,
    )
    last_a = lax.ppermute(sum_a, "frame", across)
    act_first, act_pass = kernel_call(
        split_kernel, [(flat, bf16)] * 2, [], 0, act_in, sum_a, anywhere=1
    )
    act_second = lax.ppermute(act_pass, "tile", swap)

    input_grad, done = kernel_call(
        input_grad_kernel,
        [(flat, bf16), ((8, 128), f32)],
        [ext],
        product,
        grad_flat, pre_grad, pre_other, spatial_weight, sum_a, anywhere=1,
    )
    (sum_b,) = kernel_call(
        functools.partial(forward_sum_kernel, first=half[0]),
        [(half, bf16)],
        [],
        0,
        onward, rest_in, done, anywhere=1,
    )
    last_b = lax.ppermute(sum_b, "frame", across)
    (arrived,) = kernel_call(
        order_kernel, [((8, 128), f32)], [], 20 * product, last_a, sum_b, anywhere=2
    )
    block_out, done = kernel_call(
        temporal_kernel,
        [(flat, bf16), ((8, 128), f32)],
        [three],
        product,
        feat_flat, act, act_first, act_second, temporal_weight, arrived, anywhere=1,
    )
    (weight_grad,) = kernel_call(
        functools.partial(last_sum_kernel, scale=scale),
        [(share, f32)],
        [],
        0,
        keep, rest_in, last_a, last_b, done, anywhere=1,
    )
    return (
        block_out.reshape(clip_feats.shape),
        input_grad.reshape(clip_feats.shape),
        weight_grad,
    )


def per_device(clip_feats, *rest):
    pairs = lax.axis_size("tile") == 2 and lax.axis_size("frame") == 4
    if pairs and clip_feats.shape[0] == 4 * TAP_DILATION:
        return per_device_pair(clip_feats, *rest)
    return per_device_any(clip_feats, *rest)


def solution(mesh):
    return jax.shard_map(
        per_device,
        mesh=mesh,
        in_specs=(
            P(("clip", "frame"), "tile", None, None),
            P(("clip", "frame"), "tile", None, None),
            P(),
            P(),
        ),
        out_specs=(
            P(("clip", "frame"), "tile", None, None),
            P(("clip", "frame"), "tile", None, None),
            P(("clip", "frame", "tile"), None),
        ),
        check_vma=False,
    )
```

```python
import functools
import math

import jax
import jax.numpy as jnp
from jax import lax
from jax.experimental import pallas as pl
from jax.experimental.pallas import tpu as pltpu
from jax.sharding import PartitionSpec as P

TAP_DILATION = 2
VMEM_LIMIT = 32 * 1024 * 1024


def padded_2(block, sides, width):
    for axis, dim in sides:
        count = lax.axis_size(axis)
        forward = [(i, i + 1) for i in range(count - 1)]
        backward = [(target, source) for source, target in forward]
        low = lax.ppermute(
            lax.slice_in_dim(block, block.shape[dim] - width, None, axis=dim), axis, forward
        )
        high = lax.ppermute(lax.slice_in_dim(block, 0, width, axis=dim), axis, backward)
        block = jnp.concatenate([low, block, high], axis=dim)
    return block


def tile_columns(extended, tile_rows, width_cells, backward_pass):
    padded = jnp.pad(extended, ((0, 0), (0, 0), (1, 1), (0, 0)))
    pieces = []
    for row_shift in range(3):
        for col_shift in range(3):
            row_start = 2 - row_shift if backward_pass else row_shift
            col_start = 2 - col_shift if backward_pass else col_shift
            pieces.append(
                padded[:, row_start : row_start + tile_rows, col_start : col_start + width_cells, :]
            )
    channels = extended.shape[3]
    return jnp.concatenate(pieces, axis=-1).reshape(-1, 9 * channels)


def temporal_taps(padded_seq, weight, frame_count, backward_pass):
    pieces = []
    for temporal_tap_index in range(9):
        first_frame_index = (
            (8 - temporal_tap_index) * TAP_DILATION
            if backward_pass
            else temporal_tap_index * TAP_DILATION
        )
        pieces.append(padded_seq[first_frame_index : first_frame_index + frame_count])
    channels = padded_seq.shape[2]
    columns = jnp.concatenate(pieces, axis=-1).reshape(-1, 9 * channels)
    return jnp.dot(columns, weight, preferred_element_type=jnp.float32)


def per_device_any(clip_feats, out_grad, spatial_weight, temporal_weight):
    slab_frames, tile_rows, width_cells, channels = clip_feats.shape
    row_count = slab_frames * tile_rows * width_cells
    frame_devs = lax.axis_size("frame")
    tile_devs = lax.axis_size("tile")
    grad_scale = jnp.float32(
        1.0 / math.sqrt(slab_frames * frame_devs * tile_rows * tile_devs * width_cells)
    )
    spatial_back = (
        spatial_weight.reshape(9, channels, channels)
        .transpose(0, 2, 1)
        .reshape(9 * channels, channels)
    )
    temporal_back = (
        temporal_weight.reshape(9, channels, channels)
        .transpose(0, 2, 1)
        .reshape(9 * channels, channels)
    )
    feat_ext = padded_2(clip_feats, (("tile", 1),), 1)
    feat_columns = tile_columns(feat_ext, tile_rows, width_cells, False)
    pre = jnp.dot(feat_columns, spatial_weight, preferred_element_type=jnp.float32)
    act = jax.nn.silu(pre).astype(jnp.bfloat16)
    temporal_reach = 4 * TAP_DILATION
    per_group = tile_rows * width_cells // frame_devs
    grouped = (slab_frames, frame_devs, per_group, channels)
    act_part = lax.all_to_all(
        act.reshape(grouped), "frame", split_axis=1, concat_axis=0, tiled=True
    )
    grad_part = lax.all_to_all(out_grad, "frame", split_axis=1, concat_axis=0, tiled=True)
    feat_part = lax.all_to_all(clip_feats, "frame", split_axis=1, concat_axis=0, tiled=True)
    frame_count = act_part.shape[0]
    item_count = act_part.shape[2]
    act_pad = jnp.pad(
        act_part.reshape(frame_count, item_count, channels),
        ((temporal_reach, temporal_reach), (0, 0), (0, 0)),
    )
    grad_pad = jnp.pad(
        grad_part.reshape(frame_count, item_count, channels),
        ((temporal_reach, temporal_reach), (0, 0), (0, 0)),
    )
    mixed = temporal_taps(act_pad, temporal_weight, frame_count, False)
    out_part = (feat_part.reshape(-1, channels).astype(jnp.float32) + mixed).astype(jnp.bfloat16)
    back_part = temporal_taps(grad_pad, temporal_back, frame_count, True).astype(jnp.bfloat16)
    out_part = out_part.reshape(frame_count, 1, item_count, channels)
    back_part = back_part.reshape(frame_count, 1, item_count, channels)
    out_slab = lax.all_to_all(out_part, "frame", split_axis=0, concat_axis=1, tiled=True)
    grad_slab = lax.all_to_all(back_part, "frame", split_axis=0, concat_axis=1, tiled=True)
    act_grad = grad_slab.reshape(row_count, channels)
    sig = jax.nn.sigmoid(pre)
    pre_grad = (act_grad.astype(jnp.float32) * (sig * (1.0 + pre * (1.0 - sig)))).astype(
        jnp.bfloat16
    )
    full_term = lax.dot_general(
        feat_columns, pre_grad, (((0,), (0,)), ((), ())), preferred_element_type=jnp.float32
    )
    summed = lax.psum_scatter(full_term, ("frame", "tile"), scatter_dimension=0, tiled=True)
    weight_grad = summed * grad_scale
    grad_ext = padded_2(
        pre_grad.reshape(slab_frames, tile_rows, width_cells, channels), (("tile", 1),), 1
    )
    grad_columns = tile_columns(grad_ext, tile_rows, width_cells, True)
    local_back = jnp.dot(grad_columns, spatial_back, preferred_element_type=jnp.float32)
    input_grad = (out_grad.reshape(row_count, channels).astype(jnp.float32) + local_back).astype(
        jnp.bfloat16
    )
    input_grad = input_grad.reshape(slab_frames, tile_rows, width_cells, channels)
    return (out_slab, input_grad, weight_grad)


def kernel_call(body, outs, scratch, flops, *args, anywhere=0):
    moved = sum(a.size * a.dtype.itemsize for a in args)
    moved += sum(math.prod(shape) * jnp.dtype(kind).itemsize for shape, kind in outs)
    spaces = [pltpu.VMEM] * (len(args) - anywhere) + [pl.ANY] * anywhere
    return pl.pallas_call(
        body,
        out_shape=tuple(jax.ShapeDtypeStruct(shape, kind) for shape, kind in outs),
        in_specs=[pl.BlockSpec(memory_space=space) for space in spaces],
        out_specs=tuple(pl.BlockSpec(memory_space=pltpu.VMEM) for _ in outs),
        scratch_shapes=[pltpu.VMEM(shape, kind) for shape, kind in scratch],
        compiler_params=pltpu.CompilerParams(vmem_limit_bytes=VMEM_LIMIT),
        cost_estimate=pl.CostEstimate(flops=flops, bytes_accessed=moved, transcendentals=0),
    )(*args)


def shifted(values, width, step):
    rows = values.shape[0]
    at = lax.broadcasted_iota(jnp.int32, values.shape, 0) % width
    moved = pltpu.roll(values, step % rows, 0)
    inside = at >= step if step > 0 else at < width + step
    return jnp.where(inside, moved, 0.0)


def column_shifts(values, width):
    wide = values.astype(jnp.float32)
    return (
        shifted(wide, width, 1).astype(values.dtype),
        values,
        shifted(wide, width, -1).astype(values.dtype),
    )


def with_edges(own, other, ext):
    rows = own.shape[1]
    tile = lax.axis_index("tile")
    ext[:, 1 : rows + 1] = own[...]
    above, below = other[:, rows - 1], other[:, 0]
    ext[:, 0] = jnp.where(tile == 1, above, jnp.zeros_like(above))
    ext[:, rows + 1] = jnp.where(tile == 0, below, jnp.zeros_like(below))


def whole_image(own, other, image):
    rows = own.shape[1]
    tile = lax.axis_index("tile")
    image[:, 0] = jnp.zeros_like(image[:, 0])
    image[:, 2 * rows + 1] = jnp.zeros_like(image[:, 2 * rows + 1])
    image[:, pl.ds(1 + tile * rows, rows)] = own[...]
    image[:, pl.ds(1 + (1 - tile) * rows, rows)] = other[...]


def order_kernel(*refs):
    refs[-1][...] = jnp.zeros_like(refs[-1])


def spatial_kernel(own, weight, other, _, pre_ref, act_ref, image, pre_all):
    frames, rows, width, channels = own.shape
    whole_image(own, other, image)
    shifts = column_shifts(image[...].reshape(-1, channels), width)
    shifts = [piece.reshape(image.shape) for piece in shifts]
    for half in range(2):
        columns = jnp.concatenate(
            [
                shifts[s][:, half * rows + r : half * rows + r + rows].reshape(-1, channels)
                for r in range(3)
                for s in range(3)
            ],
            axis=1,
        )
        pre = jnp.dot(columns, weight[...], preferred_element_type=jnp.float32)
        pre_all[half] = pre
        act_ref[half] = (pre * jax.nn.sigmoid(pre)).astype(jnp.bfloat16)
    pre_ref[...] = pre_all[lax.axis_index("tile")]


def split_kernel(arrived, _, mine_ref, other_ref):
    tile = lax.axis_index("tile")
    mine_ref[...] = arrived[tile]
    other_ref[...] = arrived[1 - tile]


def forward_sum_kernel(partial, arrived, *rest, first):
    sum_ref = rest[-1]
    rows = partial[first : first + sum_ref.shape[0]]
    came = arrived[: sum_ref.shape[0]].astype(jnp.float32)
    sum_ref[...] = (rows + came).astype(sum_ref.dtype)


def last_sum_kernel(keep, rest, last_a, last_b, _, out_ref, *, scale):
    for first, last in ((0, last_a), (last_a.shape[0], last_b)):
        count = last.shape[0]
        near = rest[last_b.shape[0] + first : last_b.shape[0] + first + count]
        total = keep[first : first + count] + near.astype(jnp.float32)
        out_ref[first : first + count] = (total + last[...].astype(jnp.float32)) * scale


def transpose_kernel(own, other, _, out_ref, image):
    frames, rows, width, channels = own.shape
    tile = lax.axis_index("tile")
    whole_image(own, other, image)
    for which, first in enumerate((tile * rows, (1 - tile) * rows)):
        for r in range(3):
            block = image[:, pl.ds(first + r, rows)].reshape(-1, channels)
            out_ref[which, r * channels : (r + 1) * channels] = block.T


def slabs(own, first, second, ext):
    tile = lax.axis_index("tile")
    ext[2 * tile] = first[...]
    ext[1] = own[...]
    ext[2 - 2 * tile] = second[...]
    chip = lax.axis_index("frame")

    @pl.when(chip == 0)
    def _():
        ext[0] = jnp.zeros_like(ext[0])

    @pl.when(chip == lax.axis_size("frame") - 1)
    def _():
        ext[2] = jnp.zeros_like(ext[2])

    return ext[...].reshape(-1, own.shape[1])


def act_grad_kernel(own, first_in, second_in, weight, pre_ref, _, out_ref, ext):
    count, channels = own.shape
    frames = slabs(own, first_in, second_in, ext)
    hop = count // 4
    total = None
    for k in range(9):
        first = (8 - k) * hop
        term = lax.dot_general(
            frames[first : first + count],
            weight[k * channels : (k + 1) * channels],
            (((1,), (1,)), ((), ())),
            preferred_element_type=jnp.float32,
        )
        total = term if total is None else total + term
    act_grad = total.astype(jnp.bfloat16).astype(jnp.float32)
    pre = pre_ref[...]
    sig = jax.nn.sigmoid(pre)
    out_ref[...] = (act_grad * (sig * (1.0 + pre * (1.0 - sig)))).astype(jnp.bfloat16)


def temporal_kernel(feats, act, first_in, second_in, weight, _, out_ref, done_ref, ext):
    count, channels = feats.shape
    own = act.at[lax.axis_index("tile")]
    frames = slabs(own, first_in, second_in, ext)
    hop = count // 4
    columns = jnp.concatenate([frames[k * hop : k * hop + count] for k in range(9)], axis=1)
    mixed = jnp.dot(columns, weight[...], preferred_element_type=jnp.float32)
    out_ref[...] = (feats[...].astype(jnp.float32) + mixed).astype(jnp.bfloat16)
    done_ref[...] = jnp.zeros_like(done_ref)


def own_term_kernel(feats_t, own, total_ref):
    channels = own.shape[3]
    after, same, before = column_shifts(own[...].reshape(-1, channels), own.shape[2])
    left = feats_t[0]
    for s, right in enumerate((before, same, after)):
        total_ref[s] = jnp.dot(left, right, preferred_element_type=jnp.float32)


def kernel_grad_kernel(
    feats_t, other, term, far_ref, rest_ref, pass_ref, keep_ref, total
):
    frames, rows, width, channels = other.shape
    tile = lax.axis_index("tile")
    chip = lax.axis_index("frame")
    after, same, before = column_shifts(other[...].reshape(-1, channels), width)
    left = feats_t[1]
    for s, right in enumerate((before, same, after)):
        both = term[s] + jnp.dot(left, right, preferred_element_type=jnp.float32)
        for r in range(3):
            tap = 3 * r + s
            total[tap * channels : (tap + 1) * channels] = both[r * channels : (r + 1) * channels]
    share, part = keep_ref.shape[0], far_ref.shape[0]
    for distance, skip, ref, at, count in (
        (3, 0, far_ref, 0, part),
        (3, part, rest_ref, 0, share - part),
        (1, 0, rest_ref, share - part, share),
        (2, 0, pass_ref, 0, share),
        (0, 0, keep_ref, 0, share),
    ):
        first = (2 * (chip ^ distance) + tile) * share + skip
        rows = total[pl.ds(pl.multiple_of(first, 16), count)]
        ref[at : at + count] = rows.astype(ref.dtype)


def input_grad_kernel(out_grad, own, other, weight, _, out_ref, done_ref, ext):
    frames, rows, width, channels = own.shape
    with_edges(own, other, ext)
    after, same, before = column_shifts(ext[...].reshape(-1, channels), width)
    shifts = [piece.reshape(ext.shape) for piece in (before, same, after)]
    total = out_grad[...].astype(jnp.float32)
    for r in range(3):
        for s in range(3):
            tap = 3 * r + s
            total = total + lax.dot_general(
                shifts[s][:, 2 - r : 2 - r + rows].reshape(-1, channels),
                weight[tap * channels : (tap + 1) * channels],
                (((1,), (1,)), ((), ())),
                preferred_element_type=jnp.float32,
            )
    out_ref[...] = total.astype(jnp.bfloat16)
    done_ref[...] = jnp.zeros_like(done_ref)


def per_device_pair(clip_feats, out_grad, spatial_weight, temporal_weight):
    frames, rows, width, channels = clip_feats.shape
    count = frames * rows * width
    chips = lax.axis_size("frame")
    cores = lax.axis_size("tile")
    scale = 1.0 / math.sqrt(frames * chips * rows * cores * width)
    outward = [(2 * z, 2 * z + 2) for z in range(chips - 1)]
    outward += [(2 * z + 3, 2 * z + 1) for z in range(chips - 1)]
    outward += [(2 * chips - 2, 2 * chips - 1), (1, 0)]
    inward = [(target, source) for source, target in outward]
    both = ("frame", "tile")
    swap = [(0, 1), (1, 0)]
    bf16, f32 = jnp.bfloat16, jnp.float32
    product = 2 * count * 9 * channels * channels
    flat = (count, channels)
    ext = ((frames, rows + 2, width, channels), bf16)
    image = ((frames, 2 * rows + 2, width, channels), bf16)
    three = ((3, count, channels), bf16)

    grad_flat = out_grad.reshape(flat)
    feat_flat = clip_feats.reshape(flat)
    grad_first = lax.ppermute(grad_flat, both, outward)
    grad_second = lax.ppermute(grad_flat, both, inward)
    feat_other = lax.ppermute(clip_feats, "tile", swap)

    (first,) = kernel_call(order_kernel, [((8, 128), f32)], [], 2 * product)
    pre, act = kernel_call(
        spatial_kernel,
        [(flat, f32), ((2, *flat), bf16)],
        [image, ((2, *flat), f32)],
        2 * product,
        clip_feats, spatial_weight, feat_other, first, anywhere=1,
    )
    act_in = lax.ppermute(act, both, outward)
    (feats_t,) = kernel_call(
        transpose_kernel,
        [((2, 3 * channels, count), bf16)],
        [image],
        0,
        clip_feats, feat_other, pre, anywhere=1,
    )
    (pre_grad,) = kernel_call(
        act_grad_kernel,
        [(flat, bf16)],
        [three],
        product,
        grad_flat, grad_first, grad_second, temporal_weight, pre, feats_t, anywhere=1,
    )
    pre_grad = pre_grad.reshape(clip_feats.shape)
    pre_other = lax.ppermute(pre_grad, "tile", swap)

    share = (9 * channels // (chips * cores), channels)
    (term,) = kernel_call(
        own_term_kernel,
        [((3, 3 * channels, channels), f32)],
        [],
        product,
        feats_t, pre_grad,
    )
    first_rows = share[0] * 2 // 3
    part_a, part_b = (first_rows, channels), (share[0] - first_rows, channels)
    far, rest, onward, keep = kernel_call(
        kernel_grad_kernel,
        [(part_a, bf16), ((share[0] + part_b[0], channels), bf16), (share, f32), (share, f32)],
        [((9 * channels, channels), f32)],
        product,
        feats_t, pre_other, term,
    )
    beside = [(z, z ^ 1) for z in range(chips)]
    across = [(z, z ^ 2) for z in range(chips)]
    far_in = lax.ppermute(far, "frame", beside)
    rest_in = lax.ppermute(rest, "frame", beside)
    (sum_a,) = kernel_call(
        functools.partial(forward_sum_kernel, first=0),
        [(part_a, bf16)],
        [],
        4 * product,
        onward, far_in,
    )
    last_a = lax.ppermute(sum_a, "frame", across)
    act_first, act_pass = kernel_call(
        split_kernel, [(flat, bf16)] * 2, [], 0, act_in, sum_a, anywhere=1
    )
    act_second = lax.ppermute(act_pass, "tile", swap)

    input_grad, done = kernel_call(
        input_grad_kernel,
        [(flat, bf16), ((8, 128), f32)],
        [ext],
        product,
        grad_flat, pre_grad, pre_other, spatial_weight, sum_a, anywhere=1,
    )
    (sum_b,) = kernel_call(
        functools.partial(forward_sum_kernel, first=first_rows),
        [(part_b, bf16)],
        [],
        0,
        onward, rest_in, done, anywhere=1,
    )
    last_b = lax.ppermute(sum_b, "frame", across)
    (arrived,) = kernel_call(
        order_kernel, [((8, 128), f32)], [], 20 * product, last_a, sum_b, anywhere=2
    )
    block_out, done = kernel_call(
        temporal_kernel,
        [(flat, bf16), ((8, 128), f32)],
        [three],
        product,
        feat_flat, act, act_first, act_second, temporal_weight, arrived, anywhere=1,
    )
    (weight_grad,) = kernel_call(
        functools.partial(last_sum_kernel, scale=scale),
        [(share, f32)],
        [],
        0,
        keep, rest_in, last_a, last_b, done, anywhere=1,
    )
    return (
        block_out.reshape(clip_feats.shape),
        input_grad.reshape(clip_feats.shape),
        weight_grad,
    )


def per_device(clip_feats, *rest):
    pairs = lax.axis_size("tile") == 2 and lax.axis_size("frame") == 4
    if pairs and clip_feats.shape[0] == 4 * TAP_DILATION:
        return per_device_pair(clip_feats, *rest)
    return per_device_any(clip_feats, *rest)


def solution(mesh):
    return jax.shard_map(
        per_device,
        mesh=mesh,
        in_specs=(
            P(("clip", "frame"), "tile", None, None),
            P(("clip", "frame"), "tile", None, None),
            P(),
            P(),
        ),
        out_specs=(
            P(("clip", "frame"), "tile", None, None),
            P(("clip", "frame"), "tile", None, None),
            P(("clip", "frame", "tile"), None),
        ),
        check_vma=False,
    )
```

```python
import functools
import math

import jax
import jax.numpy as jnp
from jax import lax
from jax.experimental import pallas as pl
from jax.experimental.pallas import tpu as pltpu
from jax.sharding import PartitionSpec as P

TAP_DILATION = 2
VMEM_LIMIT = 32 * 1024 * 1024


def padded_2(block, sides, width):
    for axis, dim in sides:
        count = lax.axis_size(axis)
        forward = [(i, i + 1) for i in range(count - 1)]
        backward = [(target, source) for source, target in forward]
        low = lax.ppermute(
            lax.slice_in_dim(block, block.shape[dim] - width, None, axis=dim), axis, forward
        )
        high = lax.ppermute(lax.slice_in_dim(block, 0, width, axis=dim), axis, backward)
        block = jnp.concatenate([low, block, high], axis=dim)
    return block


def tile_columns(extended, tile_rows, width_cells, backward_pass):
    padded = jnp.pad(extended, ((0, 0), (0, 0), (1, 1), (0, 0)))
    pieces = []
    for row_shift in range(3):
        for col_shift in range(3):
            row_start = 2 - row_shift if backward_pass else row_shift
            col_start = 2 - col_shift if backward_pass else col_shift
            pieces.append(
                padded[:, row_start : row_start + tile_rows, col_start : col_start + width_cells, :]
            )
    channels = extended.shape[3]
    return jnp.concatenate(pieces, axis=-1).reshape(-1, 9 * channels)


def temporal_taps(padded_seq, weight, frame_count, backward_pass):
    pieces = []
    for temporal_tap_index in range(9):
        first_frame_index = (
            (8 - temporal_tap_index) * TAP_DILATION
            if backward_pass
            else temporal_tap_index * TAP_DILATION
        )
        pieces.append(padded_seq[first_frame_index : first_frame_index + frame_count])
    channels = padded_seq.shape[2]
    columns = jnp.concatenate(pieces, axis=-1).reshape(-1, 9 * channels)
    return jnp.dot(columns, weight, preferred_element_type=jnp.float32)


def per_device_any(clip_feats, out_grad, spatial_weight, temporal_weight):
    slab_frames, tile_rows, width_cells, channels = clip_feats.shape
    row_count = slab_frames * tile_rows * width_cells
    frame_devs = lax.axis_size("frame")
    tile_devs = lax.axis_size("tile")
    grad_scale = jnp.float32(
        1.0 / math.sqrt(slab_frames * frame_devs * tile_rows * tile_devs * width_cells)
    )
    spatial_back = (
        spatial_weight.reshape(9, channels, channels)
        .transpose(0, 2, 1)
        .reshape(9 * channels, channels)
    )
    temporal_back = (
        temporal_weight.reshape(9, channels, channels)
        .transpose(0, 2, 1)
        .reshape(9 * channels, channels)
    )
    feat_ext = padded_2(clip_feats, (("tile", 1),), 1)
    feat_columns = tile_columns(feat_ext, tile_rows, width_cells, False)
    pre = jnp.dot(feat_columns, spatial_weight, preferred_element_type=jnp.float32)
    act = jax.nn.silu(pre).astype(jnp.bfloat16)
    temporal_reach = 4 * TAP_DILATION
    per_group = tile_rows * width_cells // frame_devs
    grouped = (slab_frames, frame_devs, per_group, channels)
    act_part = lax.all_to_all(
        act.reshape(grouped), "frame", split_axis=1, concat_axis=0, tiled=True
    )
    grad_part = lax.all_to_all(out_grad, "frame", split_axis=1, concat_axis=0, tiled=True)
    feat_part = lax.all_to_all(clip_feats, "frame", split_axis=1, concat_axis=0, tiled=True)
    frame_count = act_part.shape[0]
    item_count = act_part.shape[2]
    act_pad = jnp.pad(
        act_part.reshape(frame_count, item_count, channels),
        ((temporal_reach, temporal_reach), (0, 0), (0, 0)),
    )
    grad_pad = jnp.pad(
        grad_part.reshape(frame_count, item_count, channels),
        ((temporal_reach, temporal_reach), (0, 0), (0, 0)),
    )
    mixed = temporal_taps(act_pad, temporal_weight, frame_count, False)
    out_part = (feat_part.reshape(-1, channels).astype(jnp.float32) + mixed).astype(jnp.bfloat16)
    back_part = temporal_taps(grad_pad, temporal_back, frame_count, True).astype(jnp.bfloat16)
    out_part = out_part.reshape(frame_count, 1, item_count, channels)
    back_part = back_part.reshape(frame_count, 1, item_count, channels)
    out_slab = lax.all_to_all(out_part, "frame", split_axis=0, concat_axis=1, tiled=True)
    grad_slab = lax.all_to_all(back_part, "frame", split_axis=0, concat_axis=1, tiled=True)
    act_grad = grad_slab.reshape(row_count, channels)
    sig = jax.nn.sigmoid(pre)
    pre_grad = (act_grad.astype(jnp.float32) * (sig * (1.0 + pre * (1.0 - sig)))).astype(
        jnp.bfloat16
    )
    full_term = lax.dot_general(
        feat_columns, pre_grad, (((0,), (0,)), ((), ())), preferred_element_type=jnp.float32
    )
    summed = lax.psum_scatter(full_term, ("frame", "tile"), scatter_dimension=0, tiled=True)
    weight_grad = summed * grad_scale
    grad_ext = padded_2(
        pre_grad.reshape(slab_frames, tile_rows, width_cells, channels), (("tile", 1),), 1
    )
    grad_columns = tile_columns(grad_ext, tile_rows, width_cells, True)
    local_back = jnp.dot(grad_columns, spatial_back, preferred_element_type=jnp.float32)
    input_grad = (out_grad.reshape(row_count, channels).astype(jnp.float32) + local_back).astype(
        jnp.bfloat16
    )
    input_grad = input_grad.reshape(slab_frames, tile_rows, width_cells, channels)
    return (out_slab, input_grad, weight_grad)


def kernel_call(body, outs, scratch, flops, *args, anywhere=0):
    moved = sum(a.size * a.dtype.itemsize for a in args)
    moved += sum(math.prod(shape) * jnp.dtype(kind).itemsize for shape, kind in outs)
    spaces = [pltpu.VMEM] * (len(args) - anywhere) + [pl.ANY] * anywhere
    return pl.pallas_call(
        body,
        out_shape=tuple(jax.ShapeDtypeStruct(shape, kind) for shape, kind in outs),
        in_specs=[pl.BlockSpec(memory_space=space) for space in spaces],
        out_specs=tuple(pl.BlockSpec(memory_space=pltpu.VMEM) for _ in outs),
        scratch_shapes=[pltpu.VMEM(shape, kind) for shape, kind in scratch],
        compiler_params=pltpu.CompilerParams(vmem_limit_bytes=VMEM_LIMIT),
        cost_estimate=pl.CostEstimate(flops=flops, bytes_accessed=moved, transcendentals=0),
    )(*args)


def shifted(values, width, step):
    rows = values.shape[0]
    at = lax.broadcasted_iota(jnp.int32, values.shape, 0) % width
    moved = pltpu.roll(values, step % rows, 0)
    inside = at >= step if step > 0 else at < width + step
    return jnp.where(inside, moved, 0.0)


def column_shifts(values, width):
    wide = values.astype(jnp.float32)
    return (
        shifted(wide, width, 1).astype(values.dtype),
        values,
        shifted(wide, width, -1).astype(values.dtype),
    )


def with_edges(own, other, ext):
    rows = own.shape[1]
    tile = lax.axis_index("tile")
    ext[:, 1 : rows + 1] = own[...]
    above, below = other[:, rows - 1], other[:, 0]
    ext[:, 0] = jnp.where(tile == 1, above, jnp.zeros_like(above))
    ext[:, rows + 1] = jnp.where(tile == 0, below, jnp.zeros_like(below))


def whole_image(own, other, image):
    rows = own.shape[1]
    tile = lax.axis_index("tile")
    image[:, 0] = jnp.zeros_like(image[:, 0])
    image[:, 2 * rows + 1] = jnp.zeros_like(image[:, 2 * rows + 1])
    image[:, pl.ds(1 + tile * rows, rows)] = own[...]
    image[:, pl.ds(1 + (1 - tile) * rows, rows)] = other[...]


def order_kernel(*refs):
    refs[-1][...] = jnp.zeros_like(refs[-1])


def spatial_kernel(own, weight, other, _, pre_ref, act_ref, image, pre_all):
    frames, rows, width, channels = own.shape
    whole_image(own, other, image)
    shifts = column_shifts(image[...].reshape(-1, channels), width)
    shifts = [piece.reshape(image.shape) for piece in shifts]
    for half in range(2):
        columns = jnp.concatenate(
            [
                shifts[s][:, half * rows + r : half * rows + r + rows].reshape(-1, channels)
                for r in range(3)
                for s in range(3)
            ],
            axis=1,
        )
        pre = jnp.dot(columns, weight[...], preferred_element_type=jnp.float32)
        pre_all[half] = pre
        act_ref[half] = (pre * jax.nn.sigmoid(pre)).astype(jnp.bfloat16)
    pre_ref[...] = pre_all[lax.axis_index("tile")]


def split_kernel(arrived, near, _, mine_ref, other_ref, near_ref):
    tile = lax.axis_index("tile")
    near_ref[...] = near[...]
    mine_ref[...] = arrived[tile]
    other_ref[...] = arrived[1 - tile]


def forward_sum_kernel(partial, arrived, *rest, first):
    sum_ref = rest[-1]
    rows = partial[first : first + sum_ref.shape[0]]
    came = arrived[: sum_ref.shape[0]].astype(jnp.float32)
    sum_ref[...] = (rows + came).astype(sum_ref.dtype)


def last_sum_kernel(keep, near, last_a, last_b, _, out_ref, *, scale):
    half = last_a.shape[0]
    for first, last in ((0, last_a), (half, last_b)):
        total = keep[first : first + half] + near[first : first + half].astype(jnp.float32)
        out_ref[first : first + half] = (total + last[...].astype(jnp.float32)) * scale


def transpose_kernel(own, other, _, out_ref, image):
    frames, rows, width, channels = own.shape
    tile = lax.axis_index("tile")
    whole_image(own, other, image)
    for which, first in enumerate((tile * rows, (1 - tile) * rows)):
        for r in range(3):
            block = image[:, pl.ds(first + r, rows)].reshape(-1, channels)
            out_ref[which, r * channels : (r + 1) * channels] = block.T


def slabs(own, first, second, ext):
    tile = lax.axis_index("tile")
    ext[2 * tile] = first[...]
    ext[1] = own[...]
    ext[2 - 2 * tile] = second[...]
    chip = lax.axis_index("frame")

    @pl.when(chip == 0)
    def _():
        ext[0] = jnp.zeros_like(ext[0])

    @pl.when(chip == lax.axis_size("frame") - 1)
    def _():
        ext[2] = jnp.zeros_like(ext[2])

    return ext[...].reshape(-1, own.shape[1])


def act_grad_kernel(own, first_in, second_in, weight, pre_ref, _, out_ref, ext):
    count, channels = own.shape
    frames = slabs(own, first_in, second_in, ext)
    hop = count // 4
    total = None
    for k in range(9):
        first = (8 - k) * hop
        term = lax.dot_general(
            frames[first : first + count],
            weight[k * channels : (k + 1) * channels],
            (((1,), (1,)), ((), ())),
            preferred_element_type=jnp.float32,
        )
        total = term if total is None else total + term
    act_grad = total.astype(jnp.bfloat16).astype(jnp.float32)
    pre = pre_ref[...]
    sig = jax.nn.sigmoid(pre)
    out_ref[...] = (act_grad * (sig * (1.0 + pre * (1.0 - sig)))).astype(jnp.bfloat16)


def temporal_kernel(feats, act, first_in, second_in, weight, _, out_ref, done_ref, ext):
    count, channels = feats.shape
    own = act.at[lax.axis_index("tile")]
    frames = slabs(own, first_in, second_in, ext)
    hop = count // 4
    columns = jnp.concatenate([frames[k * hop : k * hop + count] for k in range(9)], axis=1)
    mixed = jnp.dot(columns, weight[...], preferred_element_type=jnp.float32)
    out_ref[...] = (feats[...].astype(jnp.float32) + mixed).astype(jnp.bfloat16)
    done_ref[...] = jnp.zeros_like(done_ref)


def own_term_kernel(feats_t, own, total_ref):
    channels = own.shape[3]
    after, same, before = column_shifts(own[...].reshape(-1, channels), own.shape[2])
    left = feats_t[0]
    for s, right in enumerate((before, same, after)):
        total_ref[s] = jnp.dot(left, right, preferred_element_type=jnp.float32)


def kernel_grad_kernel(
    feats_t, other, term, far_a_ref, far_b_ref, pass_ref, near_ref, keep_ref, total
):
    frames, rows, width, channels = other.shape
    tile = lax.axis_index("tile")
    chip = lax.axis_index("frame")
    after, same, before = column_shifts(other[...].reshape(-1, channels), width)
    left = feats_t[1]
    for s, right in enumerate((before, same, after)):
        both = term[s] + jnp.dot(left, right, preferred_element_type=jnp.float32)
        for r in range(3):
            tap = 3 * r + s
            total[tap * channels : (tap + 1) * channels] = both[r * channels : (r + 1) * channels]
    share = keep_ref.shape[0]
    half = share // 2
    for distance, skip, ref in (
        (3, 0, far_a_ref),
        (3, half, far_b_ref),
        (2, 0, pass_ref),
        (1, 0, near_ref),
        (0, 0, keep_ref),
    ):
        first = (2 * (chip ^ distance) + tile) * share + skip
        ref[...] = total[pl.ds(pl.multiple_of(first, 16), ref.shape[0])].astype(ref.dtype)


def input_grad_kernel(out_grad, own, other, weight, _, out_ref, done_ref, ext):
    frames, rows, width, channels = own.shape
    with_edges(own, other, ext)
    after, same, before = column_shifts(ext[...].reshape(-1, channels), width)
    shifts = [piece.reshape(ext.shape) for piece in (before, same, after)]
    total = out_grad[...].astype(jnp.float32)
    for r in range(3):
        for s in range(3):
            tap = 3 * r + s
            total = total + lax.dot_general(
                shifts[s][:, 2 - r : 2 - r + rows].reshape(-1, channels),
                weight[tap * channels : (tap + 1) * channels],
                (((1,), (1,)), ((), ())),
                preferred_element_type=jnp.float32,
            )
    out_ref[...] = total.astype(jnp.bfloat16)
    done_ref[...] = jnp.zeros_like(done_ref)


def per_device_pair(clip_feats, out_grad, spatial_weight, temporal_weight):
    frames, rows, width, channels = clip_feats.shape
    count = frames * rows * width
    chips = lax.axis_size("frame")
    cores = lax.axis_size("tile")
    scale = 1.0 / math.sqrt(frames * chips * rows * cores * width)
    outward = [(2 * z, 2 * z + 2) for z in range(chips - 1)]
    outward += [(2 * z + 3, 2 * z + 1) for z in range(chips - 1)]
    outward += [(2 * chips - 2, 2 * chips - 1), (1, 0)]
    inward = [(target, source) for source, target in outward]
    both = ("frame", "tile")
    swap = [(0, 1), (1, 0)]
    bf16, f32 = jnp.bfloat16, jnp.float32
    product = 2 * count * 9 * channels * channels
    flat = (count, channels)
    ext = ((frames, rows + 2, width, channels), bf16)
    image = ((frames, 2 * rows + 2, width, channels), bf16)
    three = ((3, count, channels), bf16)

    grad_flat = out_grad.reshape(flat)
    feat_flat = clip_feats.reshape(flat)
    grad_first = lax.ppermute(grad_flat, both, outward)
    grad_second = lax.ppermute(grad_flat, both, inward)
    feat_other = lax.ppermute(clip_feats, "tile", swap)

    (first,) = kernel_call(order_kernel, [((8, 128), f32)], [], 2 * product)
    pre, act = kernel_call(
        spatial_kernel,
        [(flat, f32), ((2, *flat), bf16)],
        [image, ((2, *flat), f32)],
        2 * product,
        clip_feats, spatial_weight, feat_other, first, anywhere=1,
    )
    act_in = lax.ppermute(act, both, outward)
    (feats_t,) = kernel_call(
        transpose_kernel,
        [((2, 3 * channels, count), bf16)],
        [image],
        0,
        clip_feats, feat_other, pre, anywhere=1,
    )
    (pre_grad,) = kernel_call(
        act_grad_kernel,
        [(flat, bf16)],
        [three],
        product,
        grad_flat, grad_first, grad_second, temporal_weight, pre, feats_t, anywhere=1,
    )
    pre_grad = pre_grad.reshape(clip_feats.shape)
    pre_other = lax.ppermute(pre_grad, "tile", swap)

    share = (9 * channels // (chips * cores), channels)
    (term,) = kernel_call(
        own_term_kernel,
        [((3, 3 * channels, channels), f32)],
        [],
        product,
        feats_t, pre_grad,
    )
    half = (share[0] // 2, channels)
    far_a, far_b, onward, near, keep = kernel_call(
        kernel_grad_kernel,
        [(half, bf16), (half, bf16), (share, f32), (share, bf16), (share, f32)],
        [((9 * channels, channels), f32)],
        product,
        feats_t, pre_other, term,
    )
    beside = [(z, z ^ 1) for z in range(chips)]
    across = [(z, z ^ 2) for z in range(chips)]
    far_in_a = lax.ppermute(far_a, "frame", beside)
    far_in_b = lax.ppermute(far_b, "frame", beside)
    (sum_a,) = kernel_call(
        functools.partial(forward_sum_kernel, first=0),
        [(half, bf16)],
        [],
        4 * product,
        onward, far_in_a, act_in, anywhere=1,
    )
    last_a = lax.ppermute(sum_a, "frame", across)
    (sum_b,) = kernel_call(
        functools.partial(forward_sum_kernel, first=half[0]),
        [(half, bf16)],
        [],
        0,
        onward, far_in_b, sum_a, anywhere=1,
    )
    last_b = lax.ppermute(sum_b, "frame", across)
    act_first, act_pass, near = kernel_call(
        split_kernel,
        [(flat, bf16), (flat, bf16), (share, bf16)],
        [],
        0,
        act_in, near, sum_b, anywhere=1,
    )
    near_in = lax.ppermute(near, "frame", beside)
    act_second = lax.ppermute(act_pass, "tile", swap)

    input_grad, done = kernel_call(
        input_grad_kernel,
        [(flat, bf16), ((8, 128), f32)],
        [ext],
        product,
        grad_flat, pre_grad, pre_other, spatial_weight, sum_b, anywhere=1,
    )
    (arrived,) = kernel_call(
        order_kernel, [((8, 128), f32)], [], 20 * product, last_a, done, anywhere=2
    )
    block_out, done = kernel_call(
        temporal_kernel,
        [(flat, bf16), ((8, 128), f32)],
        [three],
        product,
        feat_flat, act, act_first, act_second, temporal_weight, arrived, anywhere=1,
    )
    (weight_grad,) = kernel_call(
        functools.partial(last_sum_kernel, scale=scale),
        [(share, f32)],
        [],
        0,
        keep, near_in, last_a, last_b, done, anywhere=1,
    )
    return (
        block_out.reshape(clip_feats.shape),
        input_grad.reshape(clip_feats.shape),
        weight_grad,
    )


def per_device(clip_feats, *rest):
    pairs = lax.axis_size("tile") == 2 and lax.axis_size("frame") == 4
    if pairs and clip_feats.shape[0] == 4 * TAP_DILATION:
        return per_device_pair(clip_feats, *rest)
    return per_device_any(clip_feats, *rest)


def solution(mesh):
    return jax.shard_map(
        per_device,
        mesh=mesh,
        in_specs=(
            P(("clip", "frame"), "tile", None, None),
            P(("clip", "frame"), "tile", None, None),
            P(),
            P(),
        ),
        out_specs=(
            P(("clip", "frame"), "tile", None, None),
            P(("clip", "frame"), "tile", None, None),
            P(("clip", "frame", "tile"), None),
        ),
        check_vma=False,
    )
```

```python
import functools
import math

import jax
import jax.numpy as jnp
from jax import lax
from jax.experimental import pallas as pl
from jax.experimental.pallas import tpu as pltpu
from jax.sharding import PartitionSpec as P

TAP_DILATION = 2
VMEM_LIMIT = 32 * 1024 * 1024


def padded_2(block, sides, width):
    for axis, dim in sides:
        count = lax.axis_size(axis)
        forward = [(i, i + 1) for i in range(count - 1)]
        backward = [(target, source) for source, target in forward]
        low = lax.ppermute(
            lax.slice_in_dim(block, block.shape[dim] - width, None, axis=dim), axis, forward
        )
        high = lax.ppermute(lax.slice_in_dim(block, 0, width, axis=dim), axis, backward)
        block = jnp.concatenate([low, block, high], axis=dim)
    return block


def tile_columns(extended, tile_rows, width_cells, backward_pass):
    padded = jnp.pad(extended, ((0, 0), (0, 0), (1, 1), (0, 0)))
    pieces = []
    for row_shift in range(3):
        for col_shift in range(3):
            row_start = 2 - row_shift if backward_pass else row_shift
            col_start = 2 - col_shift if backward_pass else col_shift
            pieces.append(
                padded[:, row_start : row_start + tile_rows, col_start : col_start + width_cells, :]
            )
    channels = extended.shape[3]
    return jnp.concatenate(pieces, axis=-1).reshape(-1, 9 * channels)


def temporal_taps(padded_seq, weight, frame_count, backward_pass):
    pieces = []
    for temporal_tap_index in range(9):
        first_frame_index = (
            (8 - temporal_tap_index) * TAP_DILATION
            if backward_pass
            else temporal_tap_index * TAP_DILATION
        )
        pieces.append(padded_seq[first_frame_index : first_frame_index + frame_count])
    channels = padded_seq.shape[2]
    columns = jnp.concatenate(pieces, axis=-1).reshape(-1, 9 * channels)
    return jnp.dot(columns, weight, preferred_element_type=jnp.float32)


def per_device_any(clip_feats, out_grad, spatial_weight, temporal_weight):
    slab_frames, tile_rows, width_cells, channels = clip_feats.shape
    row_count = slab_frames * tile_rows * width_cells
    frame_devs = lax.axis_size("frame")
    tile_devs = lax.axis_size("tile")
    grad_scale = jnp.float32(
        1.0 / math.sqrt(slab_frames * frame_devs * tile_rows * tile_devs * width_cells)
    )
    spatial_back = (
        spatial_weight.reshape(9, channels, channels)
        .transpose(0, 2, 1)
        .reshape(9 * channels, channels)
    )
    temporal_back = (
        temporal_weight.reshape(9, channels, channels)
        .transpose(0, 2, 1)
        .reshape(9 * channels, channels)
    )
    feat_ext = padded_2(clip_feats, (("tile", 1),), 1)
    feat_columns = tile_columns(feat_ext, tile_rows, width_cells, False)
    pre = jnp.dot(feat_columns, spatial_weight, preferred_element_type=jnp.float32)
    act = jax.nn.silu(pre).astype(jnp.bfloat16)
    temporal_reach = 4 * TAP_DILATION
    per_group = tile_rows * width_cells // frame_devs
    grouped = (slab_frames, frame_devs, per_group, channels)
    act_part = lax.all_to_all(
        act.reshape(grouped), "frame", split_axis=1, concat_axis=0, tiled=True
    )
    grad_part = lax.all_to_all(out_grad, "frame", split_axis=1, concat_axis=0, tiled=True)
    feat_part = lax.all_to_all(clip_feats, "frame", split_axis=1, concat_axis=0, tiled=True)
    frame_count = act_part.shape[0]
    item_count = act_part.shape[2]
    act_pad = jnp.pad(
        act_part.reshape(frame_count, item_count, channels),
        ((temporal_reach, temporal_reach), (0, 0), (0, 0)),
    )
    grad_pad = jnp.pad(
        grad_part.reshape(frame_count, item_count, channels),
        ((temporal_reach, temporal_reach), (0, 0), (0, 0)),
    )
    mixed = temporal_taps(act_pad, temporal_weight, frame_count, False)
    out_part = (feat_part.reshape(-1, channels).astype(jnp.float32) + mixed).astype(jnp.bfloat16)
    back_part = temporal_taps(grad_pad, temporal_back, frame_count, True).astype(jnp.bfloat16)
    out_part = out_part.reshape(frame_count, 1, item_count, channels)
    back_part = back_part.reshape(frame_count, 1, item_count, channels)
    out_slab = lax.all_to_all(out_part, "frame", split_axis=0, concat_axis=1, tiled=True)
    grad_slab = lax.all_to_all(back_part, "frame", split_axis=0, concat_axis=1, tiled=True)
    act_grad = grad_slab.reshape(row_count, channels)
    sig = jax.nn.sigmoid(pre)
    pre_grad = (act_grad.astype(jnp.float32) * (sig * (1.0 + pre * (1.0 - sig)))).astype(
        jnp.bfloat16
    )
    full_term = lax.dot_general(
        feat_columns, pre_grad, (((0,), (0,)), ((), ())), preferred_element_type=jnp.float32
    )
    summed = lax.psum_scatter(full_term, ("frame", "tile"), scatter_dimension=0, tiled=True)
    weight_grad = summed * grad_scale
    grad_ext = padded_2(
        pre_grad.reshape(slab_frames, tile_rows, width_cells, channels), (("tile", 1),), 1
    )
    grad_columns = tile_columns(grad_ext, tile_rows, width_cells, True)
    local_back = jnp.dot(grad_columns, spatial_back, preferred_element_type=jnp.float32)
    input_grad = (out_grad.reshape(row_count, channels).astype(jnp.float32) + local_back).astype(
        jnp.bfloat16
    )
    input_grad = input_grad.reshape(slab_frames, tile_rows, width_cells, channels)
    return (out_slab, input_grad, weight_grad)


def kernel_call(body, outs, scratch, flops, *args, anywhere=0):
    moved = sum(a.size * a.dtype.itemsize for a in args)
    moved += sum(math.prod(shape) * jnp.dtype(kind).itemsize for shape, kind in outs)
    spaces = [pltpu.VMEM] * (len(args) - anywhere) + [pl.ANY] * anywhere
    return pl.pallas_call(
        body,
        out_shape=tuple(jax.ShapeDtypeStruct(shape, kind) for shape, kind in outs),
        in_specs=[pl.BlockSpec(memory_space=space) for space in spaces],
        out_specs=tuple(pl.BlockSpec(memory_space=pltpu.VMEM) for _ in outs),
        scratch_shapes=[pltpu.VMEM(shape, kind) for shape, kind in scratch],
        compiler_params=pltpu.CompilerParams(vmem_limit_bytes=VMEM_LIMIT),
        cost_estimate=pl.CostEstimate(flops=flops, bytes_accessed=moved, transcendentals=0),
    )(*args)


def shifted(values, width, step):
    rows = values.shape[0]
    at = lax.broadcasted_iota(jnp.int32, values.shape, 0) % width
    moved = pltpu.roll(values, step % rows, 0)
    inside = at >= step if step > 0 else at < width + step
    return jnp.where(inside, moved, 0.0)


def column_shifts(values, width):
    wide = values.astype(jnp.float32)
    return (
        shifted(wide, width, 1).astype(values.dtype),
        values,
        shifted(wide, width, -1).astype(values.dtype),
    )


def with_edges(own, other, ext):
    rows = own.shape[1]
    tile = lax.axis_index("tile")
    ext[:, 1 : rows + 1] = own[...]
    above, below = other[:, rows - 1], other[:, 0]
    ext[:, 0] = jnp.where(tile == 1, above, jnp.zeros_like(above))
    ext[:, rows + 1] = jnp.where(tile == 0, below, jnp.zeros_like(below))


def whole_image(own, other, image):
    rows = own.shape[1]
    tile = lax.axis_index("tile")
    image[:, 0] = jnp.zeros_like(image[:, 0])
    image[:, 2 * rows + 1] = jnp.zeros_like(image[:, 2 * rows + 1])
    image[:, pl.ds(1 + tile * rows, rows)] = own[...]
    image[:, pl.ds(1 + (1 - tile) * rows, rows)] = other[...]


def order_kernel(*refs):
    refs[-1][...] = jnp.zeros_like(refs[-1])


def spatial_kernel(own, weight, other, _, pre_ref, act_ref, image, pre_all):
    frames, rows, width, channels = own.shape
    whole_image(own, other, image)
    shifts = column_shifts(image[...].reshape(-1, channels), width)
    shifts = [piece.reshape(image.shape) for piece in shifts]
    for half in range(2):
        columns = jnp.concatenate(
            [
                shifts[s][:, half * rows + r : half * rows + r + rows].reshape(-1, channels)
                for r in range(3)
                for s in range(3)
            ],
            axis=1,
        )
        pre = jnp.dot(columns, weight[...], preferred_element_type=jnp.float32)
        pre_all[half] = pre
        act_ref[half] = (pre * jax.nn.sigmoid(pre)).astype(jnp.bfloat16)
    pre_ref[...] = pre_all[lax.axis_index("tile")]


def split_kernel(arrived, _, mine_ref, other_ref):
    tile = lax.axis_index("tile")
    mine_ref[...] = arrived[tile]
    other_ref[...] = arrived[1 - tile]


def forward_sum_kernel(partial, arrived, *rest, first):
    sum_ref = rest[-1]
    rows = partial[first : first + sum_ref.shape[0]]
    came = arrived[: sum_ref.shape[0]].astype(jnp.float32)
    sum_ref[...] = (rows + came).astype(sum_ref.dtype)


def last_sum_kernel(keep, near, last_a, last_b, _, out_ref, *, scale):
    half = last_a.shape[0]
    for first, last in ((0, last_a), (half, last_b)):
        total = keep[first : first + half] + near[first : first + half].astype(jnp.float32)
        out_ref[first : first + half] = (total + last[...].astype(jnp.float32)) * scale


def transpose_kernel(own, other, _, out_ref, image):
    frames, rows, width, channels = own.shape
    tile = lax.axis_index("tile")
    whole_image(own, other, image)
    for which, first in enumerate((tile * rows, (1 - tile) * rows)):
        for r in range(3):
            block = image[:, pl.ds(first + r, rows)].reshape(-1, channels)
            out_ref[which, r * channels : (r + 1) * channels] = block.T


def slabs(own, first, second, ext):
    tile = lax.axis_index("tile")
    ext[2 * tile] = first[...]
    ext[1] = own[...]
    ext[2 - 2 * tile] = second[...]
    chip = lax.axis_index("frame")

    @pl.when(chip == 0)
    def _():
        ext[0] = jnp.zeros_like(ext[0])

    @pl.when(chip == lax.axis_size("frame") - 1)
    def _():
        ext[2] = jnp.zeros_like(ext[2])

    return ext[...].reshape(-1, own.shape[1])


def act_grad_kernel(own, first_in, second_in, weight, pre_ref, _, out_ref, ext):
    count, channels = own.shape
    frames = slabs(own, first_in, second_in, ext)
    hop = count // 4
    total = None
    for k in range(9):
        first = (8 - k) * hop
        term = lax.dot_general(
            frames[first : first + count],
            weight[k * channels : (k + 1) * channels],
            (((1,), (1,)), ((), ())),
            preferred_element_type=jnp.float32,
        )
        total = term if total is None else total + term
    act_grad = total.astype(jnp.bfloat16).astype(jnp.float32)
    pre = pre_ref[...]
    sig = jax.nn.sigmoid(pre)
    out_ref[...] = (act_grad * (sig * (1.0 + pre * (1.0 - sig)))).astype(jnp.bfloat16)


def temporal_kernel(feats, act, first_in, second_in, weight, _, out_ref, done_ref, ext):
    count, channels = feats.shape
    own = act.at[lax.axis_index("tile")]
    frames = slabs(own, first_in, second_in, ext)
    hop = count // 4
    columns = jnp.concatenate([frames[k * hop : k * hop + count] for k in range(9)], axis=1)
    mixed = jnp.dot(columns, weight[...], preferred_element_type=jnp.float32)
    out_ref[...] = (feats[...].astype(jnp.float32) + mixed).astype(jnp.bfloat16)
    done_ref[...] = jnp.zeros_like(done_ref)


def own_term_kernel(feats_t, own, total_ref):
    channels = own.shape[3]
    after, same, before = column_shifts(own[...].reshape(-1, channels), own.shape[2])
    left = feats_t[0]
    for s, right in enumerate((before, same, after)):
        total_ref[s] = jnp.dot(left, right, preferred_element_type=jnp.float32)


def kernel_grad_kernel(
    feats_t, other, term, far_a_ref, far_b_ref, pass_ref, near_ref, keep_ref, total
):
    frames, rows, width, channels = other.shape
    tile = lax.axis_index("tile")
    chip = lax.axis_index("frame")
    after, same, before = column_shifts(other[...].reshape(-1, channels), width)
    left = feats_t[1]
    for s, right in enumerate((before, same, after)):
        both = term[s] + jnp.dot(left, right, preferred_element_type=jnp.float32)
        for r in range(3):
            tap = 3 * r + s
            total[tap * channels : (tap + 1) * channels] = both[r * channels : (r + 1) * channels]
    share = keep_ref.shape[0]
    half = share // 2
    for distance, skip, ref in (
        (3, 0, far_a_ref),
        (3, half, far_b_ref),
        (2, 0, pass_ref),
        (1, 0, near_ref),
        (0, 0, keep_ref),
    ):
        first = (2 * (chip ^ distance) + tile) * share + skip
        ref[...] = total[pl.ds(pl.multiple_of(first, 16), ref.shape[0])].astype(ref.dtype)


def input_grad_kernel(out_grad, own, other, weight, _, out_ref, done_ref, ext):
    frames, rows, width, channels = own.shape
    with_edges(own, other, ext)
    after, same, before = column_shifts(ext[...].reshape(-1, channels), width)
    shifts = [piece.reshape(ext.shape) for piece in (before, same, after)]
    total = out_grad[...].astype(jnp.float32)
    for r in range(3):
        for s in range(3):
            tap = 3 * r + s
            total = total + lax.dot_general(
                shifts[s][:, 2 - r : 2 - r + rows].reshape(-1, channels),
                weight[tap * channels : (tap + 1) * channels],
                (((1,), (1,)), ((), ())),
                preferred_element_type=jnp.float32,
            )
    out_ref[...] = total.astype(jnp.bfloat16)
    done_ref[...] = jnp.zeros_like(done_ref)


def per_device_pair(clip_feats, out_grad, spatial_weight, temporal_weight):
    frames, rows, width, channels = clip_feats.shape
    count = frames * rows * width
    chips = lax.axis_size("frame")
    cores = lax.axis_size("tile")
    scale = 1.0 / math.sqrt(frames * chips * rows * cores * width)
    outward = [(2 * z, 2 * z + 2) for z in range(chips - 1)]
    outward += [(2 * z + 3, 2 * z + 1) for z in range(chips - 1)]
    outward += [(2 * chips - 2, 2 * chips - 1), (1, 0)]
    inward = [(target, source) for source, target in outward]
    both = ("frame", "tile")
    swap = [(0, 1), (1, 0)]
    bf16, f32 = jnp.bfloat16, jnp.float32
    product = 2 * count * 9 * channels * channels
    flat = (count, channels)
    ext = ((frames, rows + 2, width, channels), bf16)
    image = ((frames, 2 * rows + 2, width, channels), bf16)
    three = ((3, count, channels), bf16)

    grad_flat = out_grad.reshape(flat)
    feat_flat = clip_feats.reshape(flat)
    grad_first = lax.ppermute(grad_flat, both, outward)
    grad_second = lax.ppermute(grad_flat, both, inward)
    feat_other = lax.ppermute(clip_feats, "tile", swap)

    (first,) = kernel_call(order_kernel, [((8, 128), f32)], [], 2 * product)
    pre, act = kernel_call(
        spatial_kernel,
        [(flat, f32), ((2, *flat), bf16)],
        [image, ((2, *flat), f32)],
        2 * product,
        clip_feats, spatial_weight, feat_other, first, anywhere=1,
    )
    act_in = lax.ppermute(act, both, outward)
    (feats_t,) = kernel_call(
        transpose_kernel,
        [((2, 3 * channels, count), bf16)],
        [image],
        0,
        clip_feats, feat_other, pre, anywhere=1,
    )
    (pre_grad,) = kernel_call(
        act_grad_kernel,
        [(flat, bf16)],
        [three],
        product,
        grad_flat, grad_first, grad_second, temporal_weight, pre, feats_t, anywhere=1,
    )
    pre_grad = pre_grad.reshape(clip_feats.shape)
    pre_other = lax.ppermute(pre_grad, "tile", swap)

    share = (9 * channels // (chips * cores), channels)
    (term,) = kernel_call(
        own_term_kernel,
        [((3, 3 * channels, channels), f32)],
        [],
        product,
        feats_t, pre_grad,
    )
    half = (share[0] // 2, channels)
    far_a, far_b, onward, near, keep = kernel_call(
        kernel_grad_kernel,
        [(half, bf16), (half, bf16), (share, f32), (share, bf16), (share, f32)],
        [((9 * channels, channels), f32)],
        product,
        feats_t, pre_other, term,
    )
    beside = [(z, z ^ 1) for z in range(chips)]
    across = [(z, z ^ 2) for z in range(chips)]
    far_in_a = lax.ppermute(far_a, "frame", beside)
    far_in_b = lax.ppermute(far_b, "frame", beside)
    near_in = lax.ppermute(near, "frame", beside)
    (sum_a,) = kernel_call(
        functools.partial(forward_sum_kernel, first=0),
        [(half, bf16)],
        [],
        4 * product,
        onward, far_in_a, act_in, anywhere=1,
    )
    last_a = lax.ppermute(sum_a, "frame", across)
    (sum_b,) = kernel_call(
        functools.partial(forward_sum_kernel, first=half[0]),
        [(half, bf16)],
        [],
        0,
        onward, far_in_b, sum_a, anywhere=1,
    )
    last_b = lax.ppermute(sum_b, "frame", across)
    act_first, act_pass = kernel_call(
        split_kernel, [(flat, bf16)] * 2, [], 0, act_in, sum_b, anywhere=1
    )
    act_second = lax.ppermute(act_pass, "tile", swap)

    input_grad, done = kernel_call(
        input_grad_kernel,
        [(flat, bf16), ((8, 128), f32)],
        [ext],
        product,
        grad_flat, pre_grad, pre_other, spatial_weight, sum_b, anywhere=1,
    )
    (arrived,) = kernel_call(
        order_kernel, [((8, 128), f32)], [], 20 * product, last_a, near_in, done, anywhere=3
    )
    block_out, done = kernel_call(
        temporal_kernel,
        [(flat, bf16), ((8, 128), f32)],
        [three],
        product,
        feat_flat, act, act_first, act_second, temporal_weight, arrived, anywhere=1,
    )
    (weight_grad,) = kernel_call(
        functools.partial(last_sum_kernel, scale=scale),
        [(share, f32)],
        [],
        0,
        keep, near_in, last_a, last_b, done, anywhere=1,
    )
    return (
        block_out.reshape(clip_feats.shape),
        input_grad.reshape(clip_feats.shape),
        weight_grad,
    )


def per_device(clip_feats, *rest):
    pairs = lax.axis_size("tile") == 2 and lax.axis_size("frame") == 4
    if pairs and clip_feats.shape[0] == 4 * TAP_DILATION:
        return per_device_pair(clip_feats, *rest)
    return per_device_any(clip_feats, *rest)


def solution(mesh):
    return jax.shard_map(
        per_device,
        mesh=mesh,
        in_specs=(
            P(("clip", "frame"), "tile", None, None),
            P(("clip", "frame"), "tile", None, None),
            P(),
            P(),
        ),
        out_specs=(
            P(("clip", "frame"), "tile", None, None),
            P(("clip", "frame"), "tile", None, None),
            P(("clip", "frame", "tile"), None),
        ),
        check_vma=False,
    )
```

```python
import functools
import math

import jax
import jax.numpy as jnp
from jax import lax
from jax.experimental import pallas as pl
from jax.experimental.pallas import tpu as pltpu
from jax.sharding import PartitionSpec as P

TAP_DILATION = 2
VMEM_LIMIT = 32 * 1024 * 1024


def padded_2(block, sides, width):
    for axis, dim in sides:
        count = lax.axis_size(axis)
        forward = [(i, i + 1) for i in range(count - 1)]
        backward = [(target, source) for source, target in forward]
        low = lax.ppermute(
            lax.slice_in_dim(block, block.shape[dim] - width, None, axis=dim), axis, forward
        )
        high = lax.ppermute(lax.slice_in_dim(block, 0, width, axis=dim), axis, backward)
        block = jnp.concatenate([low, block, high], axis=dim)
    return block


def tile_columns(extended, tile_rows, width_cells, backward_pass):
    padded = jnp.pad(extended, ((0, 0), (0, 0), (1, 1), (0, 0)))
    pieces = []
    for row_shift in range(3):
        for col_shift in range(3):
            row_start = 2 - row_shift if backward_pass else row_shift
            col_start = 2 - col_shift if backward_pass else col_shift
            pieces.append(
                padded[:, row_start : row_start + tile_rows, col_start : col_start + width_cells, :]
            )
    channels = extended.shape[3]
    return jnp.concatenate(pieces, axis=-1).reshape(-1, 9 * channels)


def temporal_taps(padded_seq, weight, frame_count, backward_pass):
    pieces = []
    for temporal_tap_index in range(9):
        first_frame_index = (
            (8 - temporal_tap_index) * TAP_DILATION
            if backward_pass
            else temporal_tap_index * TAP_DILATION
        )
        pieces.append(padded_seq[first_frame_index : first_frame_index + frame_count])
    channels = padded_seq.shape[2]
    columns = jnp.concatenate(pieces, axis=-1).reshape(-1, 9 * channels)
    return jnp.dot(columns, weight, preferred_element_type=jnp.float32)


def per_device_any(clip_feats, out_grad, spatial_weight, temporal_weight):
    slab_frames, tile_rows, width_cells, channels = clip_feats.shape
    row_count = slab_frames * tile_rows * width_cells
    frame_devs = lax.axis_size("frame")
    tile_devs = lax.axis_size("tile")
    grad_scale = jnp.float32(
        1.0 / math.sqrt(slab_frames * frame_devs * tile_rows * tile_devs * width_cells)
    )
    spatial_back = (
        spatial_weight.reshape(9, channels, channels)
        .transpose(0, 2, 1)
        .reshape(9 * channels, channels)
    )
    temporal_back = (
        temporal_weight.reshape(9, channels, channels)
        .transpose(0, 2, 1)
        .reshape(9 * channels, channels)
    )
    feat_ext = padded_2(clip_feats, (("tile", 1),), 1)
    feat_columns = tile_columns(feat_ext, tile_rows, width_cells, False)
    pre = jnp.dot(feat_columns, spatial_weight, preferred_element_type=jnp.float32)
    act = jax.nn.silu(pre).astype(jnp.bfloat16)
    temporal_reach = 4 * TAP_DILATION
    per_group = tile_rows * width_cells // frame_devs
    grouped = (slab_frames, frame_devs, per_group, channels)
    act_part = lax.all_to_all(
        act.reshape(grouped), "frame", split_axis=1, concat_axis=0, tiled=True
    )
    grad_part = lax.all_to_all(out_grad, "frame", split_axis=1, concat_axis=0, tiled=True)
    feat_part = lax.all_to_all(clip_feats, "frame", split_axis=1, concat_axis=0, tiled=True)
    frame_count = act_part.shape[0]
    item_count = act_part.shape[2]
    act_pad = jnp.pad(
        act_part.reshape(frame_count, item_count, channels),
        ((temporal_reach, temporal_reach), (0, 0), (0, 0)),
    )
    grad_pad = jnp.pad(
        grad_part.reshape(frame_count, item_count, channels),
        ((temporal_reach, temporal_reach), (0, 0), (0, 0)),
    )
    mixed = temporal_taps(act_pad, temporal_weight, frame_count, False)
    out_part = (feat_part.reshape(-1, channels).astype(jnp.float32) + mixed).astype(jnp.bfloat16)
    back_part = temporal_taps(grad_pad, temporal_back, frame_count, True).astype(jnp.bfloat16)
    out_part = out_part.reshape(frame_count, 1, item_count, channels)
    back_part = back_part.reshape(frame_count, 1, item_count, channels)
    out_slab = lax.all_to_all(out_part, "frame", split_axis=0, concat_axis=1, tiled=True)
    grad_slab = lax.all_to_all(back_part, "frame", split_axis=0, concat_axis=1, tiled=True)
    act_grad = grad_slab.reshape(row_count, channels)
    sig = jax.nn.sigmoid(pre)
    pre_grad = (act_grad.astype(jnp.float32) * (sig * (1.0 + pre * (1.0 - sig)))).astype(
        jnp.bfloat16
    )
    full_term = lax.dot_general(
        feat_columns, pre_grad, (((0,), (0,)), ((), ())), preferred_element_type=jnp.float32
    )
    summed = lax.psum_scatter(full_term, ("frame", "tile"), scatter_dimension=0, tiled=True)
    weight_grad = summed * grad_scale
    grad_ext = padded_2(
        pre_grad.reshape(slab_frames, tile_rows, width_cells, channels), (("tile", 1),), 1
    )
    grad_columns = tile_columns(grad_ext, tile_rows, width_cells, True)
    local_back = jnp.dot(grad_columns, spatial_back, preferred_element_type=jnp.float32)
    input_grad = (out_grad.reshape(row_count, channels).astype(jnp.float32) + local_back).astype(
        jnp.bfloat16
    )
    input_grad = input_grad.reshape(slab_frames, tile_rows, width_cells, channels)
    return (out_slab, input_grad, weight_grad)


def kernel_call(body, outs, scratch, flops, *args, anywhere=0):
    moved = sum(a.size * a.dtype.itemsize for a in args)
    moved += sum(math.prod(shape) * jnp.dtype(kind).itemsize for shape, kind in outs)
    spaces = [pltpu.VMEM] * (len(args) - anywhere) + [pl.ANY] * anywhere
    return pl.pallas_call(
        body,
        out_shape=tuple(jax.ShapeDtypeStruct(shape, kind) for shape, kind in outs),
        in_specs=[pl.BlockSpec(memory_space=space) for space in spaces],
        out_specs=tuple(pl.BlockSpec(memory_space=pltpu.VMEM) for _ in outs),
        scratch_shapes=[pltpu.VMEM(shape, kind) for shape, kind in scratch],
        compiler_params=pltpu.CompilerParams(vmem_limit_bytes=VMEM_LIMIT),
        cost_estimate=pl.CostEstimate(flops=flops, bytes_accessed=moved, transcendentals=0),
    )(*args)


def shifted(values, width, step):
    rows = values.shape[0]
    at = lax.broadcasted_iota(jnp.int32, values.shape, 0) % width
    moved = pltpu.roll(values, step % rows, 0)
    inside = at >= step if step > 0 else at < width + step
    return jnp.where(inside, moved, 0.0)


def column_shifts(values, width):
    wide = values.astype(jnp.float32)
    return (
        shifted(wide, width, 1).astype(values.dtype),
        values,
        shifted(wide, width, -1).astype(values.dtype),
    )


def with_edges(own, other, ext):
    rows = own.shape[1]
    tile = lax.axis_index("tile")
    ext[:, 1 : rows + 1] = own[...]
    above, below = other[:, rows - 1], other[:, 0]
    ext[:, 0] = jnp.where(tile == 1, above, jnp.zeros_like(above))
    ext[:, rows + 1] = jnp.where(tile == 0, below, jnp.zeros_like(below))


def whole_image(own, other, image):
    rows = own.shape[1]
    tile = lax.axis_index("tile")
    image[:, 0] = jnp.zeros_like(image[:, 0])
    image[:, 2 * rows + 1] = jnp.zeros_like(image[:, 2 * rows + 1])
    image[:, pl.ds(1 + tile * rows, rows)] = own[...]
    image[:, pl.ds(1 + (1 - tile) * rows, rows)] = other[...]


def order_kernel(*refs):
    refs[-1][...] = jnp.zeros_like(refs[-1])


def spatial_kernel(own, weight, other, _, pre_ref, act_ref, image, pre_all):
    frames, rows, width, channels = own.shape
    whole_image(own, other, image)
    shifts = column_shifts(image[...].reshape(-1, channels), width)
    shifts = [piece.reshape(image.shape) for piece in shifts]
    for half in range(2):
        columns = jnp.concatenate(
            [
                shifts[s][:, half * rows + r : half * rows + r + rows].reshape(-1, channels)
                for r in range(3)
                for s in range(3)
            ],
            axis=1,
        )
        pre = jnp.dot(columns, weight[...], preferred_element_type=jnp.float32)
        pre_all[half] = pre
        act_ref[half] = (pre * jax.nn.sigmoid(pre)).astype(jnp.bfloat16)
    pre_ref[...] = pre_all[lax.axis_index("tile")]


def release_kernel(act, _first, _second, out_ref):
    out_ref[...] = act[...]


def split_kernel(arrived, _, mine_ref, other_ref):
    tile = lax.axis_index("tile")
    mine_ref[...] = arrived[tile]
    other_ref[...] = arrived[1 - tile]


def forward_sum_kernel(partial, arrived, *rest, first):
    sum_ref = rest[-1]
    rows = partial[first : first + sum_ref.shape[0]]
    came = arrived[: sum_ref.shape[0]].astype(jnp.float32)
    sum_ref[...] = (rows + came).astype(sum_ref.dtype)


def last_sum_kernel(keep, near, last_a, last_b, _, out_ref, *, scale):
    half = last_a.shape[0]
    for first, last in ((0, last_a), (half, last_b)):
        total = keep[first : first + half] + near[first : first + half].astype(jnp.float32)
        out_ref[first : first + half] = (total + last[...].astype(jnp.float32)) * scale


def transpose_kernel(own, other, _, out_ref, image):
    frames, rows, width, channels = own.shape
    tile = lax.axis_index("tile")
    whole_image(own, other, image)
    for which, first in enumerate((tile * rows, (1 - tile) * rows)):
        for r in range(3):
            block = image[:, pl.ds(first + r, rows)].reshape(-1, channels)
            out_ref[which, r * channels : (r + 1) * channels] = block.T


def slabs(own, first, second, ext):
    tile = lax.axis_index("tile")
    ext[2 * tile] = first[...]
    ext[1] = own[...]
    ext[2 - 2 * tile] = second[...]
    chip = lax.axis_index("frame")

    @pl.when(chip == 0)
    def _():
        ext[0] = jnp.zeros_like(ext[0])

    @pl.when(chip == lax.axis_size("frame") - 1)
    def _():
        ext[2] = jnp.zeros_like(ext[2])

    return ext[...].reshape(-1, own.shape[1])


def act_grad_kernel(own, first_in, second_in, weight, pre_ref, _, out_ref, ext):
    count, channels = own.shape
    frames = slabs(own, first_in, second_in, ext)
    hop = count // 4
    total = None
    for k in range(9):
        first = (8 - k) * hop
        term = lax.dot_general(
            frames[first : first + count],
            weight[k * channels : (k + 1) * channels],
            (((1,), (1,)), ((), ())),
            preferred_element_type=jnp.float32,
        )
        total = term if total is None else total + term
    act_grad = total.astype(jnp.bfloat16).astype(jnp.float32)
    pre = pre_ref[...]
    sig = jax.nn.sigmoid(pre)
    out_ref[...] = (act_grad * (sig * (1.0 + pre * (1.0 - sig)))).astype(jnp.bfloat16)


def temporal_kernel(feats, act, first_in, second_in, weight, _, out_ref, done_ref, ext):
    count, channels = feats.shape
    own = act.at[lax.axis_index("tile")]
    frames = slabs(own, first_in, second_in, ext)
    hop = count // 4
    columns = jnp.concatenate([frames[k * hop : k * hop + count] for k in range(9)], axis=1)
    mixed = jnp.dot(columns, weight[...], preferred_element_type=jnp.float32)
    out_ref[...] = (feats[...].astype(jnp.float32) + mixed).astype(jnp.bfloat16)
    done_ref[...] = jnp.zeros_like(done_ref)


def own_term_kernel(feats_t, own, total_ref):
    channels = own.shape[3]
    after, same, before = column_shifts(own[...].reshape(-1, channels), own.shape[2])
    left = feats_t[0]
    for s, right in enumerate((before, same, after)):
        total_ref[s] = jnp.dot(left, right, preferred_element_type=jnp.float32)


def kernel_grad_kernel(
    feats_t, other, term, far_a_ref, far_b_ref, pass_ref, near_ref, keep_ref, total
):
    frames, rows, width, channels = other.shape
    tile = lax.axis_index("tile")
    chip = lax.axis_index("frame")
    after, same, before = column_shifts(other[...].reshape(-1, channels), width)
    left = feats_t[1]
    for s, right in enumerate((before, same, after)):
        both = term[s] + jnp.dot(left, right, preferred_element_type=jnp.float32)
        for r in range(3):
            tap = 3 * r + s
            total[tap * channels : (tap + 1) * channels] = both[r * channels : (r + 1) * channels]
    share = keep_ref.shape[0]
    half = share // 2
    for distance, skip, ref in (
        (3, 0, far_a_ref),
        (3, half, far_b_ref),
        (2, 0, pass_ref),
        (1, 0, near_ref),
        (0, 0, keep_ref),
    ):
        first = (2 * (chip ^ distance) + tile) * share + skip
        ref[...] = total[pl.ds(pl.multiple_of(first, 16), ref.shape[0])].astype(ref.dtype)


def input_grad_kernel(out_grad, own, other, weight, _, out_ref, done_ref, ext):
    frames, rows, width, channels = own.shape
    with_edges(own, other, ext)
    after, same, before = column_shifts(ext[...].reshape(-1, channels), width)
    shifts = [piece.reshape(ext.shape) for piece in (before, same, after)]
    total = out_grad[...].astype(jnp.float32)
    for r in range(3):
        for s in range(3):
            tap = 3 * r + s
            total = total + lax.dot_general(
                shifts[s][:, 2 - r : 2 - r + rows].reshape(-1, channels),
                weight[tap * channels : (tap + 1) * channels],
                (((1,), (1,)), ((), ())),
                preferred_element_type=jnp.float32,
            )
    out_ref[...] = total.astype(jnp.bfloat16)
    done_ref[...] = jnp.zeros_like(done_ref)


def per_device_pair(clip_feats, out_grad, spatial_weight, temporal_weight):
    frames, rows, width, channels = clip_feats.shape
    count = frames * rows * width
    chips = lax.axis_size("frame")
    cores = lax.axis_size("tile")
    scale = 1.0 / math.sqrt(frames * chips * rows * cores * width)
    outward = [(2 * z, 2 * z + 2) for z in range(chips - 1)]
    outward += [(2 * z + 3, 2 * z + 1) for z in range(chips - 1)]
    outward += [(2 * chips - 2, 2 * chips - 1), (1, 0)]
    inward = [(target, source) for source, target in outward]
    both = ("frame", "tile")
    swap = [(0, 1), (1, 0)]
    bf16, f32 = jnp.bfloat16, jnp.float32
    product = 2 * count * 9 * channels * channels
    flat = (count, channels)
    ext = ((frames, rows + 2, width, channels), bf16)
    image = ((frames, 2 * rows + 2, width, channels), bf16)
    three = ((3, count, channels), bf16)

    grad_flat = out_grad.reshape(flat)
    feat_flat = clip_feats.reshape(flat)
    grad_first = lax.ppermute(grad_flat, both, outward)
    grad_second = lax.ppermute(grad_flat, both, inward)
    feat_other = lax.ppermute(clip_feats, "tile", swap)

    (first,) = kernel_call(order_kernel, [((8, 128), f32)], [], 2 * product)
    pre, act = kernel_call(
        spatial_kernel,
        [(flat, f32), ((2, *flat), bf16)],
        [image, ((2, *flat), f32)],
        2 * product,
        clip_feats, spatial_weight, feat_other, first, anywhere=1,
    )
    (feats_t,) = kernel_call(
        transpose_kernel,
        [((2, 3 * channels, count), bf16)],
        [image],
        0,
        clip_feats, feat_other, pre, anywhere=1,
    )
    (act_out,) = kernel_call(
        release_kernel, [((2, *flat), bf16)], [], 0, act, grad_first, feats_t, anywhere=2
    )
    act_in = lax.ppermute(act_out, both, outward)
    (pre_grad,) = kernel_call(
        act_grad_kernel,
        [(flat, bf16)],
        [three],
        product,
        grad_flat, grad_first, grad_second, temporal_weight, pre, feats_t, anywhere=1,
    )
    pre_grad = pre_grad.reshape(clip_feats.shape)
    pre_other = lax.ppermute(pre_grad, "tile", swap)

    share = (9 * channels // (chips * cores), channels)
    (term,) = kernel_call(
        own_term_kernel,
        [((3, 3 * channels, channels), f32)],
        [],
        product,
        feats_t, pre_grad,
    )
    half = (share[0] // 2, channels)
    far_a, far_b, onward, near, keep = kernel_call(
        kernel_grad_kernel,
        [(half, bf16), (half, bf16), (share, f32), (share, bf16), (share, f32)],
        [((9 * channels, channels), f32)],
        product,
        feats_t, pre_other, term,
    )
    beside = [(z, z ^ 1) for z in range(chips)]
    across = [(z, z ^ 2) for z in range(chips)]
    far_in_a = lax.ppermute(far_a, "frame", beside)
    far_in_b = lax.ppermute(far_b, "frame", beside)
    near_in = lax.ppermute(near, "frame", beside)
    (sum_a,) = kernel_call(
        functools.partial(forward_sum_kernel, first=0),
        [(half, bf16)],
        [],
        4 * product,
        onward, far_in_a, act_in, anywhere=1,
    )
    last_a = lax.ppermute(sum_a, "frame", across)
    (sum_b,) = kernel_call(
        functools.partial(forward_sum_kernel, first=half[0]),
        [(half, bf16)],
        [],
        0,
        onward, far_in_b, sum_a, anywhere=1,
    )
    last_b = lax.ppermute(sum_b, "frame", across)
    act_first, act_pass = kernel_call(
        split_kernel, [(flat, bf16)] * 2, [], 0, act_in, sum_b, anywhere=1
    )
    act_second = lax.ppermute(act_pass, "tile", swap)

    input_grad, done = kernel_call(
        input_grad_kernel,
        [(flat, bf16), ((8, 128), f32)],
        [ext],
        product,
        grad_flat, pre_grad, pre_other, spatial_weight, sum_b, anywhere=1,
    )
    (arrived,) = kernel_call(
        order_kernel, [((8, 128), f32)], [], 20 * product, last_a, near_in, done, anywhere=3
    )
    block_out, done = kernel_call(
        temporal_kernel,
        [(flat, bf16), ((8, 128), f32)],
        [three],
        product,
        feat_flat, act, act_first, act_second, temporal_weight, arrived, anywhere=1,
    )
    (weight_grad,) = kernel_call(
        functools.partial(last_sum_kernel, scale=scale),
        [(share, f32)],
        [],
        0,
        keep, near_in, last_a, last_b, done, anywhere=1,
    )
    return (
        block_out.reshape(clip_feats.shape),
        input_grad.reshape(clip_feats.shape),
        weight_grad,
    )


def per_device(clip_feats, *rest):
    pairs = lax.axis_size("tile") == 2 and lax.axis_size("frame") == 4
    if pairs and clip_feats.shape[0] == 4 * TAP_DILATION:
        return per_device_pair(clip_feats, *rest)
    return per_device_any(clip_feats, *rest)


def solution(mesh):
    return jax.shard_map(
        per_device,
        mesh=mesh,
        in_specs=(
            P(("clip", "frame"), "tile", None, None),
            P(("clip", "frame"), "tile", None, None),
            P(),
            P(),
        ),
        out_specs=(
            P(("clip", "frame"), "tile", None, None),
            P(("clip", "frame"), "tile", None, None),
            P(("clip", "frame", "tile"), None),
        ),
        check_vma=False,
    )
```

```python
import functools
import math

import jax
import jax.numpy as jnp
from jax import lax
from jax.experimental import pallas as pl
from jax.experimental.pallas import tpu as pltpu
from jax.sharding import PartitionSpec as P

TAP_DILATION = 2
VMEM_LIMIT = 32 * 1024 * 1024


def padded_2(block, sides, width):
    for axis, dim in sides:
        count = lax.axis_size(axis)
        forward = [(i, i + 1) for i in range(count - 1)]
        backward = [(target, source) for source, target in forward]
        low = lax.ppermute(
            lax.slice_in_dim(block, block.shape[dim] - width, None, axis=dim), axis, forward
        )
        high = lax.ppermute(lax.slice_in_dim(block, 0, width, axis=dim), axis, backward)
        block = jnp.concatenate([low, block, high], axis=dim)
    return block


def tile_columns(extended, tile_rows, width_cells, backward_pass):
    padded = jnp.pad(extended, ((0, 0), (0, 0), (1, 1), (0, 0)))
    pieces = []
    for row_shift in range(3):
        for col_shift in range(3):
            row_start = 2 - row_shift if backward_pass else row_shift
            col_start = 2 - col_shift if backward_pass else col_shift
            pieces.append(
                padded[:, row_start : row_start + tile_rows, col_start : col_start + width_cells, :]
            )
    channels = extended.shape[3]
    return jnp.concatenate(pieces, axis=-1).reshape(-1, 9 * channels)


def temporal_taps(padded_seq, weight, frame_count, backward_pass):
    pieces = []
    for temporal_tap_index in range(9):
        first_frame_index = (
            (8 - temporal_tap_index) * TAP_DILATION
            if backward_pass
            else temporal_tap_index * TAP_DILATION
        )
        pieces.append(padded_seq[first_frame_index : first_frame_index + frame_count])
    channels = padded_seq.shape[2]
    columns = jnp.concatenate(pieces, axis=-1).reshape(-1, 9 * channels)
    return jnp.dot(columns, weight, preferred_element_type=jnp.float32)


def per_device_any(clip_feats, out_grad, spatial_weight, temporal_weight):
    slab_frames, tile_rows, width_cells, channels = clip_feats.shape
    row_count = slab_frames * tile_rows * width_cells
    frame_devs = lax.axis_size("frame")
    tile_devs = lax.axis_size("tile")
    grad_scale = jnp.float32(
        1.0 / math.sqrt(slab_frames * frame_devs * tile_rows * tile_devs * width_cells)
    )
    spatial_back = (
        spatial_weight.reshape(9, channels, channels)
        .transpose(0, 2, 1)
        .reshape(9 * channels, channels)
    )
    temporal_back = (
        temporal_weight.reshape(9, channels, channels)
        .transpose(0, 2, 1)
        .reshape(9 * channels, channels)
    )
    feat_ext = padded_2(clip_feats, (("tile", 1),), 1)
    feat_columns = tile_columns(feat_ext, tile_rows, width_cells, False)
    pre = jnp.dot(feat_columns, spatial_weight, preferred_element_type=jnp.float32)
    act = jax.nn.silu(pre).astype(jnp.bfloat16)
    temporal_reach = 4 * TAP_DILATION
    per_group = tile_rows * width_cells // frame_devs
    grouped = (slab_frames, frame_devs, per_group, channels)
    act_part = lax.all_to_all(
        act.reshape(grouped), "frame", split_axis=1, concat_axis=0, tiled=True
    )
    grad_part = lax.all_to_all(out_grad, "frame", split_axis=1, concat_axis=0, tiled=True)
    feat_part = lax.all_to_all(clip_feats, "frame", split_axis=1, concat_axis=0, tiled=True)
    frame_count = act_part.shape[0]
    item_count = act_part.shape[2]
    act_pad = jnp.pad(
        act_part.reshape(frame_count, item_count, channels),
        ((temporal_reach, temporal_reach), (0, 0), (0, 0)),
    )
    grad_pad = jnp.pad(
        grad_part.reshape(frame_count, item_count, channels),
        ((temporal_reach, temporal_reach), (0, 0), (0, 0)),
    )
    mixed = temporal_taps(act_pad, temporal_weight, frame_count, False)
    out_part = (feat_part.reshape(-1, channels).astype(jnp.float32) + mixed).astype(jnp.bfloat16)
    back_part = temporal_taps(grad_pad, temporal_back, frame_count, True).astype(jnp.bfloat16)
    out_part = out_part.reshape(frame_count, 1, item_count, channels)
    back_part = back_part.reshape(frame_count, 1, item_count, channels)
    out_slab = lax.all_to_all(out_part, "frame", split_axis=0, concat_axis=1, tiled=True)
    grad_slab = lax.all_to_all(back_part, "frame", split_axis=0, concat_axis=1, tiled=True)
    act_grad = grad_slab.reshape(row_count, channels)
    sig = jax.nn.sigmoid(pre)
    pre_grad = (act_grad.astype(jnp.float32) * (sig * (1.0 + pre * (1.0 - sig)))).astype(
        jnp.bfloat16
    )
    full_term = lax.dot_general(
        feat_columns, pre_grad, (((0,), (0,)), ((), ())), preferred_element_type=jnp.float32
    )
    summed = lax.psum_scatter(full_term, ("frame", "tile"), scatter_dimension=0, tiled=True)
    weight_grad = summed * grad_scale
    grad_ext = padded_2(
        pre_grad.reshape(slab_frames, tile_rows, width_cells, channels), (("tile", 1),), 1
    )
    grad_columns = tile_columns(grad_ext, tile_rows, width_cells, True)
    local_back = jnp.dot(grad_columns, spatial_back, preferred_element_type=jnp.float32)
    input_grad = (out_grad.reshape(row_count, channels).astype(jnp.float32) + local_back).astype(
        jnp.bfloat16
    )
    input_grad = input_grad.reshape(slab_frames, tile_rows, width_cells, channels)
    return (out_slab, input_grad, weight_grad)


def kernel_call(body, outs, scratch, flops, *args, anywhere=0):
    moved = sum(a.size * a.dtype.itemsize for a in args)
    moved += sum(math.prod(shape) * jnp.dtype(kind).itemsize for shape, kind in outs)
    spaces = [pltpu.VMEM] * (len(args) - anywhere) + [pl.ANY] * anywhere
    return pl.pallas_call(
        body,
        out_shape=tuple(jax.ShapeDtypeStruct(shape, kind) for shape, kind in outs),
        in_specs=[pl.BlockSpec(memory_space=space) for space in spaces],
        out_specs=tuple(pl.BlockSpec(memory_space=pltpu.VMEM) for _ in outs),
        scratch_shapes=[pltpu.VMEM(shape, kind) for shape, kind in scratch],
        compiler_params=pltpu.CompilerParams(vmem_limit_bytes=VMEM_LIMIT),
        cost_estimate=pl.CostEstimate(flops=flops, bytes_accessed=moved, transcendentals=0),
    )(*args)


def shifted(values, width, step):
    rows = values.shape[0]
    at = lax.broadcasted_iota(jnp.int32, values.shape, 0) % width
    moved = pltpu.roll(values, step % rows, 0)
    inside = at >= step if step > 0 else at < width + step
    return jnp.where(inside, moved, 0.0)


def column_shifts(values, width):
    wide = values.astype(jnp.float32)
    return (
        shifted(wide, width, 1).astype(values.dtype),
        values,
        shifted(wide, width, -1).astype(values.dtype),
    )


def with_edges(own, other, ext):
    rows = own.shape[1]
    tile = lax.axis_index("tile")
    ext[:, 1 : rows + 1] = own[...]
    above, below = other[:, rows - 1], other[:, 0]
    ext[:, 0] = jnp.where(tile == 1, above, jnp.zeros_like(above))
    ext[:, rows + 1] = jnp.where(tile == 0, below, jnp.zeros_like(below))


def whole_image(own, other, image):
    rows = own.shape[1]
    tile = lax.axis_index("tile")
    image[:, 0] = jnp.zeros_like(image[:, 0])
    image[:, 2 * rows + 1] = jnp.zeros_like(image[:, 2 * rows + 1])
    image[:, pl.ds(1 + tile * rows, rows)] = own[...]
    image[:, pl.ds(1 + (1 - tile) * rows, rows)] = other[...]


def order_kernel(*refs):
    refs[-1][...] = jnp.zeros_like(refs[-1])


def spatial_kernel(own, weight, other, _, pre_ref, act_ref, image, pre_all):
    frames, rows, width, channels = own.shape
    whole_image(own, other, image)
    shifts = column_shifts(image[...].reshape(-1, channels), width)
    shifts = [piece.reshape(image.shape) for piece in shifts]
    for half in range(2):
        columns = jnp.concatenate(
            [
                shifts[s][:, half * rows + r : half * rows + r + rows].reshape(-1, channels)
                for r in range(3)
                for s in range(3)
            ],
            axis=1,
        )
        pre = jnp.dot(columns, weight[...], preferred_element_type=jnp.float32)
        pre_all[half] = pre
        act_ref[half] = (pre * jax.nn.sigmoid(pre)).astype(jnp.bfloat16)
    pre_ref[...] = pre_all[lax.axis_index("tile")]


def split_kernel(arrived, sum_a, sum_b, mine_ref, other_ref, sum_ref):
    tile = lax.axis_index("tile")
    half = sum_a.shape[0]
    sum_ref[:half] = sum_a[...]
    sum_ref[half:] = sum_b[...]
    mine_ref[...] = arrived[tile]
    other_ref[...] = arrived[1 - tile]


def forward_sum_kernel(partial, arrived, *rest, first):
    sum_ref = rest[-1]
    rows = partial[first : first + sum_ref.shape[0]]
    came = arrived[: sum_ref.shape[0]].astype(jnp.float32)
    sum_ref[...] = (rows + came).astype(sum_ref.dtype)


def last_sum_kernel(keep, near, even_a, even_b, odd_all, _, out_ref, *, scale):
    half = even_a.shape[0]
    chip_is_even = lax.axis_index("frame") % 2 == 0
    for first, even in ((0, even_a), (half, even_b)):
        total = keep[first : first + half] + near[first : first + half].astype(jnp.float32)
        last = jnp.where(chip_is_even, even[...], odd_all[first : first + half])
        out_ref[first : first + half] = (total + last.astype(jnp.float32)) * scale


def transpose_kernel(own, other, _, out_ref, image):
    frames, rows, width, channels = own.shape
    tile = lax.axis_index("tile")
    whole_image(own, other, image)
    for which, first in enumerate((tile * rows, (1 - tile) * rows)):
        for r in range(3):
            block = image[:, pl.ds(first + r, rows)].reshape(-1, channels)
            out_ref[which, r * channels : (r + 1) * channels] = block.T


def slabs(own, first, second, ext):
    tile = lax.axis_index("tile")
    ext[2 * tile] = first[...]
    ext[1] = own[...]
    ext[2 - 2 * tile] = second[...]
    chip = lax.axis_index("frame")

    @pl.when(chip == 0)
    def _():
        ext[0] = jnp.zeros_like(ext[0])

    @pl.when(chip == lax.axis_size("frame") - 1)
    def _():
        ext[2] = jnp.zeros_like(ext[2])

    return ext[...].reshape(-1, own.shape[1])


def act_grad_kernel(own, first_in, second_in, weight, pre_ref, _, out_ref, ext):
    count, channels = own.shape
    frames = slabs(own, first_in, second_in, ext)
    hop = count // 4
    total = None
    for k in range(9):
        first = (8 - k) * hop
        term = lax.dot_general(
            frames[first : first + count],
            weight[k * channels : (k + 1) * channels],
            (((1,), (1,)), ((), ())),
            preferred_element_type=jnp.float32,
        )
        total = term if total is None else total + term
    act_grad = total.astype(jnp.bfloat16).astype(jnp.float32)
    pre = pre_ref[...]
    sig = jax.nn.sigmoid(pre)
    out_ref[...] = (act_grad * (sig * (1.0 + pre * (1.0 - sig)))).astype(jnp.bfloat16)


def temporal_kernel(feats, act, first_in, second_in, weight, _, out_ref, done_ref, ext):
    count, channels = feats.shape
    own = act.at[lax.axis_index("tile")]
    frames = slabs(own, first_in, second_in, ext)
    hop = count // 4
    columns = jnp.concatenate([frames[k * hop : k * hop + count] for k in range(9)], axis=1)
    mixed = jnp.dot(columns, weight[...], preferred_element_type=jnp.float32)
    out_ref[...] = (feats[...].astype(jnp.float32) + mixed).astype(jnp.bfloat16)
    done_ref[...] = jnp.zeros_like(done_ref)


def own_term_kernel(feats_t, own, total_ref):
    channels = own.shape[3]
    after, same, before = column_shifts(own[...].reshape(-1, channels), own.shape[2])
    left = feats_t[0]
    for s, right in enumerate((before, same, after)):
        total_ref[s] = jnp.dot(left, right, preferred_element_type=jnp.float32)


def kernel_grad_kernel(
    feats_t, other, term, far_a_ref, far_b_ref, pass_ref, near_ref, keep_ref, total
):
    frames, rows, width, channels = other.shape
    tile = lax.axis_index("tile")
    chip = lax.axis_index("frame")
    after, same, before = column_shifts(other[...].reshape(-1, channels), width)
    left = feats_t[1]
    for s, right in enumerate((before, same, after)):
        both = term[s] + jnp.dot(left, right, preferred_element_type=jnp.float32)
        for r in range(3):
            tap = 3 * r + s
            total[tap * channels : (tap + 1) * channels] = both[r * channels : (r + 1) * channels]
    share = keep_ref.shape[0]
    half = share // 2
    for distance, skip, ref in (
        (3, 0, far_a_ref),
        (3, half, far_b_ref),
        (2, 0, pass_ref),
        (1, 0, near_ref),
        (0, 0, keep_ref),
    ):
        first = (2 * (chip ^ distance) + tile) * share + skip
        ref[...] = total[pl.ds(pl.multiple_of(first, 16), ref.shape[0])].astype(ref.dtype)


def input_grad_kernel(out_grad, own, other, weight, _, out_ref, done_ref, ext):
    frames, rows, width, channels = own.shape
    with_edges(own, other, ext)
    after, same, before = column_shifts(ext[...].reshape(-1, channels), width)
    shifts = [piece.reshape(ext.shape) for piece in (before, same, after)]
    total = out_grad[...].astype(jnp.float32)
    for r in range(3):
        for s in range(3):
            tap = 3 * r + s
            total = total + lax.dot_general(
                shifts[s][:, 2 - r : 2 - r + rows].reshape(-1, channels),
                weight[tap * channels : (tap + 1) * channels],
                (((1,), (1,)), ((), ())),
                preferred_element_type=jnp.float32,
            )
    out_ref[...] = total.astype(jnp.bfloat16)
    done_ref[...] = jnp.zeros_like(done_ref)


def per_device_pair(clip_feats, out_grad, spatial_weight, temporal_weight):
    frames, rows, width, channels = clip_feats.shape
    count = frames * rows * width
    chips = lax.axis_size("frame")
    cores = lax.axis_size("tile")
    scale = 1.0 / math.sqrt(frames * chips * rows * cores * width)
    outward = [(2 * z, 2 * z + 2) for z in range(chips - 1)]
    outward += [(2 * z + 3, 2 * z + 1) for z in range(chips - 1)]
    outward += [(2 * chips - 2, 2 * chips - 1), (1, 0)]
    inward = [(target, source) for source, target in outward]
    both = ("frame", "tile")
    swap = [(0, 1), (1, 0)]
    bf16, f32 = jnp.bfloat16, jnp.float32
    product = 2 * count * 9 * channels * channels
    flat = (count, channels)
    ext = ((frames, rows + 2, width, channels), bf16)
    image = ((frames, 2 * rows + 2, width, channels), bf16)
    three = ((3, count, channels), bf16)

    grad_flat = out_grad.reshape(flat)
    feat_flat = clip_feats.reshape(flat)
    grad_first = lax.ppermute(grad_flat, both, outward)
    grad_second = lax.ppermute(grad_flat, both, inward)
    feat_other = lax.ppermute(clip_feats, "tile", swap)

    (first,) = kernel_call(order_kernel, [((8, 128), f32)], [], 2 * product)
    pre, act = kernel_call(
        spatial_kernel,
        [(flat, f32), ((2, *flat), bf16)],
        [image, ((2, *flat), f32)],
        2 * product,
        clip_feats, spatial_weight, feat_other, first, anywhere=1,
    )
    act_in = lax.ppermute(act, both, outward)
    (feats_t,) = kernel_call(
        transpose_kernel,
        [((2, 3 * channels, count), bf16)],
        [image],
        0,
        clip_feats, feat_other, pre, anywhere=1,
    )
    (pre_grad,) = kernel_call(
        act_grad_kernel,
        [(flat, bf16)],
        [three],
        product,
        grad_flat, grad_first, grad_second, temporal_weight, pre, feats_t, anywhere=1,
    )
    pre_grad = pre_grad.reshape(clip_feats.shape)
    pre_other = lax.ppermute(pre_grad, "tile", swap)

    share = (9 * channels // (chips * cores), channels)
    (term,) = kernel_call(
        own_term_kernel,
        [((3, 3 * channels, channels), f32)],
        [],
        product,
        feats_t, pre_grad,
    )
    half = (share[0] // 2, channels)
    far_a, far_b, onward, near, keep = kernel_call(
        kernel_grad_kernel,
        [(half, bf16), (half, bf16), (share, f32), (share, bf16), (share, f32)],
        [((9 * channels, channels), f32)],
        product,
        feats_t, pre_other, term,
    )
    beside = [(z, z ^ 1) for z in range(chips)]
    even, odd = (
        [(2 * z + t, 2 * (z ^ 2) + t if z % 2 == turn else 2 * z + 1 - t) for z in range(chips) for t in range(2)]
        for turn in range(2)
    )
    far_in_a = lax.ppermute(far_a, "frame", beside)
    far_in_b = lax.ppermute(far_b, "frame", beside)
    near_in = lax.ppermute(near, "frame", beside)
    (sum_a,) = kernel_call(
        functools.partial(forward_sum_kernel, first=0),
        [(half, bf16)],
        [],
        4 * product,
        onward, far_in_a, act_in, anywhere=1,
    )
    even_a = lax.ppermute(sum_a, both, even)
    (sum_b,) = kernel_call(
        functools.partial(forward_sum_kernel, first=half[0]),
        [(half, bf16)],
        [],
        0,
        onward, far_in_b, sum_a, anywhere=1,
    )
    even_b = lax.ppermute(sum_b, both, even)
    act_first, act_pass, sum_all = kernel_call(
        split_kernel, [(flat, bf16)] * 2 + [(share, bf16)], [], 0, act_in, sum_a, sum_b
    )
    odd_all = lax.ppermute(sum_all, both, odd)
    act_second = lax.ppermute(act_pass, "tile", swap)

    input_grad, done = kernel_call(
        input_grad_kernel,
        [(flat, bf16), ((8, 128), f32)],
        [ext],
        product,
        grad_flat, pre_grad, pre_other, spatial_weight, sum_b, anywhere=1,
    )
    (arrived,) = kernel_call(
        order_kernel, [((8, 128), f32)], [], 20 * product, even_a, near_in, done, anywhere=3
    )
    block_out, done = kernel_call(
        temporal_kernel,
        [(flat, bf16), ((8, 128), f32)],
        [three],
        product,
        feat_flat, act, act_first, act_second, temporal_weight, arrived, anywhere=1,
    )
    (weight_grad,) = kernel_call(
        functools.partial(last_sum_kernel, scale=scale),
        [(share, f32)],
        [],
        0,
        keep, near_in, even_a, even_b, odd_all, done, anywhere=1,
    )
    return (
        block_out.reshape(clip_feats.shape),
        input_grad.reshape(clip_feats.shape),
        weight_grad,
    )


def per_device(clip_feats, *rest):
    pairs = lax.axis_size("tile") == 2 and lax.axis_size("frame") == 4
    if pairs and clip_feats.shape[0] == 4 * TAP_DILATION:
        return per_device_pair(clip_feats, *rest)
    return per_device_any(clip_feats, *rest)


def solution(mesh):
    return jax.shard_map(
        per_device,
        mesh=mesh,
        in_specs=(
            P(("clip", "frame"), "tile", None, None),
            P(("clip", "frame"), "tile", None, None),
            P(),
            P(),
        ),
        out_specs=(
            P(("clip", "frame"), "tile", None, None),
            P(("clip", "frame"), "tile", None, None),
            P(("clip", "frame", "tile"), None),
        ),
        check_vma=False,
    )
```

```python
import functools
import math

import jax
import jax.numpy as jnp
from jax import lax
from jax.experimental import pallas as pl
from jax.experimental.pallas import tpu as pltpu
from jax.sharding import PartitionSpec as P

TAP_DILATION = 2
VMEM_LIMIT = 32 * 1024 * 1024


def padded_2(block, sides, width):
    for axis, dim in sides:
        count = lax.axis_size(axis)
        forward = [(i, i + 1) for i in range(count - 1)]
        backward = [(target, source) for source, target in forward]
        low = lax.ppermute(
            lax.slice_in_dim(block, block.shape[dim] - width, None, axis=dim), axis, forward
        )
        high = lax.ppermute(lax.slice_in_dim(block, 0, width, axis=dim), axis, backward)
        block = jnp.concatenate([low, block, high], axis=dim)
    return block


def tile_columns(extended, tile_rows, width_cells, backward_pass):
    padded = jnp.pad(extended, ((0, 0), (0, 0), (1, 1), (0, 0)))
    pieces = []
    for row_shift in range(3):
        for col_shift in range(3):
            row_start = 2 - row_shift if backward_pass else row_shift
            col_start = 2 - col_shift if backward_pass else col_shift
            pieces.append(
                padded[:, row_start : row_start + tile_rows, col_start : col_start + width_cells, :]
            )
    channels = extended.shape[3]
    return jnp.concatenate(pieces, axis=-1).reshape(-1, 9 * channels)


def temporal_taps(padded_seq, weight, frame_count, backward_pass):
    pieces = []
    for temporal_tap_index in range(9):
        first_frame_index = (
            (8 - temporal_tap_index) * TAP_DILATION
            if backward_pass
            else temporal_tap_index * TAP_DILATION
        )
        pieces.append(padded_seq[first_frame_index : first_frame_index + frame_count])
    channels = padded_seq.shape[2]
    columns = jnp.concatenate(pieces, axis=-1).reshape(-1, 9 * channels)
    return jnp.dot(columns, weight, preferred_element_type=jnp.float32)


def per_device_any(clip_feats, out_grad, spatial_weight, temporal_weight):
    slab_frames, tile_rows, width_cells, channels = clip_feats.shape
    row_count = slab_frames * tile_rows * width_cells
    frame_devs = lax.axis_size("frame")
    tile_devs = lax.axis_size("tile")
    grad_scale = jnp.float32(
        1.0 / math.sqrt(slab_frames * frame_devs * tile_rows * tile_devs * width_cells)
    )
    spatial_back = (
        spatial_weight.reshape(9, channels, channels)
        .transpose(0, 2, 1)
        .reshape(9 * channels, channels)
    )
    temporal_back = (
        temporal_weight.reshape(9, channels, channels)
        .transpose(0, 2, 1)
        .reshape(9 * channels, channels)
    )
    feat_ext = padded_2(clip_feats, (("tile", 1),), 1)
    feat_columns = tile_columns(feat_ext, tile_rows, width_cells, False)
    pre = jnp.dot(feat_columns, spatial_weight, preferred_element_type=jnp.float32)
    act = jax.nn.silu(pre).astype(jnp.bfloat16)
    temporal_reach = 4 * TAP_DILATION
    per_group = tile_rows * width_cells // frame_devs
    grouped = (slab_frames, frame_devs, per_group, channels)
    act_part = lax.all_to_all(
        act.reshape(grouped), "frame", split_axis=1, concat_axis=0, tiled=True
    )
    grad_part = lax.all_to_all(out_grad, "frame", split_axis=1, concat_axis=0, tiled=True)
    feat_part = lax.all_to_all(clip_feats, "frame", split_axis=1, concat_axis=0, tiled=True)
    frame_count = act_part.shape[0]
    item_count = act_part.shape[2]
    act_pad = jnp.pad(
        act_part.reshape(frame_count, item_count, channels),
        ((temporal_reach, temporal_reach), (0, 0), (0, 0)),
    )
    grad_pad = jnp.pad(
        grad_part.reshape(frame_count, item_count, channels),
        ((temporal_reach, temporal_reach), (0, 0), (0, 0)),
    )
    mixed = temporal_taps(act_pad, temporal_weight, frame_count, False)
    out_part = (feat_part.reshape(-1, channels).astype(jnp.float32) + mixed).astype(jnp.bfloat16)
    back_part = temporal_taps(grad_pad, temporal_back, frame_count, True).astype(jnp.bfloat16)
    out_part = out_part.reshape(frame_count, 1, item_count, channels)
    back_part = back_part.reshape(frame_count, 1, item_count, channels)
    out_slab = lax.all_to_all(out_part, "frame", split_axis=0, concat_axis=1, tiled=True)
    grad_slab = lax.all_to_all(back_part, "frame", split_axis=0, concat_axis=1, tiled=True)
    act_grad = grad_slab.reshape(row_count, channels)
    sig = jax.nn.sigmoid(pre)
    pre_grad = (act_grad.astype(jnp.float32) * (sig * (1.0 + pre * (1.0 - sig)))).astype(
        jnp.bfloat16
    )
    full_term = lax.dot_general(
        feat_columns, pre_grad, (((0,), (0,)), ((), ())), preferred_element_type=jnp.float32
    )
    summed = lax.psum_scatter(full_term, ("frame", "tile"), scatter_dimension=0, tiled=True)
    weight_grad = summed * grad_scale
    grad_ext = padded_2(
        pre_grad.reshape(slab_frames, tile_rows, width_cells, channels), (("tile", 1),), 1
    )
    grad_columns = tile_columns(grad_ext, tile_rows, width_cells, True)
    local_back = jnp.dot(grad_columns, spatial_back, preferred_element_type=jnp.float32)
    input_grad = (out_grad.reshape(row_count, channels).astype(jnp.float32) + local_back).astype(
        jnp.bfloat16
    )
    input_grad = input_grad.reshape(slab_frames, tile_rows, width_cells, channels)
    return (out_slab, input_grad, weight_grad)


def kernel_call(body, outs, scratch, flops, *args, anywhere=0):
    moved = sum(a.size * a.dtype.itemsize for a in args)
    moved += sum(math.prod(shape) * jnp.dtype(kind).itemsize for shape, kind in outs)
    spaces = [pltpu.VMEM] * (len(args) - anywhere) + [pl.ANY] * anywhere
    return pl.pallas_call(
        body,
        out_shape=tuple(jax.ShapeDtypeStruct(shape, kind) for shape, kind in outs),
        in_specs=[pl.BlockSpec(memory_space=space) for space in spaces],
        out_specs=tuple(pl.BlockSpec(memory_space=pltpu.VMEM) for _ in outs),
        scratch_shapes=[pltpu.VMEM(shape, kind) for shape, kind in scratch],
        compiler_params=pltpu.CompilerParams(vmem_limit_bytes=VMEM_LIMIT),
        cost_estimate=pl.CostEstimate(flops=flops, bytes_accessed=moved, transcendentals=0),
    )(*args)


def shifted(values, width, step):
    rows = values.shape[0]
    at = lax.broadcasted_iota(jnp.int32, values.shape, 0) % width
    moved = pltpu.roll(values, step % rows, 0)
    inside = at >= step if step > 0 else at < width + step
    return jnp.where(inside, moved, 0.0)


def column_shifts(values, width):
    wide = values.astype(jnp.float32)
    return (
        shifted(wide, width, 1).astype(values.dtype),
        values,
        shifted(wide, width, -1).astype(values.dtype),
    )


def with_edges(own, other, ext):
    rows = own.shape[1]
    tile = lax.axis_index("tile")
    ext[:, 1 : rows + 1] = own[...]
    above, below = other[:, rows - 1], other[:, 0]
    ext[:, 0] = jnp.where(tile == 1, above, jnp.zeros_like(above))
    ext[:, rows + 1] = jnp.where(tile == 0, below, jnp.zeros_like(below))


def whole_image(own, other, image):
    rows = own.shape[1]
    tile = lax.axis_index("tile")
    image[:, 0] = jnp.zeros_like(image[:, 0])
    image[:, 2 * rows + 1] = jnp.zeros_like(image[:, 2 * rows + 1])
    image[:, pl.ds(1 + tile * rows, rows)] = own[...]
    image[:, pl.ds(1 + (1 - tile) * rows, rows)] = other[...]


def order_kernel(*refs):
    refs[-1][...] = jnp.zeros_like(refs[-1])


def spatial_kernel(own, weight, other, _, pre_ref, act_ref, image, pre_all):
    frames, rows, width, channels = own.shape
    whole_image(own, other, image)
    shifts = column_shifts(image[...].reshape(-1, channels), width)
    shifts = [piece.reshape(image.shape) for piece in shifts]
    for half in range(2):
        columns = jnp.concatenate(
            [
                shifts[s][:, half * rows + r : half * rows + r + rows].reshape(-1, channels)
                for r in range(3)
                for s in range(3)
            ],
            axis=1,
        )
        pre = jnp.dot(columns, weight[...], preferred_element_type=jnp.float32)
        pre_all[half] = pre
        act_ref[half] = (pre * jax.nn.sigmoid(pre)).astype(jnp.bfloat16)
    pre_ref[...] = pre_all[lax.axis_index("tile")]


def split_kernel(arrived, _, mine_ref, other_ref):
    tile = lax.axis_index("tile")
    mine_ref[...] = arrived[tile]
    other_ref[...] = arrived[1 - tile]


def forward_sum_kernel(partial, arrived, *rest, first):
    sum_ref = rest[-1]
    rows = partial[first : first + sum_ref.shape[0]]
    came = arrived[: sum_ref.shape[0]].astype(jnp.float32)
    sum_ref[...] = (rows + came).astype(sum_ref.dtype)


def last_sum_kernel(keep, near, last_a, last_b, _, out_ref, *, scale):
    half = last_a.shape[0]
    for first, last in ((0, last_a), (half, last_b)):
        total = keep[first : first + half] + near[first : first + half].astype(jnp.float32)
        out_ref[first : first + half] = (total + last[...].astype(jnp.float32)) * scale


def transpose_kernel(own, other, _, out_ref, image):
    frames, rows, width, channels = own.shape
    tile = lax.axis_index("tile")
    whole_image(own, other, image)
    for which, first in enumerate((tile * rows, (1 - tile) * rows)):
        for r in range(3):
            block = image[:, pl.ds(first + r, rows)].reshape(-1, channels)
            out_ref[which, r * channels : (r + 1) * channels] = block.T


def slabs(own, first, second, ext):
    tile = lax.axis_index("tile")
    ext[2 * tile] = first[...]
    ext[1] = own[...]
    ext[2 - 2 * tile] = second[...]
    chip = lax.axis_index("frame")

    @pl.when(chip == 0)
    def _():
        ext[0] = jnp.zeros_like(ext[0])

    @pl.when(chip == lax.axis_size("frame") - 1)
    def _():
        ext[2] = jnp.zeros_like(ext[2])

    return ext[...].reshape(-1, own.shape[1])


def act_grad_kernel(own, first_in, second_in, weight, pre_ref, _, out_ref, ext):
    count, channels = own.shape
    frames = slabs(own, first_in, second_in, ext)
    hop = count // 4
    total = None
    for k in range(9):
        first = (8 - k) * hop
        term = lax.dot_general(
            frames[first : first + count],
            weight[k * channels : (k + 1) * channels],
            (((1,), (1,)), ((), ())),
            preferred_element_type=jnp.float32,
        )
        total = term if total is None else total + term
    act_grad = total.astype(jnp.bfloat16).astype(jnp.float32)
    pre = pre_ref[...]
    sig = jax.nn.sigmoid(pre)
    out_ref[...] = (act_grad * (sig * (1.0 + pre * (1.0 - sig)))).astype(jnp.bfloat16)


def temporal_kernel(feats, act, first_in, second_in, weight, _, out_ref, done_ref, ext):
    count, channels = feats.shape
    own = act.at[lax.axis_index("tile")]
    frames = slabs(own, first_in, second_in, ext)
    hop = count // 4
    columns = jnp.concatenate([frames[k * hop : k * hop + count] for k in range(9)], axis=1)
    mixed = jnp.dot(columns, weight[...], preferred_element_type=jnp.float32)
    out_ref[...] = (feats[...].astype(jnp.float32) + mixed).astype(jnp.bfloat16)
    done_ref[...] = jnp.zeros_like(done_ref)


def own_term_kernel(feats_t, own, total_ref):
    channels = own.shape[3]
    after, same, before = column_shifts(own[...].reshape(-1, channels), own.shape[2])
    left = feats_t[0]
    for s, right in enumerate((before, same, after)):
        total_ref[s] = jnp.dot(left, right, preferred_element_type=jnp.float32)


def kernel_grad_kernel(
    feats_t, other, term, far_a_ref, far_b_ref, pass_ref, near_ref, keep_ref, total
):
    frames, rows, width, channels = other.shape
    tile = lax.axis_index("tile")
    chip = lax.axis_index("frame")
    after, same, before = column_shifts(other[...].reshape(-1, channels), width)
    left = feats_t[1]
    for s, right in enumerate((before, same, after)):
        both = term[s] + jnp.dot(left, right, preferred_element_type=jnp.float32)
        for r in range(3):
            tap = 3 * r + s
            total[tap * channels : (tap + 1) * channels] = both[r * channels : (r + 1) * channels]
    share = keep_ref.shape[0]
    half = share // 2
    for distance, skip, ref in (
        (3, 0, far_a_ref),
        (3, half, far_b_ref),
        (2, 0, pass_ref),
        (1, 0, near_ref),
        (0, 0, keep_ref),
    ):
        first = (2 * (chip ^ distance) + tile) * share + skip
        ref[...] = total[pl.ds(pl.multiple_of(first, 16), ref.shape[0])].astype(ref.dtype)


def input_grad_kernel(out_grad, own, other, weight, _, out_ref, done_ref, ext):
    frames, rows, width, channels = own.shape
    with_edges(own, other, ext)
    after, same, before = column_shifts(ext[...].reshape(-1, channels), width)
    shifts = [piece.reshape(ext.shape) for piece in (before, same, after)]
    total = out_grad[...].astype(jnp.float32)
    for r in range(3):
        for s in range(3):
            tap = 3 * r + s
            total = total + lax.dot_general(
                shifts[s][:, 2 - r : 2 - r + rows].reshape(-1, channels),
                weight[tap * channels : (tap + 1) * channels],
                (((1,), (1,)), ((), ())),
                preferred_element_type=jnp.float32,
            )
    out_ref[...] = total.astype(jnp.bfloat16)
    done_ref[...] = jnp.zeros_like(done_ref)


def per_device_pair(clip_feats, out_grad, spatial_weight, temporal_weight):
    frames, rows, width, channels = clip_feats.shape
    count = frames * rows * width
    chips = lax.axis_size("frame")
    cores = lax.axis_size("tile")
    scale = 1.0 / math.sqrt(frames * chips * rows * cores * width)
    outward = [(2 * z, 2 * z + 2) for z in range(chips - 1)]
    outward += [(2 * z + 3, 2 * z + 1) for z in range(chips - 1)]
    outward += [(2 * chips - 2, 2 * chips - 1), (1, 0)]
    inward = [(target, source) for source, target in outward]
    both = ("frame", "tile")
    swap = [(0, 1), (1, 0)]
    bf16, f32 = jnp.bfloat16, jnp.float32
    product = 2 * count * 9 * channels * channels
    flat = (count, channels)
    ext = ((frames, rows + 2, width, channels), bf16)
    image = ((frames, 2 * rows + 2, width, channels), bf16)
    three = ((3, count, channels), bf16)

    grad_flat = out_grad.reshape(flat)
    feat_flat = clip_feats.reshape(flat)
    grad_first = lax.ppermute(grad_flat, both, outward)
    grad_second = lax.ppermute(grad_flat, both, inward)
    feat_other = lax.ppermute(clip_feats, "tile", swap)

    (first,) = kernel_call(order_kernel, [((8, 128), f32)], [], 2 * product)
    pre, act = kernel_call(
        spatial_kernel,
        [(flat, f32), ((2, *flat), bf16)],
        [image, ((2, *flat), f32)],
        2 * product,
        clip_feats, spatial_weight, feat_other, first, anywhere=1,
    )
    act_in = lax.ppermute(act, both, inward)
    (feats_t,) = kernel_call(
        transpose_kernel,
        [((2, 3 * channels, count), bf16)],
        [image],
        0,
        clip_feats, feat_other, pre, anywhere=1,
    )
    (pre_grad,) = kernel_call(
        act_grad_kernel,
        [(flat, bf16)],
        [three],
        product,
        grad_flat, grad_first, grad_second, temporal_weight, pre, feats_t, anywhere=1,
    )
    pre_grad = pre_grad.reshape(clip_feats.shape)
    pre_other = lax.ppermute(pre_grad, "tile", swap)

    share = (9 * channels // (chips * cores), channels)
    (term,) = kernel_call(
        own_term_kernel,
        [((3, 3 * channels, channels), f32)],
        [],
        product,
        feats_t, pre_grad,
    )
    half = (share[0] // 2, channels)
    far_a, far_b, onward, near, keep = kernel_call(
        kernel_grad_kernel,
        [(half, bf16), (half, bf16), (share, f32), (share, bf16), (share, f32)],
        [((9 * channels, channels), f32)],
        product,
        feats_t, pre_other, term,
    )
    beside = [(z, z ^ 1) for z in range(chips)]
    across = [(z, z ^ 2) for z in range(chips)]
    far_in_a = lax.ppermute(far_a, "frame", beside)
    far_in_b = lax.ppermute(far_b, "frame", beside)
    near_in = lax.ppermute(near, "frame", beside)
    (sum_a,) = kernel_call(
        functools.partial(forward_sum_kernel, first=0),
        [(half, bf16)],
        [],
        4 * product,
        onward, far_in_a, act_in, anywhere=1,
    )
    last_a = lax.ppermute(sum_a, "frame", across)
    (sum_b,) = kernel_call(
        functools.partial(forward_sum_kernel, first=half[0]),
        [(half, bf16)],
        [],
        0,
        onward, far_in_b, sum_a, anywhere=1,
    )
    last_b = lax.ppermute(sum_b, "frame", across)
    act_second, act_pass = kernel_call(
        split_kernel, [(flat, bf16)] * 2, [], 0, act_in, sum_b, anywhere=1
    )
    act_first = lax.ppermute(act_pass, "tile", swap)

    input_grad, done = kernel_call(
        input_grad_kernel,
        [(flat, bf16), ((8, 128), f32)],
        [ext],
        product,
        grad_flat, pre_grad, pre_other, spatial_weight, sum_b, anywhere=1,
    )
    (arrived,) = kernel_call(
        order_kernel, [((8, 128), f32)], [], 20 * product, last_a, near_in, done, anywhere=3
    )
    block_out, done = kernel_call(
        temporal_kernel,
        [(flat, bf16), ((8, 128), f32)],
        [three],
        product,
        feat_flat, act, act_first, act_second, temporal_weight, arrived, anywhere=1,
    )
    (weight_grad,) = kernel_call(
        functools.partial(last_sum_kernel, scale=scale),
        [(share, f32)],
        [],
        0,
        keep, near_in, last_a, last_b, done, anywhere=1,
    )
    return (
        block_out.reshape(clip_feats.shape),
        input_grad.reshape(clip_feats.shape),
        weight_grad,
    )


def per_device(clip_feats, *rest):
    pairs = lax.axis_size("tile") == 2 and lax.axis_size("frame") == 4
    if pairs and clip_feats.shape[0] == 4 * TAP_DILATION:
        return per_device_pair(clip_feats, *rest)
    return per_device_any(clip_feats, *rest)


def solution(mesh):
    return jax.shard_map(
        per_device,
        mesh=mesh,
        in_specs=(
            P(("clip", "frame"), "tile", None, None),
            P(("clip", "frame"), "tile", None, None),
            P(),
            P(),
        ),
        out_specs=(
            P(("clip", "frame"), "tile", None, None),
            P(("clip", "frame"), "tile", None, None),
            P(("clip", "frame", "tile"), None),
        ),
        check_vma=False,
    )
```

```python
import functools
import math

import jax
import jax.numpy as jnp
from jax import lax
from jax.experimental import pallas as pl
from jax.experimental.pallas import tpu as pltpu
from jax.sharding import PartitionSpec as P

TAP_DILATION = 2
VMEM_LIMIT = 32 * 1024 * 1024


def padded_2(block, sides, width):
    for axis, dim in sides:
        count = lax.axis_size(axis)
        forward = [(i, i + 1) for i in range(count - 1)]
        backward = [(target, source) for source, target in forward]
        low = lax.ppermute(
            lax.slice_in_dim(block, block.shape[dim] - width, None, axis=dim), axis, forward
        )
        high = lax.ppermute(lax.slice_in_dim(block, 0, width, axis=dim), axis, backward)
        block = jnp.concatenate([low, block, high], axis=dim)
    return block


def tile_columns(extended, tile_rows, width_cells, backward_pass):
    padded = jnp.pad(extended, ((0, 0), (0, 0), (1, 1), (0, 0)))
    pieces = []
    for row_shift in range(3):
        for col_shift in range(3):
            row_start = 2 - row_shift if backward_pass else row_shift
            col_start = 2 - col_shift if backward_pass else col_shift
            pieces.append(
                padded[:, row_start : row_start + tile_rows, col_start : col_start + width_cells, :]
            )
    channels = extended.shape[3]
    return jnp.concatenate(pieces, axis=-1).reshape(-1, 9 * channels)


def temporal_taps(padded_seq, weight, frame_count, backward_pass):
    pieces = []
    for temporal_tap_index in range(9):
        first_frame_index = (
            (8 - temporal_tap_index) * TAP_DILATION
            if backward_pass
            else temporal_tap_index * TAP_DILATION
        )
        pieces.append(padded_seq[first_frame_index : first_frame_index + frame_count])
    channels = padded_seq.shape[2]
    columns = jnp.concatenate(pieces, axis=-1).reshape(-1, 9 * channels)
    return jnp.dot(columns, weight, preferred_element_type=jnp.float32)


def per_device_any(clip_feats, out_grad, spatial_weight, temporal_weight):
    slab_frames, tile_rows, width_cells, channels = clip_feats.shape
    row_count = slab_frames * tile_rows * width_cells
    frame_devs = lax.axis_size("frame")
    tile_devs = lax.axis_size("tile")
    grad_scale = jnp.float32(
        1.0 / math.sqrt(slab_frames * frame_devs * tile_rows * tile_devs * width_cells)
    )
    spatial_back = (
        spatial_weight.reshape(9, channels, channels)
        .transpose(0, 2, 1)
        .reshape(9 * channels, channels)
    )
    temporal_back = (
        temporal_weight.reshape(9, channels, channels)
        .transpose(0, 2, 1)
        .reshape(9 * channels, channels)
    )
    feat_ext = padded_2(clip_feats, (("tile", 1),), 1)
    feat_columns = tile_columns(feat_ext, tile_rows, width_cells, False)
    pre = jnp.dot(feat_columns, spatial_weight, preferred_element_type=jnp.float32)
    act = jax.nn.silu(pre).astype(jnp.bfloat16)
    temporal_reach = 4 * TAP_DILATION
    per_group = tile_rows * width_cells // frame_devs
    grouped = (slab_frames, frame_devs, per_group, channels)
    act_part = lax.all_to_all(
        act.reshape(grouped), "frame", split_axis=1, concat_axis=0, tiled=True
    )
    grad_part = lax.all_to_all(out_grad, "frame", split_axis=1, concat_axis=0, tiled=True)
    feat_part = lax.all_to_all(clip_feats, "frame", split_axis=1, concat_axis=0, tiled=True)
    frame_count = act_part.shape[0]
    item_count = act_part.shape[2]
    act_pad = jnp.pad(
        act_part.reshape(frame_count, item_count, channels),
        ((temporal_reach, temporal_reach), (0, 0), (0, 0)),
    )
    grad_pad = jnp.pad(
        grad_part.reshape(frame_count, item_count, channels),
        ((temporal_reach, temporal_reach), (0, 0), (0, 0)),
    )
    mixed = temporal_taps(act_pad, temporal_weight, frame_count, False)
    out_part = (feat_part.reshape(-1, channels).astype(jnp.float32) + mixed).astype(jnp.bfloat16)
    back_part = temporal_taps(grad_pad, temporal_back, frame_count, True).astype(jnp.bfloat16)
    out_part = out_part.reshape(frame_count, 1, item_count, channels)
    back_part = back_part.reshape(frame_count, 1, item_count, channels)
    out_slab = lax.all_to_all(out_part, "frame", split_axis=0, concat_axis=1, tiled=True)
    grad_slab = lax.all_to_all(back_part, "frame", split_axis=0, concat_axis=1, tiled=True)
    act_grad = grad_slab.reshape(row_count, channels)
    sig = jax.nn.sigmoid(pre)
    pre_grad = (act_grad.astype(jnp.float32) * (sig * (1.0 + pre * (1.0 - sig)))).astype(
        jnp.bfloat16
    )
    full_term = lax.dot_general(
        feat_columns, pre_grad, (((0,), (0,)), ((), ())), preferred_element_type=jnp.float32
    )
    summed = lax.psum_scatter(full_term, ("frame", "tile"), scatter_dimension=0, tiled=True)
    weight_grad = summed * grad_scale
    grad_ext = padded_2(
        pre_grad.reshape(slab_frames, tile_rows, width_cells, channels), (("tile", 1),), 1
    )
    grad_columns = tile_columns(grad_ext, tile_rows, width_cells, True)
    local_back = jnp.dot(grad_columns, spatial_back, preferred_element_type=jnp.float32)
    input_grad = (out_grad.reshape(row_count, channels).astype(jnp.float32) + local_back).astype(
        jnp.bfloat16
    )
    input_grad = input_grad.reshape(slab_frames, tile_rows, width_cells, channels)
    return (out_slab, input_grad, weight_grad)


def kernel_call(body, outs, scratch, flops, *args, anywhere=0):
    moved = sum(a.size * a.dtype.itemsize for a in args)
    moved += sum(math.prod(shape) * jnp.dtype(kind).itemsize for shape, kind in outs)
    spaces = [pltpu.VMEM] * (len(args) - anywhere) + [pl.ANY] * anywhere
    return pl.pallas_call(
        body,
        out_shape=tuple(jax.ShapeDtypeStruct(shape, kind) for shape, kind in outs),
        in_specs=[pl.BlockSpec(memory_space=space) for space in spaces],
        out_specs=tuple(pl.BlockSpec(memory_space=pltpu.VMEM) for _ in outs),
        scratch_shapes=[pltpu.VMEM(shape, kind) for shape, kind in scratch],
        compiler_params=pltpu.CompilerParams(vmem_limit_bytes=VMEM_LIMIT),
        cost_estimate=pl.CostEstimate(flops=flops, bytes_accessed=moved, transcendentals=0),
    )(*args)


def shifted(values, width, step):
    rows = values.shape[0]
    at = lax.broadcasted_iota(jnp.int32, values.shape, 0) % width
    moved = pltpu.roll(values, step % rows, 0)
    inside = at >= step if step > 0 else at < width + step
    return jnp.where(inside, moved, 0.0)


def column_shifts(values, width):
    wide = values.astype(jnp.float32)
    return (
        shifted(wide, width, 1).astype(values.dtype),
        values,
        shifted(wide, width, -1).astype(values.dtype),
    )


def with_edges(own, other, ext):
    rows = own.shape[1]
    tile = lax.axis_index("tile")
    ext[:, 1 : rows + 1] = own[...]
    above, below = other[:, rows - 1], other[:, 0]
    ext[:, 0] = jnp.where(tile == 1, above, jnp.zeros_like(above))
    ext[:, rows + 1] = jnp.where(tile == 0, below, jnp.zeros_like(below))


def whole_image(own, other, image):
    rows = own.shape[1]
    tile = lax.axis_index("tile")
    image[:, 0] = jnp.zeros_like(image[:, 0])
    image[:, 2 * rows + 1] = jnp.zeros_like(image[:, 2 * rows + 1])
    image[:, pl.ds(1 + tile * rows, rows)] = own[...]
    image[:, pl.ds(1 + (1 - tile) * rows, rows)] = other[...]


def order_kernel(*refs):
    refs[-1][...] = jnp.zeros_like(refs[-1])


def spatial_kernel(own, weight, other, _, pre_ref, act_ref, image, pre_all):
    frames, rows, width, channels = own.shape
    whole_image(own, other, image)
    shifts = column_shifts(image[...].reshape(-1, channels), width)
    shifts = [piece.reshape(image.shape) for piece in shifts]
    for half in range(2):
        columns = jnp.concatenate(
            [
                shifts[s][:, half * rows + r : half * rows + r + rows].reshape(-1, channels)
                for r in range(3)
                for s in range(3)
            ],
            axis=1,
        )
        pre = jnp.dot(columns, weight[...], preferred_element_type=jnp.float32)
        pre_all[half] = pre
        act_ref[half] = (pre * jax.nn.sigmoid(pre)).astype(jnp.bfloat16)
    pre_ref[...] = pre_all[lax.axis_index("tile")]


def split_kernel(arrived, _, mine_ref, other_ref):
    tile = lax.axis_index("tile")
    mine_ref[...] = arrived[tile]
    other_ref[...] = arrived[1 - tile]


def forward_sum_kernel(partial, arrived, *rest, first):
    sum_ref = rest[-1]
    rows = partial[first : first + sum_ref.shape[0]]
    came = arrived[: sum_ref.shape[0]].astype(jnp.float32)
    sum_ref[...] = (rows + came).astype(sum_ref.dtype)


def last_sum_kernel(keep, near, last_a, last_b, _, out_ref, *, scale):
    half = last_a.shape[0]
    for first, last in ((0, last_a), (half, last_b)):
        total = keep[first : first + half] + near[first : first + half].astype(jnp.float32)
        out_ref[first : first + half] = (total + last[...].astype(jnp.float32)) * scale


def transpose_kernel(own, other, _, out_ref, image):
    frames, rows, width, channels = own.shape
    tile = lax.axis_index("tile")
    whole_image(own, other, image)
    for which, first in enumerate((tile * rows, (1 - tile) * rows)):
        for r in range(3):
            block = image[:, pl.ds(first + r, rows)].reshape(-1, channels)
            out_ref[which, r * channels : (r + 1) * channels] = block.T


def slabs(own, first, second, ext):
    tile = lax.axis_index("tile")
    ext[2 * tile] = first[...]
    ext[1] = own[...]
    ext[2 - 2 * tile] = second[...]
    chip = lax.axis_index("frame")

    @pl.when(chip == 0)
    def _():
        ext[0] = jnp.zeros_like(ext[0])

    @pl.when(chip == lax.axis_size("frame") - 1)
    def _():
        ext[2] = jnp.zeros_like(ext[2])

    return ext[...].reshape(-1, own.shape[1])


def act_grad_kernel(own, first_in, second_in, weight, pre_ref, _, out_ref, ext):
    count, channels = own.shape
    frames = slabs(own, first_in, second_in, ext)
    hop = count // 4
    total = None
    for k in range(9):
        first = (8 - k) * hop
        term = lax.dot_general(
            frames[first : first + count],
            weight[k * channels : (k + 1) * channels],
            (((1,), (1,)), ((), ())),
            preferred_element_type=jnp.float32,
        )
        total = term if total is None else total + term
    act_grad = total.astype(jnp.bfloat16).astype(jnp.float32)
    pre = pre_ref[...]
    sig = jax.nn.sigmoid(pre)
    out_ref[...] = (act_grad * (sig * (1.0 + pre * (1.0 - sig)))).astype(jnp.bfloat16)


def temporal_kernel(feats, act, first_in, second_in, weight, _, out_ref, done_ref, ext):
    count, channels = feats.shape
    own = act.at[lax.axis_index("tile")]
    frames = slabs(own, first_in, second_in, ext)
    hop = count // 4
    columns = jnp.concatenate([frames[k * hop : k * hop + count] for k in range(9)], axis=1)
    mixed = jnp.dot(columns, weight[...], preferred_element_type=jnp.float32)
    out_ref[...] = (feats[...].astype(jnp.float32) + mixed).astype(jnp.bfloat16)
    done_ref[...] = jnp.zeros_like(done_ref)


def own_term_kernel(feats_t, own, total_ref):
    channels = own.shape[3]
    after, same, before = column_shifts(own[...].reshape(-1, channels), own.shape[2])
    left = feats_t[0]
    for s, right in enumerate((before, same, after)):
        total_ref[s] = jnp.dot(left, right, preferred_element_type=jnp.float32)


def kernel_grad_kernel(
    feats_t, other, term, far_a_ref, far_b_ref, pass_ref, near_ref, keep_ref, total
):
    frames, rows, width, channels = other.shape
    tile = lax.axis_index("tile")
    chip = lax.axis_index("frame")
    after, same, before = column_shifts(other[...].reshape(-1, channels), width)
    left = feats_t[1]
    for s, right in enumerate((before, same, after)):
        both = term[s] + jnp.dot(left, right, preferred_element_type=jnp.float32)
        for r in range(3):
            tap = 3 * r + s
            total[tap * channels : (tap + 1) * channels] = both[r * channels : (r + 1) * channels]
    share = keep_ref.shape[0]
    half = share // 2
    for distance, skip, ref in (
        (3, 0, far_a_ref),
        (3, half, far_b_ref),
        (2, 0, pass_ref),
        (1, 0, near_ref),
        (0, 0, keep_ref),
    ):
        first = (2 * (chip ^ distance) + tile) * share + skip
        ref[...] = total[pl.ds(pl.multiple_of(first, 16), ref.shape[0])].astype(ref.dtype)


def input_grad_kernel(out_grad, own, other, weight, _, out_ref, done_ref, ext):
    frames, rows, width, channels = own.shape
    with_edges(own, other, ext)
    after, same, before = column_shifts(ext[...].reshape(-1, channels), width)
    shifts = [piece.reshape(ext.shape) for piece in (before, same, after)]
    total = out_grad[...].astype(jnp.float32)
    for r in range(3):
        for s in range(3):
            tap = 3 * r + s
            total = total + lax.dot_general(
                shifts[s][:, 2 - r : 2 - r + rows].reshape(-1, channels),
                weight[tap * channels : (tap + 1) * channels],
                (((1,), (1,)), ((), ())),
                preferred_element_type=jnp.float32,
            )
    out_ref[...] = total.astype(jnp.bfloat16)
    done_ref[...] = jnp.zeros_like(done_ref)


def per_device_pair(clip_feats, out_grad, spatial_weight, temporal_weight):
    frames, rows, width, channels = clip_feats.shape
    count = frames * rows * width
    chips = lax.axis_size("frame")
    cores = lax.axis_size("tile")
    scale = 1.0 / math.sqrt(frames * chips * rows * cores * width)
    outward = [(2 * z, 2 * z + 2) for z in range(chips - 1)]
    outward += [(2 * z + 3, 2 * z + 1) for z in range(chips - 1)]
    outward += [(2 * chips - 2, 2 * chips - 1), (1, 0)]
    inward = [(target, source) for source, target in outward]
    both = ("frame", "tile")
    swap = [(0, 1), (1, 0)]
    bf16, f32 = jnp.bfloat16, jnp.float32
    product = 2 * count * 9 * channels * channels
    flat = (count, channels)
    ext = ((frames, rows + 2, width, channels), bf16)
    image = ((frames, 2 * rows + 2, width, channels), bf16)
    three = ((3, count, channels), bf16)

    grad_flat = out_grad.reshape(flat)
    feat_flat = clip_feats.reshape(flat)
    grad_first = lax.ppermute(grad_flat, both, outward)
    grad_second = lax.ppermute(grad_flat, both, inward)
    feat_other = lax.ppermute(clip_feats, "tile", swap)

    (first,) = kernel_call(order_kernel, [((8, 128), f32)], [], 5 * product)
    pre, act = kernel_call(
        spatial_kernel,
        [(flat, f32), ((2, *flat), bf16)],
        [image, ((2, *flat), f32)],
        2 * product,
        clip_feats, spatial_weight, feat_other, first, anywhere=1,
    )
    act_in = lax.ppermute(act, both, inward)
    (feats_t,) = kernel_call(
        transpose_kernel,
        [((2, 3 * channels, count), bf16)],
        [image],
        0,
        clip_feats, feat_other, pre, anywhere=1,
    )
    (pre_grad,) = kernel_call(
        act_grad_kernel,
        [(flat, bf16)],
        [three],
        product,
        grad_flat, grad_first, grad_second, temporal_weight, pre, feats_t, anywhere=1,
    )
    pre_grad = pre_grad.reshape(clip_feats.shape)
    pre_other = lax.ppermute(pre_grad, "tile", swap)

    share = (9 * channels // (chips * cores), channels)
    (term,) = kernel_call(
        own_term_kernel,
        [((3, 3 * channels, channels), f32)],
        [],
        product,
        feats_t, pre_grad,
    )
    half = (share[0] // 2, channels)
    far_a, far_b, onward, near, keep = kernel_call(
        kernel_grad_kernel,
        [(half, bf16), (half, bf16), (share, f32), (share, bf16), (share, f32)],
        [((9 * channels, channels), f32)],
        product,
        feats_t, pre_other, term,
    )
    beside = [(z, z ^ 1) for z in range(chips)]
    across = [(z, z ^ 2) for z in range(chips)]
    far_in_a = lax.ppermute(far_a, "frame", beside)
    far_in_b = lax.ppermute(far_b, "frame", beside)
    near_in = lax.ppermute(near, "frame", beside)
    (sum_a,) = kernel_call(
        functools.partial(forward_sum_kernel, first=0),
        [(half, bf16)],
        [],
        4 * product,
        onward, far_in_a, act_in, anywhere=1,
    )
    last_a = lax.ppermute(sum_a, "frame", across)
    (sum_b,) = kernel_call(
        functools.partial(forward_sum_kernel, first=half[0]),
        [(half, bf16)],
        [],
        0,
        onward, far_in_b, sum_a, anywhere=1,
    )
    last_b = lax.ppermute(sum_b, "frame", across)
    act_second, act_pass = kernel_call(
        split_kernel, [(flat, bf16)] * 2, [], 0, act_in, sum_b, anywhere=1
    )
    act_first = lax.ppermute(act_pass, "tile", swap)

    input_grad, done = kernel_call(
        input_grad_kernel,
        [(flat, bf16), ((8, 128), f32)],
        [ext],
        product,
        grad_flat, pre_grad, pre_other, spatial_weight, sum_b, anywhere=1,
    )
    (arrived,) = kernel_call(
        order_kernel, [((8, 128), f32)], [], 20 * product, last_a, near_in, done, anywhere=3
    )
    block_out, done = kernel_call(
        temporal_kernel,
        [(flat, bf16), ((8, 128), f32)],
        [three],
        product,
        feat_flat, act, act_first, act_second, temporal_weight, arrived, anywhere=1,
    )
    (weight_grad,) = kernel_call(
        functools.partial(last_sum_kernel, scale=scale),
        [(share, f32)],
        [],
        0,
        keep, near_in, last_a, last_b, done, anywhere=1,
    )
    return (
        block_out.reshape(clip_feats.shape),
        input_grad.reshape(clip_feats.shape),
        weight_grad,
    )


def per_device(clip_feats, *rest):
    pairs = lax.axis_size("tile") == 2 and lax.axis_size("frame") == 4
    if pairs and clip_feats.shape[0] == 4 * TAP_DILATION:
        return per_device_pair(clip_feats, *rest)
    return per_device_any(clip_feats, *rest)


def solution(mesh):
    return jax.shard_map(
        per_device,
        mesh=mesh,
        in_specs=(
            P(("clip", "frame"), "tile", None, None),
            P(("clip", "frame"), "tile", None, None),
            P(),
            P(),
        ),
        out_specs=(
            P(("clip", "frame"), "tile", None, None),
            P(("clip", "frame"), "tile", None, None),
            P(("clip", "frame", "tile"), None),
        ),
        check_vma=False,
    )
```

```python
import functools
import math

import jax
import jax.numpy as jnp
from jax import lax
from jax.experimental import pallas as pl
from jax.experimental.pallas import tpu as pltpu
from jax.sharding import PartitionSpec as P

TAP_DILATION = 2
VMEM_LIMIT = 32 * 1024 * 1024


def padded_2(block, sides, width):
    for axis, dim in sides:
        count = lax.axis_size(axis)
        forward = [(i, i + 1) for i in range(count - 1)]
        backward = [(target, source) for source, target in forward]
        low = lax.ppermute(
            lax.slice_in_dim(block, block.shape[dim] - width, None, axis=dim), axis, forward
        )
        high = lax.ppermute(lax.slice_in_dim(block, 0, width, axis=dim), axis, backward)
        block = jnp.concatenate([low, block, high], axis=dim)
    return block


def tile_columns(extended, tile_rows, width_cells, backward_pass):
    padded = jnp.pad(extended, ((0, 0), (0, 0), (1, 1), (0, 0)))
    pieces = []
    for row_shift in range(3):
        for col_shift in range(3):
            row_start = 2 - row_shift if backward_pass else row_shift
            col_start = 2 - col_shift if backward_pass else col_shift
            pieces.append(
                padded[:, row_start : row_start + tile_rows, col_start : col_start + width_cells, :]
            )
    channels = extended.shape[3]
    return jnp.concatenate(pieces, axis=-1).reshape(-1, 9 * channels)


def temporal_taps(padded_seq, weight, frame_count, backward_pass):
    pieces = []
    for temporal_tap_index in range(9):
        first_frame_index = (
            (8 - temporal_tap_index) * TAP_DILATION
            if backward_pass
            else temporal_tap_index * TAP_DILATION
        )
        pieces.append(padded_seq[first_frame_index : first_frame_index + frame_count])
    channels = padded_seq.shape[2]
    columns = jnp.concatenate(pieces, axis=-1).reshape(-1, 9 * channels)
    return jnp.dot(columns, weight, preferred_element_type=jnp.float32)


def per_device_any(clip_feats, out_grad, spatial_weight, temporal_weight):
    slab_frames, tile_rows, width_cells, channels = clip_feats.shape
    row_count = slab_frames * tile_rows * width_cells
    frame_devs = lax.axis_size("frame")
    tile_devs = lax.axis_size("tile")
    grad_scale = jnp.float32(
        1.0 / math.sqrt(slab_frames * frame_devs * tile_rows * tile_devs * width_cells)
    )
    spatial_back = (
        spatial_weight.reshape(9, channels, channels)
        .transpose(0, 2, 1)
        .reshape(9 * channels, channels)
    )
    temporal_back = (
        temporal_weight.reshape(9, channels, channels)
        .transpose(0, 2, 1)
        .reshape(9 * channels, channels)
    )
    feat_ext = padded_2(clip_feats, (("tile", 1),), 1)
    feat_columns = tile_columns(feat_ext, tile_rows, width_cells, False)
    pre = jnp.dot(feat_columns, spatial_weight, preferred_element_type=jnp.float32)
    act = jax.nn.silu(pre).astype(jnp.bfloat16)
    temporal_reach = 4 * TAP_DILATION
    per_group = tile_rows * width_cells // frame_devs
    grouped = (slab_frames, frame_devs, per_group, channels)
    act_part = lax.all_to_all(
        act.reshape(grouped), "frame", split_axis=1, concat_axis=0, tiled=True
    )
    grad_part = lax.all_to_all(out_grad, "frame", split_axis=1, concat_axis=0, tiled=True)
    feat_part = lax.all_to_all(clip_feats, "frame", split_axis=1, concat_axis=0, tiled=True)
    frame_count = act_part.shape[0]
    item_count = act_part.shape[2]
    act_pad = jnp.pad(
        act_part.reshape(frame_count, item_count, channels),
        ((temporal_reach, temporal_reach), (0, 0), (0, 0)),
    )
    grad_pad = jnp.pad(
        grad_part.reshape(frame_count, item_count, channels),
        ((temporal_reach, temporal_reach), (0, 0), (0, 0)),
    )
    mixed = temporal_taps(act_pad, temporal_weight, frame_count, False)
    out_part = (feat_part.reshape(-1, channels).astype(jnp.float32) + mixed).astype(jnp.bfloat16)
    back_part = temporal_taps(grad_pad, temporal_back, frame_count, True).astype(jnp.bfloat16)
    out_part = out_part.reshape(frame_count, 1, item_count, channels)
    back_part = back_part.reshape(frame_count, 1, item_count, channels)
    out_slab = lax.all_to_all(out_part, "frame", split_axis=0, concat_axis=1, tiled=True)
    grad_slab = lax.all_to_all(back_part, "frame", split_axis=0, concat_axis=1, tiled=True)
    act_grad = grad_slab.reshape(row_count, channels)
    sig = jax.nn.sigmoid(pre)
    pre_grad = (act_grad.astype(jnp.float32) * (sig * (1.0 + pre * (1.0 - sig)))).astype(
        jnp.bfloat16
    )
    full_term = lax.dot_general(
        feat_columns, pre_grad, (((0,), (0,)), ((), ())), preferred_element_type=jnp.float32
    )
    summed = lax.psum_scatter(full_term, ("frame", "tile"), scatter_dimension=0, tiled=True)
    weight_grad = summed * grad_scale
    grad_ext = padded_2(
        pre_grad.reshape(slab_frames, tile_rows, width_cells, channels), (("tile", 1),), 1
    )
    grad_columns = tile_columns(grad_ext, tile_rows, width_cells, True)
    local_back = jnp.dot(grad_columns, spatial_back, preferred_element_type=jnp.float32)
    input_grad = (out_grad.reshape(row_count, channels).astype(jnp.float32) + local_back).astype(
        jnp.bfloat16
    )
    input_grad = input_grad.reshape(slab_frames, tile_rows, width_cells, channels)
    return (out_slab, input_grad, weight_grad)


def kernel_call(body, outs, scratch, flops, *args, anywhere=0):
    moved = sum(a.size * a.dtype.itemsize for a in args)
    moved += sum(math.prod(shape) * jnp.dtype(kind).itemsize for shape, kind in outs)
    spaces = [pltpu.VMEM] * (len(args) - anywhere) + [pl.ANY] * anywhere
    return pl.pallas_call(
        body,
        out_shape=tuple(jax.ShapeDtypeStruct(shape, kind) for shape, kind in outs),
        in_specs=[pl.BlockSpec(memory_space=space) for space in spaces],
        out_specs=tuple(pl.BlockSpec(memory_space=pltpu.VMEM) for _ in outs),
        scratch_shapes=[pltpu.VMEM(shape, kind) for shape, kind in scratch],
        compiler_params=pltpu.CompilerParams(vmem_limit_bytes=VMEM_LIMIT),
        cost_estimate=pl.CostEstimate(flops=flops, bytes_accessed=moved, transcendentals=0),
    )(*args)


def shifted(values, width, step):
    rows = values.shape[0]
    at = lax.broadcasted_iota(jnp.int32, values.shape, 0) % width
    moved = pltpu.roll(values, step % rows, 0)
    inside = at >= step if step > 0 else at < width + step
    return jnp.where(inside, moved, 0.0)


def column_shifts(values, width):
    wide = values.astype(jnp.float32)
    return (
        shifted(wide, width, 1).astype(values.dtype),
        values,
        shifted(wide, width, -1).astype(values.dtype),
    )


def with_edges(own, other, ext):
    rows = own.shape[1]
    tile = lax.axis_index("tile")
    ext[:, 1 : rows + 1] = own[...]
    above, below = other[:, rows - 1], other[:, 0]
    ext[:, 0] = jnp.where(tile == 1, above, jnp.zeros_like(above))
    ext[:, rows + 1] = jnp.where(tile == 0, below, jnp.zeros_like(below))


def whole_image(own, other, image):
    rows = own.shape[1]
    tile = lax.axis_index("tile")
    image[:, 0] = jnp.zeros_like(image[:, 0])
    image[:, 2 * rows + 1] = jnp.zeros_like(image[:, 2 * rows + 1])
    image[:, pl.ds(1 + tile * rows, rows)] = own[...]
    image[:, pl.ds(1 + (1 - tile) * rows, rows)] = other[...]


def order_kernel(*refs):
    refs[-1][...] = jnp.zeros_like(refs[-1])


def spatial_kernel(own, weight, other, _, pre_ref, act_ref, image, pre_all):
    frames, rows, width, channels = own.shape
    whole_image(own, other, image)
    shifts = column_shifts(image[...].reshape(-1, channels), width)
    shifts = [piece.reshape(image.shape) for piece in shifts]
    for half in range(2):
        columns = jnp.concatenate(
            [
                shifts[s][:, half * rows + r : half * rows + r + rows].reshape(-1, channels)
                for r in range(3)
                for s in range(3)
            ],
            axis=1,
        )
        pre = jnp.dot(columns, weight[...], preferred_element_type=jnp.float32)
        pre_all[half] = pre
        act_ref[half] = (pre * jax.nn.sigmoid(pre)).astype(jnp.bfloat16)
    pre_ref[...] = pre_all[lax.axis_index("tile")]


def split_kernel(arrived, _, mine_ref, other_ref):
    tile = lax.axis_index("tile")
    mine_ref[...] = arrived[tile]
    other_ref[...] = arrived[1 - tile]


def forward_sum_kernel(partial, arrived, *rest, first):
    sum_ref = rest[-1]
    rows = partial[first : first + sum_ref.shape[0]]
    came = arrived[: sum_ref.shape[0]].astype(jnp.float32)
    sum_ref[...] = (rows + came).astype(sum_ref.dtype)


def last_sum_kernel(keep, near, last_a, last_b, _, out_ref, *, scale):
    half = last_a.shape[0]
    for first, last in ((0, last_a), (half, last_b)):
        total = keep[first : first + half] + near[first : first + half].astype(jnp.float32)
        out_ref[first : first + half] = (total + last[...].astype(jnp.float32)) * scale


def transpose_kernel(own, other, _, out_ref, image):
    frames, rows, width, channels = own.shape
    tile = lax.axis_index("tile")
    whole_image(own, other, image)
    for which, first in enumerate((tile * rows, (1 - tile) * rows)):
        for r in range(3):
            block = image[:, pl.ds(first + r, rows)].reshape(-1, channels)
            out_ref[which, r * channels : (r + 1) * channels] = block.T


def slabs(own, first, second, ext):
    tile = lax.axis_index("tile")
    ext[2 * tile] = first[...]
    ext[1] = own[...]
    ext[2 - 2 * tile] = second[...]
    chip = lax.axis_index("frame")

    @pl.when(chip == 0)
    def _():
        ext[0] = jnp.zeros_like(ext[0])

    @pl.when(chip == lax.axis_size("frame") - 1)
    def _():
        ext[2] = jnp.zeros_like(ext[2])

    return ext[...].reshape(-1, own.shape[1])


def act_grad_kernel(own, first_in, second_in, weight, pre_ref, _, out_ref, ext):
    count, channels = own.shape
    frames = slabs(own, first_in, second_in, ext)
    hop = count // 4
    total = None
    for k in range(9):
        first = (8 - k) * hop
        term = lax.dot_general(
            frames[first : first + count],
            weight[k * channels : (k + 1) * channels],
            (((1,), (1,)), ((), ())),
            preferred_element_type=jnp.float32,
        )
        total = term if total is None else total + term
    act_grad = total.astype(jnp.bfloat16).astype(jnp.float32)
    pre = pre_ref[...]
    sig = jax.nn.sigmoid(pre)
    out_ref[...] = (act_grad * (sig * (1.0 + pre * (1.0 - sig)))).astype(jnp.bfloat16)


def temporal_kernel(feats, act, first_in, second_in, weight, _, out_ref, done_ref, ext):
    count, channels = feats.shape
    own = act.at[lax.axis_index("tile")]
    frames = slabs(own, first_in, second_in, ext)
    hop = count // 4
    columns = jnp.concatenate([frames[k * hop : k * hop + count] for k in range(9)], axis=1)
    mixed = jnp.dot(columns, weight[...], preferred_element_type=jnp.float32)
    out_ref[...] = (feats[...].astype(jnp.float32) + mixed).astype(jnp.bfloat16)
    done_ref[...] = jnp.zeros_like(done_ref)


def own_term_kernel(feats_t, own, total_ref):
    channels = own.shape[3]
    after, same, before = column_shifts(own[...].reshape(-1, channels), own.shape[2])
    left = feats_t[0]
    for s, right in enumerate((before, same, after)):
        total_ref[s] = jnp.dot(left, right, preferred_element_type=jnp.float32)


def kernel_grad_kernel(
    feats_t, other, term, far_a_ref, far_b_ref, pass_ref, near_ref, keep_ref, total
):
    frames, rows, width, channels = other.shape
    tile = lax.axis_index("tile")
    chip = lax.axis_index("frame")
    after, same, before = column_shifts(other[...].reshape(-1, channels), width)
    left = feats_t[1]
    for s, right in enumerate((before, same, after)):
        both = term[s] + jnp.dot(left, right, preferred_element_type=jnp.float32)
        for r in range(3):
            tap = 3 * r + s
            total[tap * channels : (tap + 1) * channels] = both[r * channels : (r + 1) * channels]
    share = keep_ref.shape[0]
    half = share // 2
    for distance, skip, ref in (
        (2, 0, far_a_ref),
        (2, half, far_b_ref),
        (3, 0, pass_ref),
        (1, 0, near_ref),
        (0, 0, keep_ref),
    ):
        first = (2 * (chip ^ distance) + tile) * share + skip
        ref[...] = total[pl.ds(pl.multiple_of(first, 16), ref.shape[0])].astype(ref.dtype)


def input_grad_kernel(out_grad, own, other, weight, _, out_ref, done_ref, ext):
    frames, rows, width, channels = own.shape
    with_edges(own, other, ext)
    after, same, before = column_shifts(ext[...].reshape(-1, channels), width)
    shifts = [piece.reshape(ext.shape) for piece in (before, same, after)]
    total = out_grad[...].astype(jnp.float32)
    for r in range(3):
        for s in range(3):
            tap = 3 * r + s
            total = total + lax.dot_general(
                shifts[s][:, 2 - r : 2 - r + rows].reshape(-1, channels),
                weight[tap * channels : (tap + 1) * channels],
                (((1,), (1,)), ((), ())),
                preferred_element_type=jnp.float32,
            )
    out_ref[...] = total.astype(jnp.bfloat16)
    done_ref[...] = jnp.zeros_like(done_ref)


def per_device_pair(clip_feats, out_grad, spatial_weight, temporal_weight):
    frames, rows, width, channels = clip_feats.shape
    count = frames * rows * width
    chips = lax.axis_size("frame")
    cores = lax.axis_size("tile")
    scale = 1.0 / math.sqrt(frames * chips * rows * cores * width)
    outward = [(2 * z, 2 * z + 2) for z in range(chips - 1)]
    outward += [(2 * z + 3, 2 * z + 1) for z in range(chips - 1)]
    outward += [(2 * chips - 2, 2 * chips - 1), (1, 0)]
    inward = [(target, source) for source, target in outward]
    both = ("frame", "tile")
    swap = [(0, 1), (1, 0)]
    bf16, f32 = jnp.bfloat16, jnp.float32
    product = 2 * count * 9 * channels * channels
    flat = (count, channels)
    ext = ((frames, rows + 2, width, channels), bf16)
    image = ((frames, 2 * rows + 2, width, channels), bf16)
    three = ((3, count, channels), bf16)

    grad_flat = out_grad.reshape(flat)
    feat_flat = clip_feats.reshape(flat)
    grad_first = lax.ppermute(grad_flat, both, outward)
    grad_second = lax.ppermute(grad_flat, both, inward)
    feat_other = lax.ppermute(clip_feats, "tile", swap)

    (first,) = kernel_call(order_kernel, [((8, 128), f32)], [], 5 * product)
    pre, act = kernel_call(
        spatial_kernel,
        [(flat, f32), ((2, *flat), bf16)],
        [image, ((2, *flat), f32)],
        2 * product,
        clip_feats, spatial_weight, feat_other, first, anywhere=1,
    )
    act_in = lax.ppermute(act, both, inward)
    (feats_t,) = kernel_call(
        transpose_kernel,
        [((2, 3 * channels, count), bf16)],
        [image],
        0,
        clip_feats, feat_other, pre, anywhere=1,
    )
    (pre_grad,) = kernel_call(
        act_grad_kernel,
        [(flat, bf16)],
        [three],
        product,
        grad_flat, grad_first, grad_second, temporal_weight, pre, feats_t, anywhere=1,
    )
    pre_grad = pre_grad.reshape(clip_feats.shape)
    pre_other = lax.ppermute(pre_grad, "tile", swap)

    share = (9 * channels // (chips * cores), channels)
    (term,) = kernel_call(
        own_term_kernel,
        [((3, 3 * channels, channels), f32)],
        [],
        product,
        feats_t, pre_grad,
    )
    half = (share[0] // 2, channels)
    far_a, far_b, onward, near, keep = kernel_call(
        kernel_grad_kernel,
        [(half, bf16), (half, bf16), (share, f32), (share, bf16), (share, f32)],
        [((9 * channels, channels), f32)],
        product,
        feats_t, pre_other, term,
    )
    beside = [(z, z ^ 1) for z in range(chips)]
    across = [(z, z ^ 3) for z in range(chips)]
    far_in_a = lax.ppermute(far_a, "frame", beside)
    far_in_b = lax.ppermute(far_b, "frame", beside)
    near_in = lax.ppermute(near, "frame", beside)
    (sum_a,) = kernel_call(
        functools.partial(forward_sum_kernel, first=0),
        [(half, bf16)],
        [],
        4 * product,
        onward, far_in_a, act_in, anywhere=1,
    )
    last_a = lax.ppermute(sum_a, "frame", across)
    (sum_b,) = kernel_call(
        functools.partial(forward_sum_kernel, first=half[0]),
        [(half, bf16)],
        [],
        0,
        onward, far_in_b, sum_a, anywhere=1,
    )
    last_b = lax.ppermute(sum_b, "frame", across)
    act_second, act_pass = kernel_call(
        split_kernel, [(flat, bf16)] * 2, [], 0, act_in, sum_b, anywhere=1
    )
    act_first = lax.ppermute(act_pass, "tile", swap)

    input_grad, done = kernel_call(
        input_grad_kernel,
        [(flat, bf16), ((8, 128), f32)],
        [ext],
        product,
        grad_flat, pre_grad, pre_other, spatial_weight, sum_b, anywhere=1,
    )
    (arrived,) = kernel_call(
        order_kernel, [((8, 128), f32)], [], 20 * product, last_a, near_in, done, anywhere=3
    )
    block_out, done = kernel_call(
        temporal_kernel,
        [(flat, bf16), ((8, 128), f32)],
        [three],
        product,
        feat_flat, act, act_first, act_second, temporal_weight, arrived, anywhere=1,
    )
    (weight_grad,) = kernel_call(
        functools.partial(last_sum_kernel, scale=scale),
        [(share, f32)],
        [],
        0,
        keep, near_in, last_a, last_b, done, anywhere=1,
    )
    return (
        block_out.reshape(clip_feats.shape),
        input_grad.reshape(clip_feats.shape),
        weight_grad,
    )


def per_device(clip_feats, *rest):
    pairs = lax.axis_size("tile") == 2 and lax.axis_size("frame") == 4
    if pairs and clip_feats.shape[0] == 4 * TAP_DILATION:
        return per_device_pair(clip_feats, *rest)
    return per_device_any(clip_feats, *rest)


def solution(mesh):
    return jax.shard_map(
        per_device,
        mesh=mesh,
        in_specs=(
            P(("clip", "frame"), "tile", None, None),
            P(("clip", "frame"), "tile", None, None),
            P(),
            P(),
        ),
        out_specs=(
            P(("clip", "frame"), "tile", None, None),
            P(("clip", "frame"), "tile", None, None),
            P(("clip", "frame", "tile"), None),
        ),
        check_vma=False,
    )
```

```python
import functools
import math

import jax
import jax.numpy as jnp
from jax import lax
from jax.experimental import pallas as pl
from jax.experimental.pallas import tpu as pltpu
from jax.sharding import PartitionSpec as P

TAP_DILATION = 2
VMEM_LIMIT = 32 * 1024 * 1024


def padded_2(block, sides, width):
    for axis, dim in sides:
        count = lax.axis_size(axis)
        forward = [(i, i + 1) for i in range(count - 1)]
        backward = [(target, source) for source, target in forward]
        low = lax.ppermute(
            lax.slice_in_dim(block, block.shape[dim] - width, None, axis=dim), axis, forward
        )
        high = lax.ppermute(lax.slice_in_dim(block, 0, width, axis=dim), axis, backward)
        block = jnp.concatenate([low, block, high], axis=dim)
    return block


def tile_columns(extended, tile_rows, width_cells, backward_pass):
    padded = jnp.pad(extended, ((0, 0), (0, 0), (1, 1), (0, 0)))
    pieces = []
    for row_shift in range(3):
        for col_shift in range(3):
            row_start = 2 - row_shift if backward_pass else row_shift
            col_start = 2 - col_shift if backward_pass else col_shift
            pieces.append(
                padded[:, row_start : row_start + tile_rows, col_start : col_start + width_cells, :]
            )
    channels = extended.shape[3]
    return jnp.concatenate(pieces, axis=-1).reshape(-1, 9 * channels)


def temporal_taps(padded_seq, weight, frame_count, backward_pass):
    pieces = []
    for temporal_tap_index in range(9):
        first_frame_index = (
            (8 - temporal_tap_index) * TAP_DILATION
            if backward_pass
            else temporal_tap_index * TAP_DILATION
        )
        pieces.append(padded_seq[first_frame_index : first_frame_index + frame_count])
    channels = padded_seq.shape[2]
    columns = jnp.concatenate(pieces, axis=-1).reshape(-1, 9 * channels)
    return jnp.dot(columns, weight, preferred_element_type=jnp.float32)


def per_device_any(clip_feats, out_grad, spatial_weight, temporal_weight):
    slab_frames, tile_rows, width_cells, channels = clip_feats.shape
    row_count = slab_frames * tile_rows * width_cells
    frame_devs = lax.axis_size("frame")
    tile_devs = lax.axis_size("tile")
    grad_scale = jnp.float32(
        1.0 / math.sqrt(slab_frames * frame_devs * tile_rows * tile_devs * width_cells)
    )
    spatial_back = (
        spatial_weight.reshape(9, channels, channels)
        .transpose(0, 2, 1)
        .reshape(9 * channels, channels)
    )
    temporal_back = (
        temporal_weight.reshape(9, channels, channels)
        .transpose(0, 2, 1)
        .reshape(9 * channels, channels)
    )
    feat_ext = padded_2(clip_feats, (("tile", 1),), 1)
    feat_columns = tile_columns(feat_ext, tile_rows, width_cells, False)
    pre = jnp.dot(feat_columns, spatial_weight, preferred_element_type=jnp.float32)
    act = jax.nn.silu(pre).astype(jnp.bfloat16)
    temporal_reach = 4 * TAP_DILATION
    per_group = tile_rows * width_cells // frame_devs
    grouped = (slab_frames, frame_devs, per_group, channels)
    act_part = lax.all_to_all(
        act.reshape(grouped), "frame", split_axis=1, concat_axis=0, tiled=True
    )
    grad_part = lax.all_to_all(out_grad, "frame", split_axis=1, concat_axis=0, tiled=True)
    feat_part = lax.all_to_all(clip_feats, "frame", split_axis=1, concat_axis=0, tiled=True)
    frame_count = act_part.shape[0]
    item_count = act_part.shape[2]
    act_pad = jnp.pad(
        act_part.reshape(frame_count, item_count, channels),
        ((temporal_reach, temporal_reach), (0, 0), (0, 0)),
    )
    grad_pad = jnp.pad(
        grad_part.reshape(frame_count, item_count, channels),
        ((temporal_reach, temporal_reach), (0, 0), (0, 0)),
    )
    mixed = temporal_taps(act_pad, temporal_weight, frame_count, False)
    out_part = (feat_part.reshape(-1, channels).astype(jnp.float32) + mixed).astype(jnp.bfloat16)
    back_part = temporal_taps(grad_pad, temporal_back, frame_count, True).astype(jnp.bfloat16)
    out_part = out_part.reshape(frame_count, 1, item_count, channels)
    back_part = back_part.reshape(frame_count, 1, item_count, channels)
    out_slab = lax.all_to_all(out_part, "frame", split_axis=0, concat_axis=1, tiled=True)
    grad_slab = lax.all_to_all(back_part, "frame", split_axis=0, concat_axis=1, tiled=True)
    act_grad = grad_slab.reshape(row_count, channels)
    sig = jax.nn.sigmoid(pre)
    pre_grad = (act_grad.astype(jnp.float32) * (sig * (1.0 + pre * (1.0 - sig)))).astype(
        jnp.bfloat16
    )
    full_term = lax.dot_general(
        feat_columns, pre_grad, (((0,), (0,)), ((), ())), preferred_element_type=jnp.float32
    )
    summed = lax.psum_scatter(full_term, ("frame", "tile"), scatter_dimension=0, tiled=True)
    weight_grad = summed * grad_scale
    grad_ext = padded_2(
        pre_grad.reshape(slab_frames, tile_rows, width_cells, channels), (("tile", 1),), 1
    )
    grad_columns = tile_columns(grad_ext, tile_rows, width_cells, True)
    local_back = jnp.dot(grad_columns, spatial_back, preferred_element_type=jnp.float32)
    input_grad = (out_grad.reshape(row_count, channels).astype(jnp.float32) + local_back).astype(
        jnp.bfloat16
    )
    input_grad = input_grad.reshape(slab_frames, tile_rows, width_cells, channels)
    return (out_slab, input_grad, weight_grad)


def kernel_call(body, outs, scratch, flops, *args, anywhere=0):
    moved = sum(a.size * a.dtype.itemsize for a in args)
    moved += sum(math.prod(shape) * jnp.dtype(kind).itemsize for shape, kind in outs)
    spaces = [pltpu.VMEM] * (len(args) - anywhere) + [pl.ANY] * anywhere
    return pl.pallas_call(
        body,
        out_shape=tuple(jax.ShapeDtypeStruct(shape, kind) for shape, kind in outs),
        in_specs=[pl.BlockSpec(memory_space=space) for space in spaces],
        out_specs=tuple(pl.BlockSpec(memory_space=pltpu.VMEM) for _ in outs),
        scratch_shapes=[pltpu.VMEM(shape, kind) for shape, kind in scratch],
        compiler_params=pltpu.CompilerParams(vmem_limit_bytes=VMEM_LIMIT),
        cost_estimate=pl.CostEstimate(flops=flops, bytes_accessed=moved, transcendentals=0),
    )(*args)


def shifted(values, width, step):
    rows = values.shape[0]
    at = lax.broadcasted_iota(jnp.int32, values.shape, 0) % width
    moved = pltpu.roll(values, step % rows, 0)
    inside = at >= step if step > 0 else at < width + step
    return jnp.where(inside, moved, 0.0)


def column_shifts(values, width):
    wide = values.astype(jnp.float32)
    return (
        shifted(wide, width, 1).astype(values.dtype),
        values,
        shifted(wide, width, -1).astype(values.dtype),
    )


def with_edges(own, other, ext):
    rows = own.shape[1]
    tile = lax.axis_index("tile")
    ext[:, 1 : rows + 1] = own[...]
    above, below = other[:, rows - 1], other[:, 0]
    ext[:, 0] = jnp.where(tile == 1, above, jnp.zeros_like(above))
    ext[:, rows + 1] = jnp.where(tile == 0, below, jnp.zeros_like(below))


def whole_image(own, other, image):
    rows = own.shape[1]
    tile = lax.axis_index("tile")
    image[:, 0] = jnp.zeros_like(image[:, 0])
    image[:, 2 * rows + 1] = jnp.zeros_like(image[:, 2 * rows + 1])
    image[:, pl.ds(1 + tile * rows, rows)] = own[...]
    image[:, pl.ds(1 + (1 - tile) * rows, rows)] = other[...]


def order_kernel(*refs):
    refs[-1][...] = jnp.zeros_like(refs[-1])


def spatial_kernel(own, weight, other, _, pre_ref, act_ref, image, pre_all):
    frames, rows, width, channels = own.shape
    whole_image(own, other, image)
    shifts = column_shifts(image[...].reshape(-1, channels), width)
    shifts = [piece.reshape(image.shape) for piece in shifts]
    for half in range(2):
        columns = jnp.concatenate(
            [
                shifts[s][:, half * rows + r : half * rows + r + rows].reshape(-1, channels)
                for r in range(3)
                for s in range(3)
            ],
            axis=1,
        )
        pre = jnp.dot(columns, weight[...], preferred_element_type=jnp.float32)
        pre_all[half] = pre
        act_ref[half] = (pre * jax.nn.sigmoid(pre)).astype(jnp.bfloat16)
    pre_ref[...] = pre_all[lax.axis_index("tile")]


def split_kernel(arrived, _, mine_ref, other_ref):
    tile = lax.axis_index("tile")
    mine_ref[...] = arrived[tile]
    other_ref[...] = arrived[1 - tile]


def forward_sum_kernel(partial, arrived, *rest, first):
    sum_ref = rest[-1]
    rows = partial[first : first + sum_ref.shape[0]]
    came = arrived[: sum_ref.shape[0]].astype(jnp.float32)
    sum_ref[...] = (rows + came).astype(sum_ref.dtype)


def last_sum_kernel(keep, near, last_a, last_b, block, out_ref, block_ref, *, scale):
    block_ref[...] = block[...]
    half = last_a.shape[0]
    for first, last in ((0, last_a), (half, last_b)):
        total = keep[first : first + half] + near[first : first + half].astype(jnp.float32)
        out_ref[first : first + half] = (total + last[...].astype(jnp.float32)) * scale


def transpose_kernel(own, other, _, out_ref, image):
    frames, rows, width, channels = own.shape
    tile = lax.axis_index("tile")
    whole_image(own, other, image)
    for which, first in enumerate((tile * rows, (1 - tile) * rows)):
        for r in range(3):
            block = image[:, pl.ds(first + r, rows)].reshape(-1, channels)
            out_ref[which, r * channels : (r + 1) * channels] = block.T


def slabs(own, first, second, ext):
    tile = lax.axis_index("tile")
    ext[2 * tile] = first[...]
    ext[1] = own[...]
    ext[2 - 2 * tile] = second[...]
    chip = lax.axis_index("frame")

    @pl.when(chip == 0)
    def _():
        ext[0] = jnp.zeros_like(ext[0])

    @pl.when(chip == lax.axis_size("frame") - 1)
    def _():
        ext[2] = jnp.zeros_like(ext[2])

    return ext[...].reshape(-1, own.shape[1])


def act_grad_kernel(own, first_in, second_in, weight, pre_ref, _, out_ref, ext):
    count, channels = own.shape
    frames = slabs(own, first_in, second_in, ext)
    hop = count // 4
    total = None
    for k in range(9):
        first = (8 - k) * hop
        term = lax.dot_general(
            frames[first : first + count],
            weight[k * channels : (k + 1) * channels],
            (((1,), (1,)), ((), ())),
            preferred_element_type=jnp.float32,
        )
        total = term if total is None else total + term
    act_grad = total.astype(jnp.bfloat16).astype(jnp.float32)
    pre = pre_ref[...]
    sig = jax.nn.sigmoid(pre)
    out_ref[...] = (act_grad * (sig * (1.0 + pre * (1.0 - sig)))).astype(jnp.bfloat16)


def temporal_kernel(feats, act, first_in, second_in, weight, _, out_ref, ext):
    count, channels = feats.shape
    own = act.at[lax.axis_index("tile")]
    frames = slabs(own, first_in, second_in, ext)
    hop = count // 4
    columns = jnp.concatenate([frames[k * hop : k * hop + count] for k in range(9)], axis=1)
    mixed = jnp.dot(columns, weight[...], preferred_element_type=jnp.float32)
    out_ref[...] = (feats[...].astype(jnp.float32) + mixed).astype(jnp.bfloat16)


def own_term_kernel(feats_t, own, total_ref):
    channels = own.shape[3]
    after, same, before = column_shifts(own[...].reshape(-1, channels), own.shape[2])
    left = feats_t[0]
    for s, right in enumerate((before, same, after)):
        total_ref[s] = jnp.dot(left, right, preferred_element_type=jnp.float32)


def kernel_grad_kernel(
    feats_t, other, term, far_a_ref, far_b_ref, pass_ref, near_ref, keep_ref, total
):
    frames, rows, width, channels = other.shape
    tile = lax.axis_index("tile")
    chip = lax.axis_index("frame")
    after, same, before = column_shifts(other[...].reshape(-1, channels), width)
    left = feats_t[1]
    for s, right in enumerate((before, same, after)):
        both = term[s] + jnp.dot(left, right, preferred_element_type=jnp.float32)
        for r in range(3):
            tap = 3 * r + s
            total[tap * channels : (tap + 1) * channels] = both[r * channels : (r + 1) * channels]
    share = keep_ref.shape[0]
    half = share // 2
    for distance, skip, ref in (
        (2, 0, far_a_ref),
        (2, half, far_b_ref),
        (3, 0, pass_ref),
        (1, 0, near_ref),
        (0, 0, keep_ref),
    ):
        first = (2 * (chip ^ distance) + tile) * share + skip
        ref[...] = total[pl.ds(pl.multiple_of(first, 16), ref.shape[0])].astype(ref.dtype)


def input_grad_kernel(out_grad, own, other, weight, _, out_ref, done_ref, ext):
    frames, rows, width, channels = own.shape
    with_edges(own, other, ext)
    after, same, before = column_shifts(ext[...].reshape(-1, channels), width)
    shifts = [piece.reshape(ext.shape) for piece in (before, same, after)]
    total = out_grad[...].astype(jnp.float32)
    for r in range(3):
        for s in range(3):
            tap = 3 * r + s
            total = total + lax.dot_general(
                shifts[s][:, 2 - r : 2 - r + rows].reshape(-1, channels),
                weight[tap * channels : (tap + 1) * channels],
                (((1,), (1,)), ((), ())),
                preferred_element_type=jnp.float32,
            )
    out_ref[...] = total.astype(jnp.bfloat16)
    done_ref[...] = jnp.zeros_like(done_ref)


def per_device_pair(clip_feats, out_grad, spatial_weight, temporal_weight):
    frames, rows, width, channels = clip_feats.shape
    count = frames * rows * width
    chips = lax.axis_size("frame")
    cores = lax.axis_size("tile")
    scale = 1.0 / math.sqrt(frames * chips * rows * cores * width)
    outward = [(2 * z, 2 * z + 2) for z in range(chips - 1)]
    outward += [(2 * z + 3, 2 * z + 1) for z in range(chips - 1)]
    outward += [(2 * chips - 2, 2 * chips - 1), (1, 0)]
    inward = [(target, source) for source, target in outward]
    both = ("frame", "tile")
    swap = [(0, 1), (1, 0)]
    bf16, f32 = jnp.bfloat16, jnp.float32
    product = 2 * count * 9 * channels * channels
    flat = (count, channels)
    ext = ((frames, rows + 2, width, channels), bf16)
    image = ((frames, 2 * rows + 2, width, channels), bf16)
    three = ((3, count, channels), bf16)

    grad_flat = out_grad.reshape(flat)
    feat_flat = clip_feats.reshape(flat)
    grad_first = lax.ppermute(grad_flat, both, outward)
    grad_second = lax.ppermute(grad_flat, both, inward)
    feat_other = lax.ppermute(clip_feats, "tile", swap)

    (first,) = kernel_call(order_kernel, [((8, 128), f32)], [], 5 * product)
    pre, act = kernel_call(
        spatial_kernel,
        [(flat, f32), ((2, *flat), bf16)],
        [image, ((2, *flat), f32)],
        2 * product,
        clip_feats, spatial_weight, feat_other, first, anywhere=1,
    )
    act_in = lax.ppermute(act, both, inward)
    (feats_t,) = kernel_call(
        transpose_kernel,
        [((2, 3 * channels, count), bf16)],
        [image],
        0,
        clip_feats, feat_other, pre, anywhere=1,
    )
    (pre_grad,) = kernel_call(
        act_grad_kernel,
        [(flat, bf16)],
        [three],
        product,
        grad_flat, grad_first, grad_second, temporal_weight, pre, feats_t, anywhere=1,
    )
    pre_grad = pre_grad.reshape(clip_feats.shape)
    pre_other = lax.ppermute(pre_grad, "tile", swap)

    share = (9 * channels // (chips * cores), channels)
    (term,) = kernel_call(
        own_term_kernel,
        [((3, 3 * channels, channels), f32)],
        [],
        product,
        feats_t, pre_grad,
    )
    half = (share[0] // 2, channels)
    far_a, far_b, onward, near, keep = kernel_call(
        kernel_grad_kernel,
        [(half, bf16), (half, bf16), (share, f32), (share, bf16), (share, f32)],
        [((9 * channels, channels), f32)],
        product,
        feats_t, pre_other, term,
    )
    beside = [(z, z ^ 1) for z in range(chips)]
    across = [(z, z ^ 3) for z in range(chips)]
    far_in_a = lax.ppermute(far_a, "frame", beside)
    far_in_b = lax.ppermute(far_b, "frame", beside)
    near_in = lax.ppermute(near, "frame", beside)
    (sum_a,) = kernel_call(
        functools.partial(forward_sum_kernel, first=0),
        [(half, bf16)],
        [],
        4 * product,
        onward, far_in_a, act_in, anywhere=1,
    )
    last_a = lax.ppermute(sum_a, "frame", across)
    (sum_b,) = kernel_call(
        functools.partial(forward_sum_kernel, first=half[0]),
        [(half, bf16)],
        [],
        0,
        onward, far_in_b, sum_a, anywhere=1,
    )
    last_b = lax.ppermute(sum_b, "frame", across)
    act_second, act_pass = kernel_call(
        split_kernel, [(flat, bf16)] * 2, [], 0, act_in, sum_b, anywhere=1
    )
    act_first = lax.ppermute(act_pass, "tile", swap)

    input_grad, done = kernel_call(
        input_grad_kernel,
        [(flat, bf16), ((8, 128), f32)],
        [ext],
        product,
        grad_flat, pre_grad, pre_other, spatial_weight, sum_b, anywhere=1,
    )
    (arrived,) = kernel_call(
        order_kernel, [((8, 128), f32)], [], 20 * product, last_a, near_in, done, anywhere=3
    )
    (block,) = kernel_call(
        temporal_kernel,
        [(flat, bf16)],
        [three],
        product,
        feat_flat, act, act_first, act_second, temporal_weight, arrived, anywhere=1,
    )
    weight_grad, block_out = kernel_call(
        functools.partial(last_sum_kernel, scale=scale),
        [(share, f32), (flat, bf16)],
        [],
        0,
        keep, near_in, last_a, last_b, block,
    )
    return (
        block_out.reshape(clip_feats.shape),
        input_grad.reshape(clip_feats.shape),
        weight_grad,
    )


def per_device(clip_feats, *rest):
    pairs = lax.axis_size("tile") == 2 and lax.axis_size("frame") == 4
    if pairs and clip_feats.shape[0] == 4 * TAP_DILATION:
        return per_device_pair(clip_feats, *rest)
    return per_device_any(clip_feats, *rest)


def solution(mesh):
    return jax.shard_map(
        per_device,
        mesh=mesh,
        in_specs=(
            P(("clip", "frame"), "tile", None, None),
            P(("clip", "frame"), "tile", None, None),
            P(),
            P(),
        ),
        out_specs=(
            P(("clip", "frame"), "tile", None, None),
            P(("clip", "frame"), "tile", None, None),
            P(("clip", "frame", "tile"), None),
        ),
        check_vma=False,
    )
```

```python
import functools
import math

import jax
import jax.numpy as jnp
from jax import lax
from jax.experimental import pallas as pl
from jax.experimental.pallas import tpu as pltpu
from jax.sharding import PartitionSpec as P

TAP_DILATION = 2
VMEM_LIMIT = 32 * 1024 * 1024


def padded_2(block, sides, width):
    for axis, dim in sides:
        count = lax.axis_size(axis)
        forward = [(i, i + 1) for i in range(count - 1)]
        backward = [(target, source) for source, target in forward]
        low = lax.ppermute(
            lax.slice_in_dim(block, block.shape[dim] - width, None, axis=dim), axis, forward
        )
        high = lax.ppermute(lax.slice_in_dim(block, 0, width, axis=dim), axis, backward)
        block = jnp.concatenate([low, block, high], axis=dim)
    return block


def tile_columns(extended, tile_rows, width_cells, backward_pass):
    padded = jnp.pad(extended, ((0, 0), (0, 0), (1, 1), (0, 0)))
    pieces = []
    for row_shift in range(3):
        for col_shift in range(3):
            row_start = 2 - row_shift if backward_pass else row_shift
            col_start = 2 - col_shift if backward_pass else col_shift
            pieces.append(
                padded[:, row_start : row_start + tile_rows, col_start : col_start + width_cells, :]
            )
    channels = extended.shape[3]
    return jnp.concatenate(pieces, axis=-1).reshape(-1, 9 * channels)


def temporal_taps(padded_seq, weight, frame_count, backward_pass):
    pieces = []
    for temporal_tap_index in range(9):
        first_frame_index = (
            (8 - temporal_tap_index) * TAP_DILATION
            if backward_pass
            else temporal_tap_index * TAP_DILATION
        )
        pieces.append(padded_seq[first_frame_index : first_frame_index + frame_count])
    channels = padded_seq.shape[2]
    columns = jnp.concatenate(pieces, axis=-1).reshape(-1, 9 * channels)
    return jnp.dot(columns, weight, preferred_element_type=jnp.float32)


def per_device_any(clip_feats, out_grad, spatial_weight, temporal_weight):
    slab_frames, tile_rows, width_cells, channels = clip_feats.shape
    row_count = slab_frames * tile_rows * width_cells
    frame_devs = lax.axis_size("frame")
    tile_devs = lax.axis_size("tile")
    grad_scale = jnp.float32(
        1.0 / math.sqrt(slab_frames * frame_devs * tile_rows * tile_devs * width_cells)
    )
    spatial_back = (
        spatial_weight.reshape(9, channels, channels)
        .transpose(0, 2, 1)
        .reshape(9 * channels, channels)
    )
    temporal_back = (
        temporal_weight.reshape(9, channels, channels)
        .transpose(0, 2, 1)
        .reshape(9 * channels, channels)
    )
    feat_ext = padded_2(clip_feats, (("tile", 1),), 1)
    feat_columns = tile_columns(feat_ext, tile_rows, width_cells, False)
    pre = jnp.dot(feat_columns, spatial_weight, preferred_element_type=jnp.float32)
    act = jax.nn.silu(pre).astype(jnp.bfloat16)
    temporal_reach = 4 * TAP_DILATION
    per_group = tile_rows * width_cells // frame_devs
    grouped = (slab_frames, frame_devs, per_group, channels)
    act_part = lax.all_to_all(
        act.reshape(grouped), "frame", split_axis=1, concat_axis=0, tiled=True
    )
    grad_part = lax.all_to_all(out_grad, "frame", split_axis=1, concat_axis=0, tiled=True)
    feat_part = lax.all_to_all(clip_feats, "frame", split_axis=1, concat_axis=0, tiled=True)
    frame_count = act_part.shape[0]
    item_count = act_part.shape[2]
    act_pad = jnp.pad(
        act_part.reshape(frame_count, item_count, channels),
        ((temporal_reach, temporal_reach), (0, 0), (0, 0)),
    )
    grad_pad = jnp.pad(
        grad_part.reshape(frame_count, item_count, channels),
        ((temporal_reach, temporal_reach), (0, 0), (0, 0)),
    )
    mixed = temporal_taps(act_pad, temporal_weight, frame_count, False)
    out_part = (feat_part.reshape(-1, channels).astype(jnp.float32) + mixed).astype(jnp.bfloat16)
    back_part = temporal_taps(grad_pad, temporal_back, frame_count, True).astype(jnp.bfloat16)
    out_part = out_part.reshape(frame_count, 1, item_count, channels)
    back_part = back_part.reshape(frame_count, 1, item_count, channels)
    out_slab = lax.all_to_all(out_part, "frame", split_axis=0, concat_axis=1, tiled=True)
    grad_slab = lax.all_to_all(back_part, "frame", split_axis=0, concat_axis=1, tiled=True)
    act_grad = grad_slab.reshape(row_count, channels)
    sig = jax.nn.sigmoid(pre)
    pre_grad = (act_grad.astype(jnp.float32) * (sig * (1.0 + pre * (1.0 - sig)))).astype(
        jnp.bfloat16
    )
    full_term = lax.dot_general(
        feat_columns, pre_grad, (((0,), (0,)), ((), ())), preferred_element_type=jnp.float32
    )
    summed = lax.psum_scatter(full_term, ("frame", "tile"), scatter_dimension=0, tiled=True)
    weight_grad = summed * grad_scale
    grad_ext = padded_2(
        pre_grad.reshape(slab_frames, tile_rows, width_cells, channels), (("tile", 1),), 1
    )
    grad_columns = tile_columns(grad_ext, tile_rows, width_cells, True)
    local_back = jnp.dot(grad_columns, spatial_back, preferred_element_type=jnp.float32)
    input_grad = (out_grad.reshape(row_count, channels).astype(jnp.float32) + local_back).astype(
        jnp.bfloat16
    )
    input_grad = input_grad.reshape(slab_frames, tile_rows, width_cells, channels)
    return (out_slab, input_grad, weight_grad)


def kernel_call(body, outs, scratch, flops, *args, anywhere=0):
    moved = sum(a.size * a.dtype.itemsize for a in args)
    moved += sum(math.prod(shape) * jnp.dtype(kind).itemsize for shape, kind in outs)
    spaces = [pltpu.VMEM] * (len(args) - anywhere) + [pl.ANY] * anywhere
    return pl.pallas_call(
        body,
        out_shape=tuple(jax.ShapeDtypeStruct(shape, kind) for shape, kind in outs),
        in_specs=[pl.BlockSpec(memory_space=space) for space in spaces],
        out_specs=tuple(pl.BlockSpec(memory_space=pltpu.VMEM) for _ in outs),
        scratch_shapes=[pltpu.VMEM(shape, kind) for shape, kind in scratch],
        compiler_params=pltpu.CompilerParams(vmem_limit_bytes=VMEM_LIMIT),
        cost_estimate=pl.CostEstimate(flops=flops, bytes_accessed=moved, transcendentals=0),
    )(*args)


def shifted(values, width, step):
    rows = values.shape[0]
    at = lax.broadcasted_iota(jnp.int32, values.shape, 0) % width
    moved = pltpu.roll(values, step % rows, 0)
    inside = at >= step if step > 0 else at < width + step
    return jnp.where(inside, moved, 0.0)


def column_shifts(values, width):
    wide = values.astype(jnp.float32)
    return (
        shifted(wide, width, 1).astype(values.dtype),
        values,
        shifted(wide, width, -1).astype(values.dtype),
    )


def with_edges(own, other, ext):
    rows = own.shape[1]
    tile = lax.axis_index("tile")
    ext[:, 1 : rows + 1] = own[...]
    above, below = other[:, rows - 1], other[:, 0]
    ext[:, 0] = jnp.where(tile == 1, above, jnp.zeros_like(above))
    ext[:, rows + 1] = jnp.where(tile == 0, below, jnp.zeros_like(below))


def whole_image(own, other, image):
    rows = own.shape[1]
    tile = lax.axis_index("tile")
    image[:, 0] = jnp.zeros_like(image[:, 0])
    image[:, 2 * rows + 1] = jnp.zeros_like(image[:, 2 * rows + 1])
    image[:, pl.ds(1 + tile * rows, rows)] = own[...]
    image[:, pl.ds(1 + (1 - tile) * rows, rows)] = other[...]


def order_kernel(*refs):
    refs[-1][...] = jnp.zeros_like(refs[-1])


def spatial_kernel(own, weight, other, _, pre_ref, act_ref, image, pre_all):
    frames, rows, width, channels = own.shape
    whole_image(own, other, image)
    shifts = column_shifts(image[...].reshape(-1, channels), width)
    shifts = [piece.reshape(image.shape) for piece in shifts]
    for half in range(2):
        columns = jnp.concatenate(
            [
                shifts[s][:, half * rows + r : half * rows + r + rows].reshape(-1, channels)
                for r in range(3)
                for s in range(3)
            ],
            axis=1,
        )
        pre = jnp.dot(columns, weight[...], preferred_element_type=jnp.float32)
        pre_all[half] = pre
        act_ref[half] = (pre * jax.nn.sigmoid(pre)).astype(jnp.bfloat16)
    pre_ref[...] = pre_all[lax.axis_index("tile")]


def split_kernel(arrived, mine_ref, other_ref):
    tile = lax.axis_index("tile")
    mine_ref[...] = arrived[tile]
    other_ref[...] = arrived[1 - tile]


def forward_sum_kernel(partial, arrived, *rest, first):
    sum_ref = rest[-1]
    rows = partial[first : first + sum_ref.shape[0]]
    came = arrived[: sum_ref.shape[0]].astype(jnp.float32)
    sum_ref[...] = (rows + came).astype(sum_ref.dtype)


def share_rows(keep, near, last, first, scale):
    count = last.shape[0]
    total = keep[first : first + count] + near[first : first + count].astype(jnp.float32)
    return (total + last[...].astype(jnp.float32)) * scale


def first_rows_kernel(keep, near, last, block, _, out_hbm, block_hbm, rows, sems, *, scale):
    block_copy = pltpu.make_async_copy(block, block_hbm, sems.at[0])
    block_copy.start()
    rows[...] = share_rows(keep, near, last, 0, scale)
    copy = pltpu.make_async_copy(rows, out_hbm.at[pl.ds(0, last.shape[0])], sems.at[1])
    copy.start()
    block_copy.wait()
    copy.wait()


def other_rows_kernel(keep, near, last, _, out_hbm, rows, sems, *, scale):
    first = keep.shape[0] - last.shape[0]
    rows[...] = share_rows(keep, near, last, first, scale)
    copy = pltpu.make_async_copy(rows, out_hbm.at[pl.ds(first, last.shape[0])], sems.at[0])
    copy.start()
    copy.wait()


def transpose_kernel(own, other, _, out_ref, image):
    frames, rows, width, channels = own.shape
    tile = lax.axis_index("tile")
    whole_image(own, other, image)
    for which, first in enumerate((tile * rows, (1 - tile) * rows)):
        for r in range(3):
            block = image[:, pl.ds(first + r, rows)].reshape(-1, channels)
            out_ref[which, r * channels : (r + 1) * channels] = block.T


def slabs(own, first, second, ext):
    tile = lax.axis_index("tile")
    ext[2 * tile] = first[...]
    ext[1] = own[...]
    ext[2 - 2 * tile] = second[...]
    chip = lax.axis_index("frame")

    @pl.when(chip == 0)
    def _():
        ext[0] = jnp.zeros_like(ext[0])

    @pl.when(chip == lax.axis_size("frame") - 1)
    def _():
        ext[2] = jnp.zeros_like(ext[2])

    return ext[...].reshape(-1, own.shape[1])


def act_grad_kernel(own, first_in, second_in, weight, pre_ref, _, out_ref, ext):
    count, channels = own.shape
    frames = slabs(own, first_in, second_in, ext)
    hop = count // 4
    total = None
    for k in range(9):
        first = (8 - k) * hop
        term = lax.dot_general(
            frames[first : first + count],
            weight[k * channels : (k + 1) * channels],
            (((1,), (1,)), ((), ())),
            preferred_element_type=jnp.float32,
        )
        total = term if total is None else total + term
    act_grad = total.astype(jnp.bfloat16).astype(jnp.float32)
    pre = pre_ref[...]
    sig = jax.nn.sigmoid(pre)
    out_ref[...] = (act_grad * (sig * (1.0 + pre * (1.0 - sig)))).astype(jnp.bfloat16)


def temporal_kernel(feats, act, first_in, second_in, weight, out_ref, ext):
    count, channels = feats.shape
    own = act.at[lax.axis_index("tile")]
    frames = slabs(own, first_in, second_in, ext)
    hop = count // 4
    columns = jnp.concatenate([frames[k * hop : k * hop + count] for k in range(9)], axis=1)
    mixed = jnp.dot(columns, weight[...], preferred_element_type=jnp.float32)
    out_ref[...] = (feats[...].astype(jnp.float32) + mixed).astype(jnp.bfloat16)


def own_term_kernel(feats_t, own, total_ref):
    channels = own.shape[3]
    after, same, before = column_shifts(own[...].reshape(-1, channels), own.shape[2])
    left = feats_t[0]
    for s, right in enumerate((before, same, after)):
        total_ref[s] = jnp.dot(left, right, preferred_element_type=jnp.float32)


def kernel_grad_kernel(
    feats_t, other, term, far_a_ref, far_b_ref, pass_ref, near_ref, keep_ref, total
):
    frames, rows, width, channels = other.shape
    tile = lax.axis_index("tile")
    chip = lax.axis_index("frame")
    after, same, before = column_shifts(other[...].reshape(-1, channels), width)
    left = feats_t[1]
    for s, right in enumerate((before, same, after)):
        both = term[s] + jnp.dot(left, right, preferred_element_type=jnp.float32)
        for r in range(3):
            tap = 3 * r + s
            total[tap * channels : (tap + 1) * channels] = both[r * channels : (r + 1) * channels]
    share = keep_ref.shape[0]
    half = share // 2
    for distance, skip, ref in (
        (2, 0, far_a_ref),
        (2, half, far_b_ref),
        (3, 0, pass_ref),
        (1, 0, near_ref),
        (0, 0, keep_ref),
    ):
        first = (2 * (chip ^ distance) + tile) * share + skip
        ref[...] = total[pl.ds(pl.multiple_of(first, 16), ref.shape[0])].astype(ref.dtype)


def input_grad_kernel(out_grad, own, other, weight, _, out_ref, done_ref, ext):
    frames, rows, width, channels = own.shape
    with_edges(own, other, ext)
    after, same, before = column_shifts(ext[...].reshape(-1, channels), width)
    shifts = [piece.reshape(ext.shape) for piece in (before, same, after)]
    total = out_grad[...].astype(jnp.float32)
    for r in range(3):
        for s in range(3):
            tap = 3 * r + s
            total = total + lax.dot_general(
                shifts[s][:, 2 - r : 2 - r + rows].reshape(-1, channels),
                weight[tap * channels : (tap + 1) * channels],
                (((1,), (1,)), ((), ())),
                preferred_element_type=jnp.float32,
            )
    out_ref[...] = total.astype(jnp.bfloat16)
    done_ref[...] = jnp.zeros_like(done_ref)


def per_device_pair(clip_feats, out_grad, spatial_weight, temporal_weight):
    frames, rows, width, channels = clip_feats.shape
    count = frames * rows * width
    chips = lax.axis_size("frame")
    cores = lax.axis_size("tile")
    scale = 1.0 / math.sqrt(frames * chips * rows * cores * width)
    outward = [(2 * z, 2 * z + 2) for z in range(chips - 1)]
    outward += [(2 * z + 3, 2 * z + 1) for z in range(chips - 1)]
    outward += [(2 * chips - 2, 2 * chips - 1), (1, 0)]
    inward = [(target, source) for source, target in outward]
    both = ("frame", "tile")
    swap = [(0, 1), (1, 0)]
    bf16, f32 = jnp.bfloat16, jnp.float32
    product = 2 * count * 9 * channels * channels
    flat = (count, channels)
    ext = ((frames, rows + 2, width, channels), bf16)
    image = ((frames, 2 * rows + 2, width, channels), bf16)
    three = ((3, count, channels), bf16)

    grad_flat = out_grad.reshape(flat)
    feat_flat = clip_feats.reshape(flat)
    grad_first = lax.ppermute(grad_flat, both, outward)
    grad_second = lax.ppermute(grad_flat, both, inward)
    feat_other = lax.ppermute(clip_feats, "tile", swap)

    (first,) = kernel_call(order_kernel, [((8, 128), f32)], [], 5 * product)
    pre, act = kernel_call(
        spatial_kernel,
        [(flat, f32), ((2, *flat), bf16)],
        [image, ((2, *flat), f32)],
        2 * product,
        clip_feats, spatial_weight, feat_other, first, anywhere=1,
    )
    act_in = lax.ppermute(act, both, inward)
    (feats_t,) = kernel_call(
        transpose_kernel,
        [((2, 3 * channels, count), bf16)],
        [image],
        0,
        clip_feats, feat_other, pre, anywhere=1,
    )
    (pre_grad,) = kernel_call(
        act_grad_kernel,
        [(flat, bf16)],
        [three],
        product,
        grad_flat, grad_first, grad_second, temporal_weight, pre, feats_t, anywhere=1,
    )
    pre_grad = pre_grad.reshape(clip_feats.shape)
    pre_other = lax.ppermute(pre_grad, "tile", swap)

    share = (9 * channels // (chips * cores), channels)
    (term,) = kernel_call(
        own_term_kernel,
        [((3, 3 * channels, channels), f32)],
        [],
        product,
        feats_t, pre_grad,
    )
    half = (share[0] // 2, channels)
    far_a, far_b, onward, near, keep = kernel_call(
        kernel_grad_kernel,
        [(half, bf16), (half, bf16), (share, f32), (share, bf16), (share, f32)],
        [((9 * channels, channels), f32)],
        product,
        feats_t, pre_other, term,
    )
    beside = [(z, z ^ 1) for z in range(chips)]
    across = [(z, z ^ 3) for z in range(chips)]
    far_in_a = lax.ppermute(far_a, "frame", beside)
    far_in_b = lax.ppermute(far_b, "frame", beside)
    near_in = lax.ppermute(near, "frame", beside)
    act_second, act_pass = kernel_call(
        split_kernel, [(flat, bf16)] * 2, [], 0, act_in
    )
    act_first = lax.ppermute(act_pass, "tile", swap)

    (sum_a,) = kernel_call(
        functools.partial(forward_sum_kernel, first=0),
        [(half, bf16)],
        [],
        20 * product,
        onward, far_in_a, act_pass, anywhere=1,
    )
    last_a = lax.ppermute(sum_a, "frame", across)
    (sum_b,) = kernel_call(
        functools.partial(forward_sum_kernel, first=half[0]),
        [(half, bf16)],
        [],
        0,
        onward, far_in_b, sum_a, act_first, anywhere=2,
    )
    last_b = lax.ppermute(sum_b, "frame", across)
    input_grad, done = kernel_call(
        input_grad_kernel,
        [(flat, bf16), ((8, 128), f32)],
        [ext],
        product,
        grad_flat, pre_grad, pre_other, spatial_weight, sum_b, anywhere=1,
    )
    (block,) = kernel_call(
        temporal_kernel,
        [(flat, bf16)],
        [three],
        product,
        feat_flat, act, act_first, act_second, temporal_weight,
    )
    (arrived,) = kernel_call(
        order_kernel, [((8, 128), f32)], [], 20 * product, last_a, near_in, done, block, anywhere=4
    )
    weight_grad, block_out = pl.pallas_call(
        functools.partial(first_rows_kernel, scale=scale),
        out_shape=(jax.ShapeDtypeStruct(share, f32), jax.ShapeDtypeStruct(flat, bf16)),
        in_specs=[pl.BlockSpec(memory_space=pltpu.VMEM)] * 4 + [pl.BlockSpec(memory_space=pl.ANY)],
        out_specs=(
            pl.BlockSpec(memory_space=pltpu.HBM),
            pl.BlockSpec(memory_space=pltpu.HBM),
        ),
        scratch_shapes=[pltpu.VMEM(half, f32), pltpu.SemaphoreType.DMA((2,))],
        compiler_params=pltpu.CompilerParams(vmem_limit_bytes=VMEM_LIMIT),
    )(keep, near_in, last_a, block, arrived)
    weight_grad = pl.pallas_call(
        functools.partial(other_rows_kernel, scale=scale),
        out_shape=jax.ShapeDtypeStruct(share, f32),
        in_specs=[pl.BlockSpec(memory_space=pltpu.VMEM)] * 3 + [pl.BlockSpec(memory_space=pltpu.HBM)],
        out_specs=pl.BlockSpec(memory_space=pltpu.HBM),
        scratch_shapes=[pltpu.VMEM(half, f32), pltpu.SemaphoreType.DMA((1,))],
        input_output_aliases={3: 0},
        compiler_params=pltpu.CompilerParams(vmem_limit_bytes=VMEM_LIMIT),
    )(keep, near_in, last_b, weight_grad)
    return (
        block_out.reshape(clip_feats.shape),
        input_grad.reshape(clip_feats.shape),
        weight_grad,
    )


def per_device(clip_feats, *rest):
    pairs = lax.axis_size("tile") == 2 and lax.axis_size("frame") == 4
    if pairs and clip_feats.shape[0] == 4 * TAP_DILATION:
        return per_device_pair(clip_feats, *rest)
    return per_device_any(clip_feats, *rest)


def solution(mesh):
    return jax.shard_map(
        per_device,
        mesh=mesh,
        in_specs=(
            P(("clip", "frame"), "tile", None, None),
            P(("clip", "frame"), "tile", None, None),
            P(),
            P(),
        ),
        out_specs=(
            P(("clip", "frame"), "tile", None, None),
            P(("clip", "frame"), "tile", None, None),
            P(("clip", "frame", "tile"), None),
        ),
        check_vma=False,
    )
```

```python
import functools
import math

import jax
import jax.numpy as jnp
from jax import lax
from jax.experimental import pallas as pl
from jax.experimental.pallas import tpu as pltpu
from jax.sharding import PartitionSpec as P

TAP_DILATION = 2
VMEM_LIMIT = 32 * 1024 * 1024


def padded_2(block, sides, width):
    for axis, dim in sides:
        count = lax.axis_size(axis)
        forward = [(i, i + 1) for i in range(count - 1)]
        backward = [(target, source) for source, target in forward]
        low = lax.ppermute(
            lax.slice_in_dim(block, block.shape[dim] - width, None, axis=dim), axis, forward
        )
        high = lax.ppermute(lax.slice_in_dim(block, 0, width, axis=dim), axis, backward)
        block = jnp.concatenate([low, block, high], axis=dim)
    return block


def tile_columns(extended, tile_rows, width_cells, backward_pass):
    padded = jnp.pad(extended, ((0, 0), (0, 0), (1, 1), (0, 0)))
    pieces = []
    for row_shift in range(3):
        for col_shift in range(3):
            row_start = 2 - row_shift if backward_pass else row_shift
            col_start = 2 - col_shift if backward_pass else col_shift
            pieces.append(
                padded[:, row_start : row_start + tile_rows, col_start : col_start + width_cells, :]
            )
    channels = extended.shape[3]
    return jnp.concatenate(pieces, axis=-1).reshape(-1, 9 * channels)


def temporal_taps(padded_seq, weight, frame_count, backward_pass):
    pieces = []
    for temporal_tap_index in range(9):
        first_frame_index = (
            (8 - temporal_tap_index) * TAP_DILATION
            if backward_pass
            else temporal_tap_index * TAP_DILATION
        )
        pieces.append(padded_seq[first_frame_index : first_frame_index + frame_count])
    channels = padded_seq.shape[2]
    columns = jnp.concatenate(pieces, axis=-1).reshape(-1, 9 * channels)
    return jnp.dot(columns, weight, preferred_element_type=jnp.float32)


def per_device_any(clip_feats, out_grad, spatial_weight, temporal_weight):
    slab_frames, tile_rows, width_cells, channels = clip_feats.shape
    row_count = slab_frames * tile_rows * width_cells
    frame_devs = lax.axis_size("frame")
    tile_devs = lax.axis_size("tile")
    grad_scale = jnp.float32(
        1.0 / math.sqrt(slab_frames * frame_devs * tile_rows * tile_devs * width_cells)
    )
    spatial_back = (
        spatial_weight.reshape(9, channels, channels)
        .transpose(0, 2, 1)
        .reshape(9 * channels, channels)
    )
    temporal_back = (
        temporal_weight.reshape(9, channels, channels)
        .transpose(0, 2, 1)
        .reshape(9 * channels, channels)
    )
    feat_ext = padded_2(clip_feats, (("tile", 1),), 1)
    feat_columns = tile_columns(feat_ext, tile_rows, width_cells, False)
    pre = jnp.dot(feat_columns, spatial_weight, preferred_element_type=jnp.float32)
    act = jax.nn.silu(pre).astype(jnp.bfloat16)
    temporal_reach = 4 * TAP_DILATION
    per_group = tile_rows * width_cells // frame_devs
    grouped = (slab_frames, frame_devs, per_group, channels)
    act_part = lax.all_to_all(
        act.reshape(grouped), "frame", split_axis=1, concat_axis=0, tiled=True
    )
    grad_part = lax.all_to_all(out_grad, "frame", split_axis=1, concat_axis=0, tiled=True)
    feat_part = lax.all_to_all(clip_feats, "frame", split_axis=1, concat_axis=0, tiled=True)
    frame_count = act_part.shape[0]
    item_count = act_part.shape[2]
    act_pad = jnp.pad(
        act_part.reshape(frame_count, item_count, channels),
        ((temporal_reach, temporal_reach), (0, 0), (0, 0)),
    )
    grad_pad = jnp.pad(
        grad_part.reshape(frame_count, item_count, channels),
        ((temporal_reach, temporal_reach), (0, 0), (0, 0)),
    )
    mixed = temporal_taps(act_pad, temporal_weight, frame_count, False)
    out_part = (feat_part.reshape(-1, channels).astype(jnp.float32) + mixed).astype(jnp.bfloat16)
    back_part = temporal_taps(grad_pad, temporal_back, frame_count, True).astype(jnp.bfloat16)
    out_part = out_part.reshape(frame_count, 1, item_count, channels)
    back_part = back_part.reshape(frame_count, 1, item_count, channels)
    out_slab = lax.all_to_all(out_part, "frame", split_axis=0, concat_axis=1, tiled=True)
    grad_slab = lax.all_to_all(back_part, "frame", split_axis=0, concat_axis=1, tiled=True)
    act_grad = grad_slab.reshape(row_count, channels)
    sig = jax.nn.sigmoid(pre)
    pre_grad = (act_grad.astype(jnp.float32) * (sig * (1.0 + pre * (1.0 - sig)))).astype(
        jnp.bfloat16
    )
    full_term = lax.dot_general(
        feat_columns, pre_grad, (((0,), (0,)), ((), ())), preferred_element_type=jnp.float32
    )
    summed = lax.psum_scatter(full_term, ("frame", "tile"), scatter_dimension=0, tiled=True)
    weight_grad = summed * grad_scale
    grad_ext = padded_2(
        pre_grad.reshape(slab_frames, tile_rows, width_cells, channels), (("tile", 1),), 1
    )
    grad_columns = tile_columns(grad_ext, tile_rows, width_cells, True)
    local_back = jnp.dot(grad_columns, spatial_back, preferred_element_type=jnp.float32)
    input_grad = (out_grad.reshape(row_count, channels).astype(jnp.float32) + local_back).astype(
        jnp.bfloat16
    )
    input_grad = input_grad.reshape(slab_frames, tile_rows, width_cells, channels)
    return (out_slab, input_grad, weight_grad)


def kernel_call(body, outs, scratch, flops, *args, anywhere=0):
    moved = sum(a.size * a.dtype.itemsize for a in args)
    moved += sum(math.prod(shape) * jnp.dtype(kind).itemsize for shape, kind in outs)
    spaces = [pltpu.VMEM] * (len(args) - anywhere) + [pl.ANY] * anywhere
    return pl.pallas_call(
        body,
        out_shape=tuple(jax.ShapeDtypeStruct(shape, kind) for shape, kind in outs),
        in_specs=[pl.BlockSpec(memory_space=space) for space in spaces],
        out_specs=tuple(pl.BlockSpec(memory_space=pltpu.VMEM) for _ in outs),
        scratch_shapes=[pltpu.VMEM(shape, kind) for shape, kind in scratch],
        compiler_params=pltpu.CompilerParams(vmem_limit_bytes=VMEM_LIMIT),
        cost_estimate=pl.CostEstimate(flops=flops, bytes_accessed=moved, transcendentals=0),
    )(*args)


def shifted(values, width, step):
    rows = values.shape[0]
    at = lax.broadcasted_iota(jnp.int32, values.shape, 0) % width
    moved = pltpu.roll(values, step % rows, 0)
    inside = at >= step if step > 0 else at < width + step
    return jnp.where(inside, moved, 0.0)


def column_shifts(values, width):
    wide = values.astype(jnp.float32)
    return (
        shifted(wide, width, 1).astype(values.dtype),
        values,
        shifted(wide, width, -1).astype(values.dtype),
    )


def with_edges(own, other, ext):
    rows = own.shape[1]
    tile = lax.axis_index("tile")
    ext[:, 1 : rows + 1] = own[...]
    above, below = other[:, rows - 1], other[:, 0]
    ext[:, 0] = jnp.where(tile == 1, above, jnp.zeros_like(above))
    ext[:, rows + 1] = jnp.where(tile == 0, below, jnp.zeros_like(below))


def whole_image(own, other, image):
    rows = own.shape[1]
    tile = lax.axis_index("tile")
    image[:, 0] = jnp.zeros_like(image[:, 0])
    image[:, 2 * rows + 1] = jnp.zeros_like(image[:, 2 * rows + 1])
    image[:, pl.ds(1 + tile * rows, rows)] = own[...]
    image[:, pl.ds(1 + (1 - tile) * rows, rows)] = other[...]


def order_kernel(*refs):
    refs[-1][...] = jnp.zeros_like(refs[-1])


def spatial_kernel(own, weight, other, _, pre_ref, act_ref, image, pre_all):
    frames, rows, width, channels = own.shape
    whole_image(own, other, image)
    shifts = column_shifts(image[...].reshape(-1, channels), width)
    shifts = [piece.reshape(image.shape) for piece in shifts]
    for half in range(2):
        columns = jnp.concatenate(
            [
                shifts[s][:, half * rows + r : half * rows + r + rows].reshape(-1, channels)
                for r in range(3)
                for s in range(3)
            ],
            axis=1,
        )
        pre = jnp.dot(columns, weight[...], preferred_element_type=jnp.float32)
        pre_all[half] = pre
        act_ref[half] = (pre * jax.nn.sigmoid(pre)).astype(jnp.bfloat16)
    pre_ref[...] = pre_all[lax.axis_index("tile")]


def split_kernel(arrived, mine_ref, other_ref):
    tile = lax.axis_index("tile")
    mine_ref[...] = arrived[tile]
    other_ref[...] = arrived[1 - tile]


def forward_sum_kernel(partial, arrived, *rest, first):
    sum_ref = rest[-1]
    rows = partial[first : first + sum_ref.shape[0]]
    came = arrived[: sum_ref.shape[0]].astype(jnp.float32)
    sum_ref[...] = (rows + came).astype(sum_ref.dtype)


def share_rows(keep, near, last, first, scale):
    count = last.shape[0]
    total = keep[first : first + count] + near[first : first + count].astype(jnp.float32)
    return (total + last[...].astype(jnp.float32)) * scale


def first_rows_kernel(keep, near, last, block, _, out_hbm, block_hbm, rows, sems, *, scale):
    block_copy = pltpu.make_async_copy(block, block_hbm, sems.at[0])
    block_copy.start()
    rows[...] = share_rows(keep, near, last, 0, scale)
    copy = pltpu.make_async_copy(rows, out_hbm.at[pl.ds(0, last.shape[0])], sems.at[1])
    copy.start()
    block_copy.wait()
    copy.wait()


def other_rows_kernel(keep, near, last, _, out_hbm, rows, sems, *, scale):
    first = keep.shape[0] - last.shape[0]
    rows[...] = share_rows(keep, near, last, first, scale)
    copy = pltpu.make_async_copy(rows, out_hbm.at[pl.ds(first, last.shape[0])], sems.at[0])
    copy.start()
    copy.wait()


def transpose_kernel(own, other, _, out_ref, image):
    frames, rows, width, channels = own.shape
    tile = lax.axis_index("tile")
    whole_image(own, other, image)
    for which, first in enumerate((tile * rows, (1 - tile) * rows)):
        for r in range(3):
            block = image[:, pl.ds(first + r, rows)].reshape(-1, channels)
            out_ref[which, r * channels : (r + 1) * channels] = block.T


def slabs(own, first, second, ext):
    tile = lax.axis_index("tile")
    ext[2 * tile] = first[...]
    ext[1] = own[...]
    ext[2 - 2 * tile] = second[...]
    chip = lax.axis_index("frame")

    @pl.when(chip == 0)
    def _():
        ext[0] = jnp.zeros_like(ext[0])

    @pl.when(chip == lax.axis_size("frame") - 1)
    def _():
        ext[2] = jnp.zeros_like(ext[2])

    return ext[...].reshape(-1, own.shape[1])


def act_grad_kernel(own, first_in, second_in, weight, pre_ref, _, out_ref, ext):
    count, channels = own.shape
    frames = slabs(own, first_in, second_in, ext)
    hop = count // 4
    total = None
    for k in range(9):
        first = (8 - k) * hop
        term = lax.dot_general(
            frames[first : first + count],
            weight[k * channels : (k + 1) * channels],
            (((1,), (1,)), ((), ())),
            preferred_element_type=jnp.float32,
        )
        total = term if total is None else total + term
    act_grad = total.astype(jnp.bfloat16).astype(jnp.float32)
    pre = pre_ref[...]
    sig = jax.nn.sigmoid(pre)
    out_ref[...] = (act_grad * (sig * (1.0 + pre * (1.0 - sig)))).astype(jnp.bfloat16)


def temporal_kernel(feats, act, first_in, second_in, weight, out_ref, ext):
    count, channels = feats.shape
    own = act.at[lax.axis_index("tile")]
    frames = slabs(own, first_in, second_in, ext)
    hop = count // 4
    columns = jnp.concatenate([frames[k * hop : k * hop + count] for k in range(9)], axis=1)
    mixed = jnp.dot(columns, weight[...], preferred_element_type=jnp.float32)
    out_ref[...] = (feats[...].astype(jnp.float32) + mixed).astype(jnp.bfloat16)


def own_term_kernel(feats_t, own, total_ref):
    channels = own.shape[3]
    after, same, before = column_shifts(own[...].reshape(-1, channels), own.shape[2])
    left = feats_t[0]
    for s, right in enumerate((before, same, after)):
        total_ref[s] = jnp.dot(left, right, preferred_element_type=jnp.float32)


def kernel_grad_kernel(
    feats_t, other, term, far_a_ref, far_b_ref, pass_ref, near_ref, keep_ref, total
):
    frames, rows, width, channels = other.shape
    tile = lax.axis_index("tile")
    chip = lax.axis_index("frame")
    after, same, before = column_shifts(other[...].reshape(-1, channels), width)
    left = feats_t[1]
    for s, right in enumerate((before, same, after)):
        both = term[s] + jnp.dot(left, right, preferred_element_type=jnp.float32)
        for r in range(3):
            tap = 3 * r + s
            total[tap * channels : (tap + 1) * channels] = both[r * channels : (r + 1) * channels]
    share = keep_ref.shape[0]
    half = far_a_ref.shape[0]
    for distance, skip, ref in (
        (2, 0, far_a_ref),
        (2, half, far_b_ref),
        (3, 0, pass_ref),
        (1, 0, near_ref),
        (0, 0, keep_ref),
    ):
        first = (2 * (chip ^ distance) + tile) * share + skip
        ref[...] = total[pl.ds(pl.multiple_of(first, 16), ref.shape[0])].astype(ref.dtype)


def input_grad_kernel(out_grad, own, other, weight, _, out_ref, done_ref, ext):
    frames, rows, width, channels = own.shape
    with_edges(own, other, ext)
    after, same, before = column_shifts(ext[...].reshape(-1, channels), width)
    shifts = [piece.reshape(ext.shape) for piece in (before, same, after)]
    total = out_grad[...].astype(jnp.float32)
    for r in range(3):
        for s in range(3):
            tap = 3 * r + s
            total = total + lax.dot_general(
                shifts[s][:, 2 - r : 2 - r + rows].reshape(-1, channels),
                weight[tap * channels : (tap + 1) * channels],
                (((1,), (1,)), ((), ())),
                preferred_element_type=jnp.float32,
            )
    out_ref[...] = total.astype(jnp.bfloat16)
    done_ref[...] = jnp.zeros_like(done_ref)


def per_device_pair(clip_feats, out_grad, spatial_weight, temporal_weight):
    frames, rows, width, channels = clip_feats.shape
    count = frames * rows * width
    chips = lax.axis_size("frame")
    cores = lax.axis_size("tile")
    scale = 1.0 / math.sqrt(frames * chips * rows * cores * width)
    outward = [(2 * z, 2 * z + 2) for z in range(chips - 1)]
    outward += [(2 * z + 3, 2 * z + 1) for z in range(chips - 1)]
    outward += [(2 * chips - 2, 2 * chips - 1), (1, 0)]
    inward = [(target, source) for source, target in outward]
    both = ("frame", "tile")
    swap = [(0, 1), (1, 0)]
    bf16, f32 = jnp.bfloat16, jnp.float32
    product = 2 * count * 9 * channels * channels
    flat = (count, channels)
    ext = ((frames, rows + 2, width, channels), bf16)
    image = ((frames, 2 * rows + 2, width, channels), bf16)
    three = ((3, count, channels), bf16)

    grad_flat = out_grad.reshape(flat)
    feat_flat = clip_feats.reshape(flat)
    grad_first = lax.ppermute(grad_flat, both, outward)
    grad_second = lax.ppermute(grad_flat, both, inward)
    feat_other = lax.ppermute(clip_feats, "tile", swap)

    (first,) = kernel_call(order_kernel, [((8, 128), f32)], [], 5 * product)
    pre, act = kernel_call(
        spatial_kernel,
        [(flat, f32), ((2, *flat), bf16)],
        [image, ((2, *flat), f32)],
        2 * product,
        clip_feats, spatial_weight, feat_other, first, anywhere=1,
    )
    act_in = lax.ppermute(act, both, inward)
    (feats_t,) = kernel_call(
        transpose_kernel,
        [((2, 3 * channels, count), bf16)],
        [image],
        0,
        clip_feats, feat_other, pre, anywhere=1,
    )
    (pre_grad,) = kernel_call(
        act_grad_kernel,
        [(flat, bf16)],
        [three],
        product,
        grad_flat, grad_first, grad_second, temporal_weight, pre, feats_t, anywhere=1,
    )
    pre_grad = pre_grad.reshape(clip_feats.shape)
    pre_other = lax.ppermute(pre_grad, "tile", swap)

    share = (9 * channels // (chips * cores), channels)
    (term,) = kernel_call(
        own_term_kernel,
        [((3, 3 * channels, channels), f32)],
        [],
        product,
        feats_t, pre_grad,
    )
    part_a = (share[0] * 2 // 3, channels)
    part_b = (share[0] - part_a[0], channels)
    far_a, far_b, onward, near, keep = kernel_call(
        kernel_grad_kernel,
        [(part_a, bf16), (part_b, bf16), (share, f32), (share, bf16), (share, f32)],
        [((9 * channels, channels), f32)],
        product,
        feats_t, pre_other, term,
    )
    beside = [(z, z ^ 1) for z in range(chips)]
    across = [(z, z ^ 3) for z in range(chips)]
    far_in_a = lax.ppermute(far_a, "frame", beside)
    far_in_b = lax.ppermute(far_b, "frame", beside)
    near_in = lax.ppermute(near, "frame", beside)
    act_second, act_pass = kernel_call(
        split_kernel, [(flat, bf16)] * 2, [], 0, act_in
    )
    act_first = lax.ppermute(act_pass, "tile", swap)

    (sum_a,) = kernel_call(
        functools.partial(forward_sum_kernel, first=0),
        [(part_a, bf16)],
        [],
        20 * product,
        onward, far_in_a, act_pass, anywhere=1,
    )
    last_a = lax.ppermute(sum_a, "frame", across)
    (sum_b,) = kernel_call(
        functools.partial(forward_sum_kernel, first=part_a[0]),
        [(part_b, bf16)],
        [],
        0,
        onward, far_in_b, sum_a, act_first, anywhere=2,
    )
    last_b = lax.ppermute(sum_b, "frame", across)
    input_grad, done = kernel_call(
        input_grad_kernel,
        [(flat, bf16), ((8, 128), f32)],
        [ext],
        product,
        grad_flat, pre_grad, pre_other, spatial_weight, sum_b, anywhere=1,
    )
    (block,) = kernel_call(
        temporal_kernel,
        [(flat, bf16)],
        [three],
        product,
        feat_flat, act, act_first, act_second, temporal_weight,
    )
    (arrived,) = kernel_call(
        order_kernel, [((8, 128), f32)], [], 20 * product, last_a, near_in, done, block, anywhere=4
    )
    weight_grad, block_out = pl.pallas_call(
        functools.partial(first_rows_kernel, scale=scale),
        out_shape=(jax.ShapeDtypeStruct(share, f32), jax.ShapeDtypeStruct(flat, bf16)),
        in_specs=[pl.BlockSpec(memory_space=pltpu.VMEM)] * 4 + [pl.BlockSpec(memory_space=pl.ANY)],
        out_specs=(
            pl.BlockSpec(memory_space=pltpu.HBM),
            pl.BlockSpec(memory_space=pltpu.HBM),
        ),
        scratch_shapes=[pltpu.VMEM(part_a, f32), pltpu.SemaphoreType.DMA((2,))],
        compiler_params=pltpu.CompilerParams(vmem_limit_bytes=VMEM_LIMIT),
    )(keep, near_in, last_a, block, arrived)
    weight_grad = pl.pallas_call(
        functools.partial(other_rows_kernel, scale=scale),
        out_shape=jax.ShapeDtypeStruct(share, f32),
        in_specs=[pl.BlockSpec(memory_space=pltpu.VMEM)] * 3 + [pl.BlockSpec(memory_space=pltpu.HBM)],
        out_specs=pl.BlockSpec(memory_space=pltpu.HBM),
        scratch_shapes=[pltpu.VMEM(part_b, f32), pltpu.SemaphoreType.DMA((1,))],
        input_output_aliases={3: 0},
        compiler_params=pltpu.CompilerParams(vmem_limit_bytes=VMEM_LIMIT),
    )(keep, near_in, last_b, weight_grad)
    return (
        block_out.reshape(clip_feats.shape),
        input_grad.reshape(clip_feats.shape),
        weight_grad,
    )


def per_device(clip_feats, *rest):
    pairs = lax.axis_size("tile") == 2 and lax.axis_size("frame") == 4
    if pairs and clip_feats.shape[0] == 4 * TAP_DILATION:
        return per_device_pair(clip_feats, *rest)
    return per_device_any(clip_feats, *rest)


def solution(mesh):
    return jax.shard_map(
        per_device,
        mesh=mesh,
        in_specs=(
            P(("clip", "frame"), "tile", None, None),
            P(("clip", "frame"), "tile", None, None),
            P(),
            P(),
        ),
        out_specs=(
            P(("clip", "frame"), "tile", None, None),
            P(("clip", "frame"), "tile", None, None),
            P(("clip", "frame", "tile"), None),
        ),
        check_vma=False,
    )
```

```python
import functools
import math

import jax
import jax.numpy as jnp
from jax import lax
from jax.experimental import pallas as pl
from jax.experimental.pallas import tpu as pltpu
from jax.sharding import PartitionSpec as P

TAP_DILATION = 2
VMEM_LIMIT = 32 * 1024 * 1024


def padded_2(block, sides, width):
    for axis, dim in sides:
        count = lax.axis_size(axis)
        forward = [(i, i + 1) for i in range(count - 1)]
        backward = [(target, source) for source, target in forward]
        low = lax.ppermute(
            lax.slice_in_dim(block, block.shape[dim] - width, None, axis=dim), axis, forward
        )
        high = lax.ppermute(lax.slice_in_dim(block, 0, width, axis=dim), axis, backward)
        block = jnp.concatenate([low, block, high], axis=dim)
    return block


def tile_columns(extended, tile_rows, width_cells, backward_pass):
    padded = jnp.pad(extended, ((0, 0), (0, 0), (1, 1), (0, 0)))
    pieces = []
    for row_shift in range(3):
        for col_shift in range(3):
            row_start = 2 - row_shift if backward_pass else row_shift
            col_start = 2 - col_shift if backward_pass else col_shift
            pieces.append(
                padded[:, row_start : row_start + tile_rows, col_start : col_start + width_cells, :]
            )
    channels = extended.shape[3]
    return jnp.concatenate(pieces, axis=-1).reshape(-1, 9 * channels)


def temporal_taps(padded_seq, weight, frame_count, backward_pass):
    pieces = []
    for temporal_tap_index in range(9):
        first_frame_index = (
            (8 - temporal_tap_index) * TAP_DILATION
            if backward_pass
            else temporal_tap_index * TAP_DILATION
        )
        pieces.append(padded_seq[first_frame_index : first_frame_index + frame_count])
    channels = padded_seq.shape[2]
    columns = jnp.concatenate(pieces, axis=-1).reshape(-1, 9 * channels)
    return jnp.dot(columns, weight, preferred_element_type=jnp.float32)


def per_device_any(clip_feats, out_grad, spatial_weight, temporal_weight):
    slab_frames, tile_rows, width_cells, channels = clip_feats.shape
    row_count = slab_frames * tile_rows * width_cells
    frame_devs = lax.axis_size("frame")
    tile_devs = lax.axis_size("tile")
    grad_scale = jnp.float32(
        1.0 / math.sqrt(slab_frames * frame_devs * tile_rows * tile_devs * width_cells)
    )
    spatial_back = (
        spatial_weight.reshape(9, channels, channels)
        .transpose(0, 2, 1)
        .reshape(9 * channels, channels)
    )
    temporal_back = (
        temporal_weight.reshape(9, channels, channels)
        .transpose(0, 2, 1)
        .reshape(9 * channels, channels)
    )
    feat_ext = padded_2(clip_feats, (("tile", 1),), 1)
    feat_columns = tile_columns(feat_ext, tile_rows, width_cells, False)
    pre = jnp.dot(feat_columns, spatial_weight, preferred_element_type=jnp.float32)
    act = jax.nn.silu(pre).astype(jnp.bfloat16)
    temporal_reach = 4 * TAP_DILATION
    per_group = tile_rows * width_cells // frame_devs
    grouped = (slab_frames, frame_devs, per_group, channels)
    act_part = lax.all_to_all(
        act.reshape(grouped), "frame", split_axis=1, concat_axis=0, tiled=True
    )
    grad_part = lax.all_to_all(out_grad, "frame", split_axis=1, concat_axis=0, tiled=True)
    feat_part = lax.all_to_all(clip_feats, "frame", split_axis=1, concat_axis=0, tiled=True)
    frame_count = act_part.shape[0]
    item_count = act_part.shape[2]
    act_pad = jnp.pad(
        act_part.reshape(frame_count, item_count, channels),
        ((temporal_reach, temporal_reach), (0, 0), (0, 0)),
    )
    grad_pad = jnp.pad(
        grad_part.reshape(frame_count, item_count, channels),
        ((temporal_reach, temporal_reach), (0, 0), (0, 0)),
    )
    mixed = temporal_taps(act_pad, temporal_weight, frame_count, False)
    out_part = (feat_part.reshape(-1, channels).astype(jnp.float32) + mixed).astype(jnp.bfloat16)
    back_part = temporal_taps(grad_pad, temporal_back, frame_count, True).astype(jnp.bfloat16)
    out_part = out_part.reshape(frame_count, 1, item_count, channels)
    back_part = back_part.reshape(frame_count, 1, item_count, channels)
    out_slab = lax.all_to_all(out_part, "frame", split_axis=0, concat_axis=1, tiled=True)
    grad_slab = lax.all_to_all(back_part, "frame", split_axis=0, concat_axis=1, tiled=True)
    act_grad = grad_slab.reshape(row_count, channels)
    sig = jax.nn.sigmoid(pre)
    pre_grad = (act_grad.astype(jnp.float32) * (sig * (1.0 + pre * (1.0 - sig)))).astype(
        jnp.bfloat16
    )
    full_term = lax.dot_general(
        feat_columns, pre_grad, (((0,), (0,)), ((), ())), preferred_element_type=jnp.float32
    )
    summed = lax.psum_scatter(full_term, ("frame", "tile"), scatter_dimension=0, tiled=True)
    weight_grad = summed * grad_scale
    grad_ext = padded_2(
        pre_grad.reshape(slab_frames, tile_rows, width_cells, channels), (("tile", 1),), 1
    )
    grad_columns = tile_columns(grad_ext, tile_rows, width_cells, True)
    local_back = jnp.dot(grad_columns, spatial_back, preferred_element_type=jnp.float32)
    input_grad = (out_grad.reshape(row_count, channels).astype(jnp.float32) + local_back).astype(
        jnp.bfloat16
    )
    input_grad = input_grad.reshape(slab_frames, tile_rows, width_cells, channels)
    return (out_slab, input_grad, weight_grad)


def kernel_call(body, outs, scratch, flops, *args, anywhere=0):
    moved = sum(a.size * a.dtype.itemsize for a in args)
    moved += sum(math.prod(shape) * jnp.dtype(kind).itemsize for shape, kind in outs)
    spaces = [pltpu.VMEM] * (len(args) - anywhere) + [pl.ANY] * anywhere
    return pl.pallas_call(
        body,
        out_shape=tuple(jax.ShapeDtypeStruct(shape, kind) for shape, kind in outs),
        in_specs=[pl.BlockSpec(memory_space=space) for space in spaces],
        out_specs=tuple(pl.BlockSpec(memory_space=pltpu.VMEM) for _ in outs),
        scratch_shapes=[pltpu.VMEM(shape, kind) for shape, kind in scratch],
        compiler_params=pltpu.CompilerParams(vmem_limit_bytes=VMEM_LIMIT),
        cost_estimate=pl.CostEstimate(flops=flops, bytes_accessed=moved, transcendentals=0),
    )(*args)


def shifted(values, width, step):
    rows = values.shape[0]
    at = lax.broadcasted_iota(jnp.int32, values.shape, 0) % width
    moved = pltpu.roll(values, step % rows, 0)
    inside = at >= step if step > 0 else at < width + step
    return jnp.where(inside, moved, 0.0)


def column_shifts(values, width):
    wide = values.astype(jnp.float32)
    return (
        shifted(wide, width, 1).astype(values.dtype),
        values,
        shifted(wide, width, -1).astype(values.dtype),
    )


def with_edges(own, other, ext):
    rows = own.shape[1]
    tile = lax.axis_index("tile")
    ext[:, 1 : rows + 1] = own[...]
    above, below = other[:, rows - 1], other[:, 0]
    ext[:, 0] = jnp.where(tile == 1, above, jnp.zeros_like(above))
    ext[:, rows + 1] = jnp.where(tile == 0, below, jnp.zeros_like(below))


def whole_image(own, other, image):
    rows = own.shape[1]
    tile = lax.axis_index("tile")
    image[:, 0] = jnp.zeros_like(image[:, 0])
    image[:, 2 * rows + 1] = jnp.zeros_like(image[:, 2 * rows + 1])
    image[:, pl.ds(1 + tile * rows, rows)] = own[...]
    image[:, pl.ds(1 + (1 - tile) * rows, rows)] = other[...]


def order_kernel(*refs):
    refs[-1][...] = jnp.zeros_like(refs[-1])


def spatial_kernel(own, weight, other, _, pre_ref, act_ref, image, pre_all):
    frames, rows, width, channels = own.shape
    whole_image(own, other, image)
    shifts = column_shifts(image[...].reshape(-1, channels), width)
    shifts = [piece.reshape(image.shape) for piece in shifts]
    for half in range(2):
        columns = jnp.concatenate(
            [
                shifts[s][:, half * rows + r : half * rows + r + rows].reshape(-1, channels)
                for r in range(3)
                for s in range(3)
            ],
            axis=1,
        )
        pre = jnp.dot(columns, weight[...], preferred_element_type=jnp.float32)
        pre_all[half] = pre
        act_ref[half] = (pre * jax.nn.sigmoid(pre)).astype(jnp.bfloat16)
    pre_ref[...] = pre_all[lax.axis_index("tile")]


def split_kernel(arrived, mine_ref, other_ref):
    tile = lax.axis_index("tile")
    mine_ref[...] = arrived[tile]
    other_ref[...] = arrived[1 - tile]


def forward_sum_kernel(partial, arrived, *rest, first):
    sum_ref = rest[-1]
    rows = partial[first : first + sum_ref.shape[0]]
    came = arrived[: sum_ref.shape[0]].astype(jnp.float32)
    sum_ref[...] = (rows + came).astype(sum_ref.dtype)


def share_rows(keep, near, last, first, scale):
    count = last.shape[0]
    total = keep[first : first + count] + near[first : first + count].astype(jnp.float32)
    return (total + last[...].astype(jnp.float32)) * scale


def first_rows_kernel(keep, near, last, block, _, out_hbm, block_hbm, rows, sems, *, scale):
    block_copy = pltpu.make_async_copy(block, block_hbm, sems.at[0])
    block_copy.start()
    rows[...] = share_rows(keep, near, last, 0, scale)
    copy = pltpu.make_async_copy(rows, out_hbm.at[pl.ds(0, last.shape[0])], sems.at[1])
    copy.start()
    block_copy.wait()
    copy.wait()


def other_rows_kernel(keep, near, last, _, out_hbm, rows, sems, *, scale):
    first = keep.shape[0] - last.shape[0]
    rows[...] = share_rows(keep, near, last, first, scale)
    copy = pltpu.make_async_copy(rows, out_hbm.at[pl.ds(first, last.shape[0])], sems.at[0])
    copy.start()
    copy.wait()


def transpose_kernel(own, other, _, out_ref, image):
    frames, rows, width, channels = own.shape
    tile = lax.axis_index("tile")
    whole_image(own, other, image)
    for which, first in enumerate((tile * rows, (1 - tile) * rows)):
        for r in range(3):
            block = image[:, pl.ds(first + r, rows)].reshape(-1, channels)
            out_ref[which, r * channels : (r + 1) * channels] = block.T


def slabs(own, first, second, ext):
    tile = lax.axis_index("tile")
    ext[2 * tile] = first[...]
    ext[1] = own[...]
    ext[2 - 2 * tile] = second[...]
    chip = lax.axis_index("frame")

    @pl.when(chip == 0)
    def _():
        ext[0] = jnp.zeros_like(ext[0])

    @pl.when(chip == lax.axis_size("frame") - 1)
    def _():
        ext[2] = jnp.zeros_like(ext[2])

    return ext[...].reshape(-1, own.shape[1])


def act_grad_kernel(own, first_in, second_in, weight, pre_ref, _, out_ref, ext):
    count, channels = own.shape
    frames = slabs(own, first_in, second_in, ext)
    hop = count // 4
    total = None
    for k in range(9):
        first = (8 - k) * hop
        term = lax.dot_general(
            frames[first : first + count],
            weight[k * channels : (k + 1) * channels],
            (((1,), (1,)), ((), ())),
            preferred_element_type=jnp.float32,
        )
        total = term if total is None else total + term
    act_grad = total.astype(jnp.bfloat16).astype(jnp.float32)
    pre = pre_ref[...]
    sig = jax.nn.sigmoid(pre)
    out_ref[...] = (act_grad * (sig * (1.0 + pre * (1.0 - sig)))).astype(jnp.bfloat16)


def temporal_kernel(feats, act, first_in, second_in, weight, out_ref, ext):
    count, channels = feats.shape
    own = act.at[lax.axis_index("tile")]
    frames = slabs(own, first_in, second_in, ext)
    hop = count // 4
    columns = jnp.concatenate([frames[k * hop : k * hop + count] for k in range(9)], axis=1)
    mixed = jnp.dot(columns, weight[...], preferred_element_type=jnp.float32)
    out_ref[...] = (feats[...].astype(jnp.float32) + mixed).astype(jnp.bfloat16)


def own_term_kernel(feats_t, own, total_ref):
    channels = own.shape[3]
    after, same, before = column_shifts(own[...].reshape(-1, channels), own.shape[2])
    left = feats_t[0]
    for s, right in enumerate((before, same, after)):
        total_ref[s] = jnp.dot(left, right, preferred_element_type=jnp.float32)


def kernel_grad_kernel(
    feats_t, other, term, far_a_ref, far_b_ref, pass_ref, near_ref, keep_ref, total
):
    frames, rows, width, channels = other.shape
    tile = lax.axis_index("tile")
    chip = lax.axis_index("frame")
    after, same, before = column_shifts(other[...].reshape(-1, channels), width)
    left = feats_t[1]
    for s, right in enumerate((before, same, after)):
        both = term[s] + jnp.dot(left, right, preferred_element_type=jnp.float32)
        for r in range(3):
            tap = 3 * r + s
            total[tap * channels : (tap + 1) * channels] = both[r * channels : (r + 1) * channels]
    share = keep_ref.shape[0]
    half = share // 2
    for distance, skip, ref in (
        (3, 0, far_a_ref),
        (3, half, far_b_ref),
        (2, 0, pass_ref),
        (1, 0, near_ref),
        (0, 0, keep_ref),
    ):
        first = (2 * (chip ^ distance) + tile) * share + skip
        ref[...] = total[pl.ds(pl.multiple_of(first, 16), ref.shape[0])].astype(ref.dtype)


def input_grad_kernel(out_grad, own, other, weight, _, out_ref, done_ref, ext):
    frames, rows, width, channels = own.shape
    with_edges(own, other, ext)
    after, same, before = column_shifts(ext[...].reshape(-1, channels), width)
    shifts = [piece.reshape(ext.shape) for piece in (before, same, after)]
    total = out_grad[...].astype(jnp.float32)
    for r in range(3):
        for s in range(3):
            tap = 3 * r + s
            total = total + lax.dot_general(
                shifts[s][:, 2 - r : 2 - r + rows].reshape(-1, channels),
                weight[tap * channels : (tap + 1) * channels],
                (((1,), (1,)), ((), ())),
                preferred_element_type=jnp.float32,
            )
    out_ref[...] = total.astype(jnp.bfloat16)
    done_ref[...] = jnp.zeros_like(done_ref)


def per_device_pair(clip_feats, out_grad, spatial_weight, temporal_weight):
    frames, rows, width, channels = clip_feats.shape
    count = frames * rows * width
    chips = lax.axis_size("frame")
    cores = lax.axis_size("tile")
    scale = 1.0 / math.sqrt(frames * chips * rows * cores * width)
    outward = [(2 * z, 2 * z + 2) for z in range(chips - 1)]
    outward += [(2 * z + 3, 2 * z + 1) for z in range(chips - 1)]
    outward += [(2 * chips - 2, 2 * chips - 1), (1, 0)]
    inward = [(target, source) for source, target in outward]
    both = ("frame", "tile")
    swap = [(0, 1), (1, 0)]
    bf16, f32 = jnp.bfloat16, jnp.float32
    product = 2 * count * 9 * channels * channels
    flat = (count, channels)
    ext = ((frames, rows + 2, width, channels), bf16)
    image = ((frames, 2 * rows + 2, width, channels), bf16)
    three = ((3, count, channels), bf16)

    grad_flat = out_grad.reshape(flat)
    feat_flat = clip_feats.reshape(flat)
    grad_first = lax.ppermute(grad_flat, both, outward)
    grad_second = lax.ppermute(grad_flat, both, inward)
    feat_other = lax.ppermute(clip_feats, "tile", swap)

    (first,) = kernel_call(order_kernel, [((8, 128), f32)], [], 5 * product)
    pre, act = kernel_call(
        spatial_kernel,
        [(flat, f32), ((2, *flat), bf16)],
        [image, ((2, *flat), f32)],
        2 * product,
        clip_feats, spatial_weight, feat_other, first, anywhere=1,
    )
    act_in = lax.ppermute(act, both, inward)
    (feats_t,) = kernel_call(
        transpose_kernel,
        [((2, 3 * channels, count), bf16)],
        [image],
        0,
        clip_feats, feat_other, pre, anywhere=1,
    )
    (pre_grad,) = kernel_call(
        act_grad_kernel,
        [(flat, bf16)],
        [three],
        product,
        grad_flat, grad_first, grad_second, temporal_weight, pre, feats_t, anywhere=1,
    )
    pre_grad = pre_grad.reshape(clip_feats.shape)
    pre_other = lax.ppermute(pre_grad, "tile", swap)

    share = (9 * channels // (chips * cores), channels)
    (term,) = kernel_call(
        own_term_kernel,
        [((3, 3 * channels, channels), f32)],
        [],
        product,
        feats_t, pre_grad,
    )
    half = (share[0] // 2, channels)
    far_a, far_b, onward, near, keep = kernel_call(
        kernel_grad_kernel,
        [(half, bf16), (half, bf16), (share, f32), (share, bf16), (share, f32)],
        [((9 * channels, channels), f32)],
        product,
        feats_t, pre_other, term,
    )
    beside = [(z, z ^ 1) for z in range(chips)]
    across = [(z, z ^ 2) for z in range(chips)]
    far_in_a = lax.ppermute(far_a, "frame", beside)
    far_in_b = lax.ppermute(far_b, "frame", beside)
    near_in = lax.ppermute(near, "frame", beside)
    act_second, act_pass = kernel_call(
        split_kernel, [(flat, bf16)] * 2, [], 0, act_in
    )
    act_first = lax.ppermute(act_pass, "tile", swap)

    (sum_a,) = kernel_call(
        functools.partial(forward_sum_kernel, first=0),
        [(half, bf16)],
        [],
        20 * product,
        onward, far_in_a, act_pass, anywhere=1,
    )
    last_a = lax.ppermute(sum_a, "frame", across)
    (sum_b,) = kernel_call(
        functools.partial(forward_sum_kernel, first=half[0]),
        [(half, bf16)],
        [],
        0,
        onward, far_in_b, sum_a, act_first, anywhere=2,
    )
    last_b = lax.ppermute(sum_b, "frame", across)
    input_grad, done = kernel_call(
        input_grad_kernel,
        [(flat, bf16), ((8, 128), f32)],
        [ext],
        product,
        grad_flat, pre_grad, pre_other, spatial_weight, sum_b, anywhere=1,
    )
    (block,) = kernel_call(
        temporal_kernel,
        [(flat, bf16)],
        [three],
        product,
        feat_flat, act, act_first, act_second, temporal_weight,
    )
    (arrived,) = kernel_call(
        order_kernel, [((8, 128), f32)], [], 20 * product, last_a, near_in, done, block, anywhere=4
    )
    weight_grad, block_out = pl.pallas_call(
        functools.partial(first_rows_kernel, scale=scale),
        out_shape=(jax.ShapeDtypeStruct(share, f32), jax.ShapeDtypeStruct(flat, bf16)),
        in_specs=[pl.BlockSpec(memory_space=pltpu.VMEM)] * 4 + [pl.BlockSpec(memory_space=pl.ANY)],
        out_specs=(
            pl.BlockSpec(memory_space=pltpu.HBM),
            pl.BlockSpec(memory_space=pltpu.HBM),
        ),
        scratch_shapes=[pltpu.VMEM(half, f32), pltpu.SemaphoreType.DMA((2,))],
        compiler_params=pltpu.CompilerParams(vmem_limit_bytes=VMEM_LIMIT),
    )(keep, near_in, last_a, block, arrived)
    weight_grad = pl.pallas_call(
        functools.partial(other_rows_kernel, scale=scale),
        out_shape=jax.ShapeDtypeStruct(share, f32),
        in_specs=[pl.BlockSpec(memory_space=pltpu.VMEM)] * 3 + [pl.BlockSpec(memory_space=pltpu.HBM)],
        out_specs=pl.BlockSpec(memory_space=pltpu.HBM),
        scratch_shapes=[pltpu.VMEM(half, f32), pltpu.SemaphoreType.DMA((1,))],
        input_output_aliases={3: 0},
        compiler_params=pltpu.CompilerParams(vmem_limit_bytes=VMEM_LIMIT),
    )(keep, near_in, last_b, weight_grad)
    return (
        block_out.reshape(clip_feats.shape),
        input_grad.reshape(clip_feats.shape),
        weight_grad,
    )


def per_device(clip_feats, *rest):
    pairs = lax.axis_size("tile") == 2 and lax.axis_size("frame") == 4
    if pairs and clip_feats.shape[0] == 4 * TAP_DILATION:
        return per_device_pair(clip_feats, *rest)
    return per_device_any(clip_feats, *rest)


def solution(mesh):
    return jax.shard_map(
        per_device,
        mesh=mesh,
        in_specs=(
            P(("clip", "frame"), "tile", None, None),
            P(("clip", "frame"), "tile", None, None),
            P(),
            P(),
        ),
        out_specs=(
            P(("clip", "frame"), "tile", None, None),
            P(("clip", "frame"), "tile", None, None),
            P(("clip", "frame", "tile"), None),
        ),
        check_vma=False,
    )
```

```python
import functools
import math

import jax
import jax.numpy as jnp
from jax import lax
from jax.experimental import pallas as pl
from jax.experimental.pallas import tpu as pltpu
from jax.sharding import PartitionSpec as P

TAP_DILATION = 2
VMEM_LIMIT = 32 * 1024 * 1024


def padded_2(block, sides, width):
    for axis, dim in sides:
        count = lax.axis_size(axis)
        forward = [(i, i + 1) for i in range(count - 1)]
        backward = [(target, source) for source, target in forward]
        low = lax.ppermute(
            lax.slice_in_dim(block, block.shape[dim] - width, None, axis=dim), axis, forward
        )
        high = lax.ppermute(lax.slice_in_dim(block, 0, width, axis=dim), axis, backward)
        block = jnp.concatenate([low, block, high], axis=dim)
    return block


def tile_columns(extended, tile_rows, width_cells, backward_pass):
    padded = jnp.pad(extended, ((0, 0), (0, 0), (1, 1), (0, 0)))
    pieces = []
    for row_shift in range(3):
        for col_shift in range(3):
            row_start = 2 - row_shift if backward_pass else row_shift
            col_start = 2 - col_shift if backward_pass else col_shift
            pieces.append(
                padded[:, row_start : row_start + tile_rows, col_start : col_start + width_cells, :]
            )
    channels = extended.shape[3]
    return jnp.concatenate(pieces, axis=-1).reshape(-1, 9 * channels)


def temporal_taps(padded_seq, weight, frame_count, backward_pass):
    pieces = []
    for temporal_tap_index in range(9):
        first_frame_index = (
            (8 - temporal_tap_index) * TAP_DILATION
            if backward_pass
            else temporal_tap_index * TAP_DILATION
        )
        pieces.append(padded_seq[first_frame_index : first_frame_index + frame_count])
    channels = padded_seq.shape[2]
    columns = jnp.concatenate(pieces, axis=-1).reshape(-1, 9 * channels)
    return jnp.dot(columns, weight, preferred_element_type=jnp.float32)


def per_device_any(clip_feats, out_grad, spatial_weight, temporal_weight):
    slab_frames, tile_rows, width_cells, channels = clip_feats.shape
    row_count = slab_frames * tile_rows * width_cells
    frame_devs = lax.axis_size("frame")
    tile_devs = lax.axis_size("tile")
    grad_scale = jnp.float32(
        1.0 / math.sqrt(slab_frames * frame_devs * tile_rows * tile_devs * width_cells)
    )
    spatial_back = (
        spatial_weight.reshape(9, channels, channels)
        .transpose(0, 2, 1)
        .reshape(9 * channels, channels)
    )
    temporal_back = (
        temporal_weight.reshape(9, channels, channels)
        .transpose(0, 2, 1)
        .reshape(9 * channels, channels)
    )
    feat_ext = padded_2(clip_feats, (("tile", 1),), 1)
    feat_columns = tile_columns(feat_ext, tile_rows, width_cells, False)
    pre = jnp.dot(feat_columns, spatial_weight, preferred_element_type=jnp.float32)
    act = jax.nn.silu(pre).astype(jnp.bfloat16)
    temporal_reach = 4 * TAP_DILATION
    per_group = tile_rows * width_cells // frame_devs
    grouped = (slab_frames, frame_devs, per_group, channels)
    act_part = lax.all_to_all(
        act.reshape(grouped), "frame", split_axis=1, concat_axis=0, tiled=True
    )
    grad_part = lax.all_to_all(out_grad, "frame", split_axis=1, concat_axis=0, tiled=True)
    feat_part = lax.all_to_all(clip_feats, "frame", split_axis=1, concat_axis=0, tiled=True)
    frame_count = act_part.shape[0]
    item_count = act_part.shape[2]
    act_pad = jnp.pad(
        act_part.reshape(frame_count, item_count, channels),
        ((temporal_reach, temporal_reach), (0, 0), (0, 0)),
    )
    grad_pad = jnp.pad(
        grad_part.reshape(frame_count, item_count, channels),
        ((temporal_reach, temporal_reach), (0, 0), (0, 0)),
    )
    mixed = temporal_taps(act_pad, temporal_weight, frame_count, False)
    out_part = (feat_part.reshape(-1, channels).astype(jnp.float32) + mixed).astype(jnp.bfloat16)
    back_part = temporal_taps(grad_pad, temporal_back, frame_count, True).astype(jnp.bfloat16)
    out_part = out_part.reshape(frame_count, 1, item_count, channels)
    back_part = back_part.reshape(frame_count, 1, item_count, channels)
    out_slab = lax.all_to_all(out_part, "frame", split_axis=0, concat_axis=1, tiled=True)
    grad_slab = lax.all_to_all(back_part, "frame", split_axis=0, concat_axis=1, tiled=True)
    act_grad = grad_slab.reshape(row_count, channels)
    sig = jax.nn.sigmoid(pre)
    pre_grad = (act_grad.astype(jnp.float32) * (sig * (1.0 + pre * (1.0 - sig)))).astype(
        jnp.bfloat16
    )
    full_term = lax.dot_general(
        feat_columns, pre_grad, (((0,), (0,)), ((), ())), preferred_element_type=jnp.float32
    )
    summed = lax.psum_scatter(full_term, ("frame", "tile"), scatter_dimension=0, tiled=True)
    weight_grad = summed * grad_scale
    grad_ext = padded_2(
        pre_grad.reshape(slab_frames, tile_rows, width_cells, channels), (("tile", 1),), 1
    )
    grad_columns = tile_columns(grad_ext, tile_rows, width_cells, True)
    local_back = jnp.dot(grad_columns, spatial_back, preferred_element_type=jnp.float32)
    input_grad = (out_grad.reshape(row_count, channels).astype(jnp.float32) + local_back).astype(
        jnp.bfloat16
    )
    input_grad = input_grad.reshape(slab_frames, tile_rows, width_cells, channels)
    return (out_slab, input_grad, weight_grad)


def kernel_call(body, outs, scratch, flops, *args, anywhere=0):
    moved = sum(a.size * a.dtype.itemsize for a in args)
    moved += sum(math.prod(shape) * jnp.dtype(kind).itemsize for shape, kind in outs)
    spaces = [pltpu.VMEM] * (len(args) - anywhere) + [pl.ANY] * anywhere
    return pl.pallas_call(
        body,
        out_shape=tuple(jax.ShapeDtypeStruct(shape, kind) for shape, kind in outs),
        in_specs=[pl.BlockSpec(memory_space=space) for space in spaces],
        out_specs=tuple(pl.BlockSpec(memory_space=pltpu.VMEM) for _ in outs),
        scratch_shapes=[pltpu.VMEM(shape, kind) for shape, kind in scratch],
        compiler_params=pltpu.CompilerParams(vmem_limit_bytes=VMEM_LIMIT),
        cost_estimate=pl.CostEstimate(flops=flops, bytes_accessed=moved, transcendentals=0),
    )(*args)


def shifted(values, width, step):
    rows = values.shape[0]
    at = lax.broadcasted_iota(jnp.int32, values.shape, 0) % width
    moved = pltpu.roll(values, step % rows, 0)
    inside = at >= step if step > 0 else at < width + step
    return jnp.where(inside, moved, 0.0)


def column_shifts(values, width):
    wide = values.astype(jnp.float32)
    return (
        shifted(wide, width, 1).astype(values.dtype),
        values,
        shifted(wide, width, -1).astype(values.dtype),
    )


def with_edges(own, other, ext):
    rows = own.shape[1]
    tile = lax.axis_index("tile")
    ext[:, 1 : rows + 1] = own[...]
    above, below = other[:, rows - 1], other[:, 0]
    ext[:, 0] = jnp.where(tile == 1, above, jnp.zeros_like(above))
    ext[:, rows + 1] = jnp.where(tile == 0, below, jnp.zeros_like(below))


def whole_image(own, other, image):
    rows = own.shape[1]
    tile = lax.axis_index("tile")
    image[:, 0] = jnp.zeros_like(image[:, 0])
    image[:, 2 * rows + 1] = jnp.zeros_like(image[:, 2 * rows + 1])
    image[:, pl.ds(1 + tile * rows, rows)] = own[...]
    image[:, pl.ds(1 + (1 - tile) * rows, rows)] = other[...]


def order_kernel(*refs):
    refs[-1][...] = jnp.zeros_like(refs[-1])


def spatial_kernel(own, weight, other, _, pre_ref, act_ref, image, pre_all):
    frames, rows, width, channels = own.shape
    whole_image(own, other, image)
    shifts = column_shifts(image[...].reshape(-1, channels), width)
    shifts = [piece.reshape(image.shape) for piece in shifts]
    for half in range(2):
        columns = jnp.concatenate(
            [
                shifts[s][:, half * rows + r : half * rows + r + rows].reshape(-1, channels)
                for r in range(3)
                for s in range(3)
            ],
            axis=1,
        )
        pre = jnp.dot(columns, weight[...], preferred_element_type=jnp.float32)
        pre_all[half] = pre
        act_ref[half] = (pre * jax.nn.sigmoid(pre)).astype(jnp.bfloat16)
    pre_ref[...] = pre_all[lax.axis_index("tile")]


def split_kernel(arrived, mine_ref, other_ref):
    tile = lax.axis_index("tile")
    mine_ref[...] = arrived[tile]
    other_ref[...] = arrived[1 - tile]


def forward_sum_kernel(partial, arrived, *rest, first):
    sum_ref = rest[-1]
    rows = partial[first : first + sum_ref.shape[0]]
    came = arrived[: sum_ref.shape[0]].astype(jnp.float32)
    sum_ref[...] = (rows + came).astype(sum_ref.dtype)


def share_rows(keep, near, last, first, scale):
    count = last.shape[0]
    total = keep[first : first + count] + near[first : first + count].astype(jnp.float32)
    return (total + last[...].astype(jnp.float32)) * scale


def first_rows_kernel(keep, near, last, block, _, out_hbm, block_hbm, rows, sems, *, scale):
    block_copy = pltpu.make_async_copy(block, block_hbm, sems.at[0])
    block_copy.start()
    rows[...] = share_rows(keep, near, last, 0, scale)
    copy = pltpu.make_async_copy(rows, out_hbm.at[pl.ds(0, last.shape[0])], sems.at[1])
    copy.start()
    block_copy.wait()
    copy.wait()


def other_rows_kernel(keep, near, last, _, out_hbm, rows, sems, *, scale):
    first = keep.shape[0] - last.shape[0]
    rows[...] = share_rows(keep, near, last, first, scale)
    copy = pltpu.make_async_copy(rows, out_hbm.at[pl.ds(first, last.shape[0])], sems.at[0])
    copy.start()
    copy.wait()


def transpose_kernel(own, other, _, out_ref, image):
    frames, rows, width, channels = own.shape
    tile = lax.axis_index("tile")
    whole_image(own, other, image)
    for which, first in enumerate((tile * rows, (1 - tile) * rows)):
        for r in range(3):
            block = image[:, pl.ds(first + r, rows)].reshape(-1, channels)
            out_ref[which, r * channels : (r + 1) * channels] = block.T


def slabs(own, first, second, ext):
    tile = lax.axis_index("tile")
    ext[2 * tile] = first[...]
    ext[1] = own[...]
    ext[2 - 2 * tile] = second[...]
    chip = lax.axis_index("frame")

    @pl.when(chip == 0)
    def _():
        ext[0] = jnp.zeros_like(ext[0])

    @pl.when(chip == lax.axis_size("frame") - 1)
    def _():
        ext[2] = jnp.zeros_like(ext[2])

    return ext[...].reshape(-1, own.shape[1])


def act_grad_kernel(own, first_in, second_in, weight, pre_ref, _, out_ref, ext):
    count, channels = own.shape
    frames = slabs(own, first_in, second_in, ext)
    hop = count // 4
    total = None
    for k in range(9):
        first = (8 - k) * hop
        term = lax.dot_general(
            frames[first : first + count],
            weight[k * channels : (k + 1) * channels],
            (((1,), (1,)), ((), ())),
            preferred_element_type=jnp.float32,
        )
        total = term if total is None else total + term
    act_grad = total.astype(jnp.bfloat16).astype(jnp.float32)
    pre = pre_ref[...]
    sig = jax.nn.sigmoid(pre)
    out_ref[...] = (act_grad * (sig * (1.0 + pre * (1.0 - sig)))).astype(jnp.bfloat16)


def temporal_kernel(feats, act, first_in, second_in, weight, out_ref, ext):
    count, channels = feats.shape
    own = act.at[lax.axis_index("tile")]
    frames = slabs(own, first_in, second_in, ext)
    hop = count // 4
    columns = jnp.concatenate([frames[k * hop : k * hop + count] for k in range(9)], axis=1)
    mixed = jnp.dot(columns, weight[...], preferred_element_type=jnp.float32)
    out_ref[...] = (feats[...].astype(jnp.float32) + mixed).astype(jnp.bfloat16)


def own_term_kernel(feats_t, own, total_ref):
    channels = own.shape[3]
    after, same, before = column_shifts(own[...].reshape(-1, channels), own.shape[2])
    left = feats_t[0]
    for s, right in enumerate((before, same, after)):
        total_ref[s] = jnp.dot(left, right, preferred_element_type=jnp.float32)


def kernel_grad_kernel(
    feats_t, other, term, far_a_ref, far_b_ref, pass_ref, near_ref, keep_ref, total
):
    frames, rows, width, channels = other.shape
    tile = lax.axis_index("tile")
    chip = lax.axis_index("frame")
    after, same, before = column_shifts(other[...].reshape(-1, channels), width)
    left = feats_t[1]
    for s, right in enumerate((before, same, after)):
        both = term[s] + jnp.dot(left, right, preferred_element_type=jnp.float32)
        for r in range(3):
            tap = 3 * r + s
            total[tap * channels : (tap + 1) * channels] = both[r * channels : (r + 1) * channels]
    share = keep_ref.shape[0]
    half = far_a_ref.shape[0]
    for distance, skip, ref in (
        (2, 0, far_a_ref),
        (2, half, far_b_ref),
        (3, 0, pass_ref),
        (1, 0, near_ref),
        (0, 0, keep_ref),
    ):
        first = (2 * (chip ^ distance) + tile) * share + skip
        ref[...] = total[pl.ds(pl.multiple_of(first, 16), ref.shape[0])].astype(ref.dtype)


def input_grad_kernel(out_grad, own, other, weight, _, out_ref, done_ref, ext):
    frames, rows, width, channels = own.shape
    with_edges(own, other, ext)
    after, same, before = column_shifts(ext[...].reshape(-1, channels), width)
    shifts = [piece.reshape(ext.shape) for piece in (before, same, after)]
    total = out_grad[...].astype(jnp.float32)
    for r in range(3):
        for s in range(3):
            tap = 3 * r + s
            total = total + lax.dot_general(
                shifts[s][:, 2 - r : 2 - r + rows].reshape(-1, channels),
                weight[tap * channels : (tap + 1) * channels],
                (((1,), (1,)), ((), ())),
                preferred_element_type=jnp.float32,
            )
    out_ref[...] = total.astype(jnp.bfloat16)
    done_ref[...] = jnp.zeros_like(done_ref)


def per_device_pair(clip_feats, out_grad, spatial_weight, temporal_weight):
    frames, rows, width, channels = clip_feats.shape
    count = frames * rows * width
    chips = lax.axis_size("frame")
    cores = lax.axis_size("tile")
    scale = 1.0 / math.sqrt(frames * chips * rows * cores * width)
    outward = [(2 * z, 2 * z + 2) for z in range(chips - 1)]
    outward += [(2 * z + 3, 2 * z + 1) for z in range(chips - 1)]
    outward += [(2 * chips - 2, 2 * chips - 1), (1, 0)]
    inward = [(target, source) for source, target in outward]
    both = ("frame", "tile")
    swap = [(0, 1), (1, 0)]
    bf16, f32 = jnp.bfloat16, jnp.float32
    product = 2 * count * 9 * channels * channels
    flat = (count, channels)
    ext = ((frames, rows + 2, width, channels), bf16)
    image = ((frames, 2 * rows + 2, width, channels), bf16)
    three = ((3, count, channels), bf16)

    grad_flat = out_grad.reshape(flat)
    feat_flat = clip_feats.reshape(flat)
    grad_first = lax.ppermute(grad_flat, both, outward)
    grad_second = lax.ppermute(grad_flat, both, inward)
    feat_other = lax.ppermute(clip_feats, "tile", swap)

    (first,) = kernel_call(order_kernel, [((8, 128), f32)], [], 5 * product)
    pre, act = kernel_call(
        spatial_kernel,
        [(flat, f32), ((2, *flat), bf16)],
        [image, ((2, *flat), f32)],
        2 * product,
        clip_feats, spatial_weight, feat_other, first, anywhere=1,
    )
    act_in = lax.ppermute(act, both, inward)
    (feats_t,) = kernel_call(
        transpose_kernel,
        [((2, 3 * channels, count), bf16)],
        [image],
        0,
        clip_feats, feat_other, pre, anywhere=1,
    )
    (pre_grad,) = kernel_call(
        act_grad_kernel,
        [(flat, bf16)],
        [three],
        product,
        grad_flat, grad_first, grad_second, temporal_weight, pre, feats_t, anywhere=1,
    )
    pre_grad = pre_grad.reshape(clip_feats.shape)
    pre_other = lax.ppermute(pre_grad, "tile", swap)

    share = (9 * channels // (chips * cores), channels)
    (term,) = kernel_call(
        own_term_kernel,
        [((3, 3 * channels, channels), f32)],
        [],
        product,
        feats_t, pre_grad,
    )
    part_a = (share[0] // 3, channels)
    part_b = (share[0] - part_a[0], channels)
    far_a, far_b, onward, near, keep = kernel_call(
        kernel_grad_kernel,
        [(part_a, bf16), (part_b, bf16), (share, f32), (share, bf16), (share, f32)],
        [((9 * channels, channels), f32)],
        product,
        feats_t, pre_other, term,
    )
    beside = [(z, z ^ 1) for z in range(chips)]
    across = [(z, z ^ 3) for z in range(chips)]
    far_in_a = lax.ppermute(far_a, "frame", beside)
    far_in_b = lax.ppermute(far_b, "frame", beside)
    near_in = lax.ppermute(near, "frame", beside)
    act_second, act_pass = kernel_call(
        split_kernel, [(flat, bf16)] * 2, [], 0, act_in
    )
    act_first = lax.ppermute(act_pass, "tile", swap)

    (sum_a,) = kernel_call(
        functools.partial(forward_sum_kernel, first=0),
        [(part_a, bf16)],
        [],
        20 * product,
        onward, far_in_a, act_pass, anywhere=1,
    )
    last_a = lax.ppermute(sum_a, "frame", across)
    (sum_b,) = kernel_call(
        functools.partial(forward_sum_kernel, first=part_a[0]),
        [(part_b, bf16)],
        [],
        0,
        onward, far_in_b, sum_a, act_first, anywhere=2,
    )
    last_b = lax.ppermute(sum_b, "frame", across)
    input_grad, done = kernel_call(
        input_grad_kernel,
        [(flat, bf16), ((8, 128), f32)],
        [ext],
        product,
        grad_flat, pre_grad, pre_other, spatial_weight, sum_b, anywhere=1,
    )
    (block,) = kernel_call(
        temporal_kernel,
        [(flat, bf16)],
        [three],
        product,
        feat_flat, act, act_first, act_second, temporal_weight,
    )
    (arrived,) = kernel_call(
        order_kernel, [((8, 128), f32)], [], 20 * product, last_a, near_in, done, block, anywhere=4
    )
    weight_grad, block_out = pl.pallas_call(
        functools.partial(first_rows_kernel, scale=scale),
        out_shape=(jax.ShapeDtypeStruct(share, f32), jax.ShapeDtypeStruct(flat, bf16)),
        in_specs=[pl.BlockSpec(memory_space=pltpu.VMEM)] * 4 + [pl.BlockSpec(memory_space=pl.ANY)],
        out_specs=(
            pl.BlockSpec(memory_space=pltpu.HBM),
            pl.BlockSpec(memory_space=pltpu.HBM),
        ),
        scratch_shapes=[pltpu.VMEM(part_a, f32), pltpu.SemaphoreType.DMA((2,))],
        compiler_params=pltpu.CompilerParams(vmem_limit_bytes=VMEM_LIMIT),
    )(keep, near_in, last_a, block, arrived)
    weight_grad = pl.pallas_call(
        functools.partial(other_rows_kernel, scale=scale),
        out_shape=jax.ShapeDtypeStruct(share, f32),
        in_specs=[pl.BlockSpec(memory_space=pltpu.VMEM)] * 3 + [pl.BlockSpec(memory_space=pltpu.HBM)],
        out_specs=pl.BlockSpec(memory_space=pltpu.HBM),
        scratch_shapes=[pltpu.VMEM(part_b, f32), pltpu.SemaphoreType.DMA((1,))],
        input_output_aliases={3: 0},
        compiler_params=pltpu.CompilerParams(vmem_limit_bytes=VMEM_LIMIT),
    )(keep, near_in, last_b, weight_grad)
    return (
        block_out.reshape(clip_feats.shape),
        input_grad.reshape(clip_feats.shape),
        weight_grad,
    )


def per_device(clip_feats, *rest):
    pairs = lax.axis_size("tile") == 2 and lax.axis_size("frame") == 4
    if pairs and clip_feats.shape[0] == 4 * TAP_DILATION:
        return per_device_pair(clip_feats, *rest)
    return per_device_any(clip_feats, *rest)


def solution(mesh):
    return jax.shard_map(
        per_device,
        mesh=mesh,
        in_specs=(
            P(("clip", "frame"), "tile", None, None),
            P(("clip", "frame"), "tile", None, None),
            P(),
            P(),
        ),
        out_specs=(
            P(("clip", "frame"), "tile", None, None),
            P(("clip", "frame"), "tile", None, None),
            P(("clip", "frame", "tile"), None),
        ),
        check_vma=False,
    )
```
